32 devices in a mesh: dp: 4 (over z), fsdp: 8 (over y, x, core).
Axes of the slice: x: 2, y: 2, z: 4, core: 2. Of those that a mesh axis runs over, the one named last changes fastest.
Arguments:
- patches: bfloat16 [4, 32, 1024, 768], P(None, ('dp', 'fsdp')), may hold values from -6 to 6
- labels: int32 [4, 32], P(None, ('dp', 'fsdp')), may hold values from 0 to 999
- valid: int32 [4, 32], P(None, ('dp', 'fsdp')), may hold values from 0 to 1, as said below
- mat3: float32 [320, 2560], P('fsdp'), may hold values from -0.3125 to 0.3125
- tall3: float32 [3328, 320], P('fsdp'), may hold values from -0.15625 to 0.15625
- mat4: float32 [512, 5096], P('fsdp'), may hold values from -0.25 to 0.25
- tall4: float32 [3328, 512], P('fsdp'), may hold values from -0.15625 to 0.15625
- depth: float32 [9, 3328], P(None, 'fsdp'), may hold values from -2 to 2
- norms3: float32 [8, 320], P(None, 'fsdp')
- norms4: float32 [8, 512], P(None, 'fsdp')
- mom_mat3: float32 [320, 2560], P('fsdp'), may hold values from -2.3841858e-07 to 2.3841858e-07
- mom_tall3: float32 [3328, 320], P('fsdp'), may hold values from -2.3841858e-07 to 2.3841858e-07
- mom_mat4: float32 [512, 5096], P('fsdp'), may hold values from -2.3841858e-07 to 2.3841858e-07
- mom_tall4: float32 [3328, 512], P('fsdp'), may hold values from -2.3841858e-07 to 2.3841858e-07
- mom_depth: float32 [9, 3328], P(None, 'fsdp'), may hold values from -2.3841858e-07 to 2.3841858e-07
- mom_norms3: float32 [8, 320], P(None, 'fsdp'), may hold values from -2.3841858e-07 to 2.3841858e-07
- mom_norms4: float32 [8, 512], P(None, 'fsdp'), may hold values from -2.3841858e-07 to 2.3841858e-07
- sq_mat3: float32 [320, 2560], P('fsdp'), may hold values from 1.6041436e-16 to 6.416574e-16
- sq_tall3: float32 [3328, 320], P('fsdp'), may hold values from 1.6041436e-16 to 6.416574e-16
- sq_mat4: float32 [512, 5096], P('fsdp'), may hold values from 1.6041436e-16 to 6.416574e-16
- sq_tall4: float32 [3328, 512], P('fsdp'), may hold values from 1.6041436e-16 to 6.416574e-16
- sq_depth: float32 [9, 3328], P(None, 'fsdp'), may hold values from 1.6041436e-16 to 6.416574e-16
- sq_norms3: float32 [8, 320], P(None, 'fsdp'), may hold values from 1.6041436e-16 to 6.416574e-16
- sq_norms4: float32 [8, 512], P(None, 'fsdp'), may hold values from 1.6041436e-16 to 6.416574e-16
Outputs:
- new_mat3: float32 [320, 2560], P('fsdp')
- new_tall3: float32 [3328, 320], P('fsdp')
- new_mat4: float32 [512, 5096], P('fsdp')
- new_tall4: float32 [3328, 512], P('fsdp')
- new_depth: float32 [9, 3328], P(None, 'fsdp')
- new_norms3: float32 [8, 320], P(None, 'fsdp')
- new_norms4: float32 [8, 512], P(None, 'fsdp')
- first_mat3: float32 [320, 2560], P('fsdp')
- first_tall3: float32 [3328, 320], P('fsdp')
- first_mat4: float32 [512, 5096], P('fsdp')
- first_tall4: float32 [3328, 512], P('fsdp')
- first_depth: float32 [9, 3328], P(None, 'fsdp')
- first_norms3: float32 [8, 320], P(None, 'fsdp')
- first_norms4: float32 [8, 512], P(None, 'fsdp')
- second_mat3: float32 [320, 2560], P('fsdp')
- second_tall3: float32 [3328, 320], P('fsdp')
- second_mat4: float32 [512, 5096], P('fsdp')
- second_tall4: float32 [3328, 512], P('fsdp')
- second_depth: float32 [9, 3328], P(None, 'fsdp')
- second_norms3: float32 [8, 320], P(None, 'fsdp')
- second_norms4: float32 [8, 512], P(None, 'fsdp')
- loss_sum: float32 [], replicated
- image_count: float32 [], replicated
- grad_norm: float32 [], replicated
The draws below stay inside these ranges and needn't reach their ends.
Inputs may be any that keep to these rules, and one draw needn't show every extreme that they name: `valid`: 1 where the slot holds an image; in every micro-batch the last image slot holds one.
All inputs are finite; a program needn't handle non-finite values.
Results may differ from the reference program's by a relative error of at most 0.0078.
Values may be sent and summed in bfloat16 or wider, within the bound.
No kernel may reach another device: no remote copies, remote signals or barrier semaphores. Data moves between devices by JAX's collectives and lax.ppermute only.
A program may use at most 512 MiB of HBM per device.

```python
import math
import jax
import jax.numpy as jnp
from jax import lax

C3 = 320
H3 = 5
F3 = 1280
C4 = 512
H4 = 8
F4 = 2048
CLASSES = 1000
PATCH = 768
GRID_ROWS = 32
GRID_COLS = 32
MB = 4
STEP = 10
TOK3 = 1024
IMAGES = 32
PARAMS = 6233856


def draw_rows(key, count, width):
    gain_key, shift_key = jax.random.split(key)
    gains = 1.0 + 0.1 * jax.random.normal(gain_key, (count // 2, 1, width), jnp.float32)
    shifts = 0.1 * jax.random.normal(shift_key, (count // 2, 1, width), jnp.float32)
    return jnp.concatenate([gains, shifts], axis=1).reshape(count, width)


def draw_norms3(key, part):
    key = jax.random.fold_in(key, 3)
    return draw_rows(key, 8, C3)


def draw_norms4(key, part):
    key = jax.random.fold_in(key, 4)
    return draw_rows(key, 8, C4)


def draw_valid(key, part):
    key = jax.random.fold_in(key, 5)
    places = jnp.arange(IMAGES, dtype=jnp.int32)
    limits = 300 + 650 * places // max(IMAGES - 1, 1)
    rolled = jax.random.randint(key, (MB, IMAGES), 0, 1000, dtype=jnp.int32)
    present = (rolled < limits[None, :]).astype(jnp.int32)
    return present.at[:, IMAGES - 1].set(1)


def place_ends(array, own_key, smallest, largest):
    index_at = [jax.random.randint(jax.random.fold_in(own_key, axis), (), 0, length) for axis, length in enumerate(array.shape)]
    widest = array.shape.index(max(array.shape))
    beside = index_at[:widest] + [(index_at[widest] + 1) % array.shape[widest]] + index_at[widest + 1:]
    return array.at[tuple(index_at)].set(smallest).at[tuple(beside)].set(largest)


def levels(key, shape, cuts, least, top_value):
    loudness = 1.0
    for axis_at, shards_of in cuts:
        steps = jax.random.uniform(jax.random.fold_in(jax.random.fold_in(key, 6), axis_at), (shards_of,), jnp.float32, least / len(cuts), top_value / len(cuts))
        loudness = loudness * jnp.repeat(jnp.exp(steps), shape[axis_at] // shards_of).reshape((-1,) + (1,) * (len(shape) - 1 - axis_at))
    return loudness


def scatter_about(own_key, dims, scale, limit, cuts=(), kind=jnp.bfloat16):
    values = scale * jax.random.normal(own_key, dims, jnp.float32)
    if cuts:
        values = values * levels(own_key, dims, cuts, -0.22, 0.18)
    return jnp.clip(values, -limit, limit).astype(kind)


def setup_inputs(seed: int = 0) -> dict:
    key_of = jax.random.split(jax.random.key(seed), 25)
    patches = scatter_about(key_of[0], (MB, IMAGES, TOK3, PATCH), 1.0, 6.0, ((1, 32),))
    labels = place_ends(jax.random.randint(key_of[1], (MB, IMAGES), 0, CLASSES), jax.random.fold_in(key_of[1], 1), 0, CLASSES - 1).astype(jnp.int32)
    valid = draw_valid(jax.random.fold_in(key_of[24], 71), 0)
    mat3 = scatter_about(key_of[3], (C3, 4 * C3 + F3), C3 ** -0.5, 0.3125, ((0, 8),), jnp.float32)
    tall3 = scatter_about(key_of[4], (PATCH + 4 * C3 + F3, C3), (4 * C3) ** -0.5, 0.15625, ((0, 8),), jnp.float32)
    mat4 = scatter_about(key_of[5], (C4, 4 * C4 + F4 + CLASSES), C4 ** -0.5, 0.25, ((0, 8),), jnp.float32)
    tall4 = scatter_about(key_of[6], (4 * C3 + F4, C4), (4 * C3) ** -0.5, 0.15625, ((0, 8),), jnp.float32)
    depth = scatter_about(key_of[7], (9, F3 + F4), 9 ** -0.5, 2.0, ((1, 8),), jnp.float32)
    norms3 = draw_norms3(jax.random.fold_in(key_of[24], 71), 0)
    norms4 = draw_norms4(jax.random.fold_in(key_of[24], 71), 0)
    mom_mat3 = scatter_about(key_of[10], (C3, 4 * C3 + F3), (0.000111 / PARAMS ** 0.5), 2.384185791015625e-07, ((0, 8),), jnp.float32)
    mom_tall3 = scatter_about(key_of[11], (PATCH + 4 * C3 + F3, C3), (0.000111 / PARAMS ** 0.5), 2.384185791015625e-07, ((0, 8),), jnp.float32)
    mom_mat4 = scatter_about(key_of[12], (C4, 4 * C4 + F4 + CLASSES), (0.000111 / PARAMS ** 0.5), 2.384185791015625e-07, ((0, 8),), jnp.float32)
    mom_tall4 = scatter_about(key_of[13], (4 * C3 + F4, C4), (0.000111 / PARAMS ** 0.5), 2.384185791015625e-07, ((0, 8),), jnp.float32)
    mom_depth = scatter_about(key_of[14], (9, F3 + F4), (0.000111 / PARAMS ** 0.5), 2.384185791015625e-07, ((1, 8),), jnp.float32)
    mom_norms3 = scatter_about(key_of[15], (8, C3), (0.000111 / PARAMS ** 0.5), 2.384185791015625e-07, ((1, 8),), jnp.float32)
    mom_norms4 = scatter_about(key_of[16], (8, C4), (0.000111 / PARAMS ** 0.5), 2.384185791015625e-07, ((1, 8),), jnp.float32)
    sq_mat3 = jnp.clip(jnp.exp(math.log(6.416574213356416e-16) - 1.3862944 * jax.random.uniform(key_of[17], (C3, 4 * C3 + F3), jnp.float32) ** levels(key_of[17], (C3, 4 * C3 + F3), ((0, 8),), -0.2, 0.2)), 1.604143553339104e-16, 6.416574213356416e-16)
    sq_tall3 = jnp.clip(jnp.exp(math.log(6.416574213356416e-16) - 1.3862944 * jax.random.uniform(key_of[18], (PATCH + 4 * C3 + F3, C3), jnp.float32) ** levels(key_of[18], (PATCH + 4 * C3 + F3, C3), ((0, 8),), -0.2, 0.2)), 1.604143553339104e-16, 6.416574213356416e-16)
    sq_mat4 = jnp.clip(jnp.exp(math.log(6.416574213356416e-16) - 1.3862944 * jax.random.uniform(key_of[19], (C4, 4 * C4 + F4 + CLASSES), jnp.float32) ** levels(key_of[19], (C4, 4 * C4 + F4 + CLASSES), ((0, 8),), -0.2, 0.2)), 1.604143553339104e-16, 6.416574213356416e-16)
    sq_tall4 = jnp.clip(jnp.exp(math.log(6.416574213356416e-16) - 1.3862944 * jax.random.uniform(key_of[20], (4 * C3 + F4, C4), jnp.float32) ** levels(key_of[20], (4 * C3 + F4, C4), ((0, 8),), -0.2, 0.2)), 1.604143553339104e-16, 6.416574213356416e-16)
    sq_depth = jnp.clip(jnp.exp(math.log(6.416574213356416e-16) - 1.3862944 * jax.random.uniform(key_of[21], (9, F3 + F4), jnp.float32) ** levels(key_of[21], (9, F3 + F4), ((1, 8),), -0.2, 0.2)), 1.604143553339104e-16, 6.416574213356416e-16)
    sq_norms3 = jnp.clip(jnp.exp(math.log(6.416574213356416e-16) - 1.3862944 * jax.random.uniform(key_of[22], (8, C3), jnp.float32) ** levels(key_of[22], (8, C3), ((1, 8),), -0.2, 0.2)), 1.604143553339104e-16, 6.416574213356416e-16)
    sq_norms4 = jnp.clip(jnp.exp(math.log(6.416574213356416e-16) - 1.3862944 * jax.random.uniform(key_of[23], (8, C4), jnp.float32) ** levels(key_of[23], (8, C4), ((1, 8),), -0.2, 0.2)), 1.604143553339104e-16, 6.416574213356416e-16)
    return dict(patches=patches, labels=labels, valid=valid, mat3=mat3, tall3=tall3, mat4=mat4, tall4=tall4, depth=depth, norms3=norms3, norms4=norms4, mom_mat3=mom_mat3, mom_tall3=mom_tall3, mom_mat4=mom_mat4, mom_tall4=mom_tall4, mom_depth=mom_depth, mom_norms3=mom_norms3, mom_norms4=mom_norms4, sq_mat3=sq_mat3, sq_tall3=sq_tall3, sq_mat4=sq_mat4, sq_tall4=sq_tall4, sq_depth=sq_depth, sq_norms3=sq_norms3, sq_norms4=sq_norms4)


@jax.custom_vjp
def low(v):
    return lax.optimization_barrier(v.astype(jnp.bfloat16)).astype(jnp.float32)

@jax.custom_vjp
def low_back(v):
    return v

def low_keep(v):
    return (low(v), None)

def low_pass(kept, grad):
    return (grad,)

def back_keep(v):
    return (v, None)

def back_low(kept, grad):
    return (low(grad),)
low.defvjp(low_keep, low_pass)
low_back.defvjp(back_keep, back_low)
eps_norm = 1e-06
smoothing = 0.1
clip_level = 0.001

def matmul(left, right):
    return jnp.dot(left, right, precision=lax.Precision.HIGHEST, preferred_element_type=jnp.float32)

def contract(form, left, right):
    return jnp.einsum(form, left, right, precision=lax.Precision.HIGHEST)

def rounded(value):
    return low_back(low(value))

def layer_norm(inputs, gain, shift):
    average = lax.optimization_barrier(jnp.mean(inputs, axis=-1, keepdims=True))
    centred = inputs - average
    spread = lax.optimization_barrier(jnp.mean(centred * centred, axis=-1, keepdims=True))
    return centred * lax.rsqrt(spread + eps_norm) * gain + shift

def merge_quads(inputs, row_count, column_count):
    width = inputs.shape[-1]
    squares = inputs.reshape(row_count // 2, 2, column_count // 2, 2, width).transpose(0, 2, 1, 3, 4)
    return squares.reshape(row_count // 2 * (column_count // 2), 4 * width)

def depthwise(inputs, kernel, row_count, column_count):
    width = inputs.shape[-1]
    padded = jnp.pad(inputs.reshape(row_count, column_count, width), ((1, 1), (1, 1), (0, 0)))
    total = jnp.zeros((row_count, column_count, width), jnp.float32)
    for offset in range(9):
        total = total + padded[offset // 3:offset // 3 + row_count, offset % 3:offset % 3 + column_count] * kernel[offset]
    return total.reshape(row_count * column_count, width)

def block(inputs, row_count, column_count, mat, w_second, kernel, gains, reduce_w, head_count):
    width = inputs.shape[-1]
    tokens = inputs.shape[0]
    normed = low(layer_norm(inputs, gains[0], gains[1]))
    query = rounded(matmul(normed, mat[:, :width]))
    if reduce_w is None:
        source = normed
        later = gains[2:]
    else:
        reduced = low_back(matmul(merge_quads(normed, row_count, column_count), reduce_w))
        source = low(layer_norm(reduced, gains[2], gains[3]))
        later = gains[4:]
    keys_out = rounded(matmul(source, mat[:, width:2 * width]))
    values_out = rounded(matmul(source, mat[:, 2 * width:3 * width]))
    key_count = source.shape[0]
    head_size = width // head_count
    query_heads = query.reshape(tokens, head_count, head_size)
    key_heads = keys_out.reshape(key_count, head_count, head_size)
    value_heads = values_out.reshape(key_count, head_count, head_size)
    scores = low_back(contract('qhd,khd->hqk', query_heads, key_heads) * head_size ** (-0.5))
    scores = scores - lax.optimization_barrier(jnp.max(scores, axis=-1, keepdims=True))
    exponent = jnp.exp(scores)
    weights_soft = low(exponent / lax.optimization_barrier(jnp.sum(exponent, axis=-1, keepdims=True)))
    mixed = rounded(contract('hqk,khd->qhd', weights_soft, value_heads).reshape(tokens, width))
    after = inputs + low_back(matmul(mixed, mat[:, 3 * width:4 * width]))
    hidden_count = w_second.shape[0]
    normed = low(layer_norm(after, later[0], later[1]))
    hidden = low_back(matmul(normed, mat[:, 4 * width:4 * width + hidden_count]))
    activated = low(jax.nn.gelu(depthwise(hidden, kernel, row_count, column_count)))
    return after + low_back(matmul(activated, w_second))

def image_loss(weights, pixels, target):
    mat3, tall3, mat4, tall4, depth, norms3, norms4 = [low(weight) for weight in weights]
    width3 = mat3.shape[0]
    width4 = mat4.shape[0]
    features = pixels.shape[-1]
    hidden3 = mat3.shape[1] - 4 * width3
    hidden4 = tall4.shape[0] - 4 * width3
    embedded = layer_norm(low_back(matmul(pixels, tall3[:features])), norms3[0], norms3[1])
    state = block(embedded, GRID_ROWS, GRID_COLS, mat3, tall3[features + 4 * width3:], depth[:, :hidden3], norms3[2:], tall3[features:features + 4 * width3], H3)
    merged = merge_quads(low(state), GRID_ROWS, GRID_COLS)
    state = layer_norm(low_back(matmul(merged, tall4[:4 * width3])), norms4[0], norms4[1])
    state = block(state, GRID_ROWS // 2, GRID_COLS // 2, mat4, tall4[4 * width3:], depth[:, hidden3:], norms4[2:6], None, H4)
    pooled = low(lax.optimization_barrier(jnp.mean(layer_norm(state, norms4[6], norms4[7]), axis=0, keepdims=True)))
    logits = low_back(matmul(pooled, mat4[:, 4 * width4 + hidden4:]))[0]
    shifted = logits - jnp.max(logits)
    log_probs = shifted - jnp.log(jnp.sum(jnp.exp(shifted)))
    classes = logits.shape[0]
    one_hot = (jnp.arange(classes, dtype=jnp.int32) == target).astype(jnp.float32)
    return -jnp.sum(((1.0 - smoothing) * one_hot + smoothing / classes) * log_probs)

def group_loss(weights, pixel_group, target_group, present_group):

    def advance(running, element):
        pixels, target, present = element
        return (running + present * jax.checkpoint(image_loss)(weights, pixels.astype(jnp.float32), target), None)
    running, unused = lax.scan(advance, jnp.float32(0.0), (pixel_group, target_group, present_group))
    return running

def adamw(master, moment, second, gradient, is_norm):
    step_rate = 0.5 if is_norm else 0.05
    decay_now = 0.0 if is_norm else 0.05
    first = 0.9 * moment + 0.1 * gradient
    second_new = 0.999 * second + 0.001 * gradient * gradient
    first_hat = first / (1.0 - 0.9 ** STEP)
    second_hat = second_new / (1.0 - 0.999 ** STEP)
    updated = master - step_rate * (first_hat / (jnp.sqrt(second_hat) + 1e-08) + decay_now * master)
    return (updated, first, second_new)

def reference(patches, labels, valid, mat3, tall3, mat4, tall4, depth, norms3, norms4, mom_mat3, mom_tall3, mom_mat4, mom_tall4, mom_depth, mom_norms3, mom_norms4, sq_mat3, sq_tall3, sq_mat4, sq_tall4, sq_depth, sq_norms3, sq_norms4):
    weights = (mat3, tall3, mat4, tall4, depth, norms3, norms4)
    moments = (mom_mat3, mom_tall3, mom_mat4, mom_tall4, mom_depth, mom_norms3, mom_norms4)
    seconds = (sq_mat3, sq_tall3, sq_mat4, sq_tall4, sq_depth, sq_norms3, sq_norms4)
    image_count = jnp.sum(valid).astype(jnp.float32)
    flat_pixels = patches.reshape(MB * IMAGES, TOK3, PATCH)
    flat_targets = labels.reshape(MB * IMAGES)
    flat_present = valid.reshape(MB * IMAGES).astype(jnp.float32)
    loss_sum, pullback = jax.vjp(lambda weights_now: group_loss(weights_now, flat_pixels, flat_targets, flat_present), weights)
    gradients = pullback(jnp.float32(1.0) / image_count)[0]
    total = jnp.float32(0.0)
    for gradient in gradients:
        total = total + jnp.sum(gradient * gradient)
    grad_norm = jnp.sqrt(total)
    clip_factor = jnp.minimum(1.0, clip_level / (grad_norm + 1e-06))
    results = [adamw(weights[place], moments[place], seconds[place], clip_factor * gradients[place], place >= 5) for place in range(7)]
    return (results[0][0], results[1][0], results[2][0], results[3][0], results[4][0], results[5][0], results[6][0], results[0][1], results[1][1], results[2][1], results[3][1], results[4][1], results[5][1], results[6][1], results[0][2], results[1][2], results[2][2], results[3][2], results[4][2], results[5][2], results[6][2], loss_sum, image_count, grad_norm)
```

```python
import functools

import jax
import jax.numpy as jnp
from jax import lax
from jax.experimental import pallas as pl
from jax.experimental.pallas import tpu as pltpu
from jax.sharding import PartitionSpec as P

BF = jnp.bfloat16
F32 = jnp.float32
C3 = 320
C3P = 384
H3 = 5
F3 = 1280
C4 = 512
H4 = 8
F4 = 2048
CLASSES = 1000
PATCH = 768
STEP = 10
IMGS = 4
TOK3 = 1024
TOK4 = 256
LC = 256
EPS = 1e-06
SMOOTHING = 0.1
CLIP_LEVEL = 0.001
SCALE = 0.125
VMEM_BYTES = 63 * 2**20


def contract(a, b, ca, cb):
    return lax.dot_general(a, b, (((ca,), (cb,)), ((), ())), preferred_element_type=F32)


def nn(a, b):
    return contract(a, b, 1, 0)


def nt(a, b):
    return contract(a, b, 1, 1)


def tn(a, b):
    return contract(a, b, 0, 0)


def normalize(x):
    centred = x - jnp.mean(x, axis=-1, keepdims=True)
    rstd = lax.rsqrt(jnp.mean(centred * centred, axis=-1, keepdims=True) + EPS)
    return centred * rstd, rstd


def norm_grad(dy, xhat, rstd, gain):
    dx = dy * gain
    return rstd * (dx - jnp.mean(dx, axis=-1, keepdims=True) - xhat * jnp.mean(dx * xhat, axis=-1, keepdims=True))


def column_sum(x):
    return jnp.sum(x, axis=0, keepdims=True)


def half_of(x, half):
    lane = lax.broadcasted_iota(jnp.int32, x.shape, 1)
    keep = (lane < 64) if half == 0 else (lane >= 64)
    return jnp.where(keep, x, jnp.zeros_like(x))


def softmax_rows0(scores):
    top = jnp.max(scores, axis=0, keepdims=True)
    exponent = jnp.exp(scores - top)
    return exponent * (1.0 / jnp.sum(exponent, axis=0, keepdims=True))


def gelu_both(c):
    k0 = 0.7978845608028654
    k1 = 0.044715 * k0
    c2 = c * c
    t = jnp.tanh(c * (k1 * c2 + k0))
    half = 0.5 * t + 0.5
    slope = half + c * (half - half * half) * (6.0 * k1 * c2 + 2.0 * k0)
    return c * half, slope


def shift_down(v):
    lane = lax.broadcasted_iota(jnp.int32, v.shape, 1)
    return jnp.where(lane == 0, 0.0, pltpu.roll(v, 1, 1))


def shift_up(v):
    lane = lax.broadcasted_iota(jnp.int32, v.shape, 1)
    return jnp.where(lane == 7, 0.0, pltpu.roll(v, 7, 1))


def class3(py, xm):
    return py * 4 + (xm & 1) * 2 + (xm >> 1)


def store3(plain, moved, plane, value):
    py, px = plane // 2, plane % 2
    value = value.reshape(2, 16, 8, value.shape[-1])
    for qx in range(2):
        plain[plane * 2 + qx, 1:17] = value[qx]
    if px == 1:
        moved[py * 2, 1:17] = shift_down(value[1])
    else:
        moved[py * 2 + 1, 1:17] = shift_up(value[0])


def tap3(plain, moved, py, xm, dy, dx, lanes):
    row = (py + dy) % 2
    start = 1 + (py + dy) // 2
    at = xm + dx
    if at == -1:
        return moved[row * 2, start : start + 16, :, lanes]
    if at == 4:
        return moved[row * 2 + 1, start : start + 16, :, lanes]
    return plain[class3(row, at), start : start + 16, :, lanes]


def store4(plain, moved, image, value):
    value = value.reshape(2, 16, 8, value.shape[-1])
    for qx in range(2):
        plain[image, qx, 1:17] = value[qx]
    moved[image, 0, 1:17] = shift_down(value[1])
    moved[image, 1, 1:17] = shift_up(value[0])


def tap4(plain, moved, image, qx, dy, dx, lanes):
    start = 1 + dy
    at = qx + dx
    if at == -1:
        return moved[image, 0, start : start + 16, :, lanes]
    if at == 2:
        return moved[image, 1, start : start + 16, :, lanes]
    return plain[image, at, start : start + 16, :, lanes]


TAPS = [(t, t // 3 - 1, t % 3 - 1) for t in range(9)]


def embed_attend(patches, tall3, mat3, norms, z_o, h_o, red_o, q_o, k_o, v_o, p_o, mix_o, x1_o, x0_s, vt_s):
    we = tall3[0:PATCH]
    reduced = None
    for b in range(4):
        rows = pl.ds(b * 256, 256)
        z = nn(patches[0, rows, :], we)
        z_o[0, rows, :] = z
        x0 = normalize(z)[0] * norms[0:1] + norms[1:2]
        x0_s[rows, :] = x0
        h = (normalize(x0)[0] * norms[2:3] + norms[3:4]).astype(BF)
        h_o[0, rows, :] = h
        q_o[0, rows, :] = nn(h, mat3[:, 0:C3P]).astype(BF)
        part = nn(h, tall3[PATCH + C3 * b : PATCH + C3 * (b + 1)])
        reduced = part if reduced is None else reduced + part
    red_o[0] = reduced
    r = (normalize(reduced)[0] * norms[4:5] + norms[5:6]).astype(BF)
    k = nn(r, mat3[:, C3P : 2 * C3P]).astype(BF)
    v = nn(r, mat3[:, 2 * C3P : 3 * C3P]).astype(BF)
    k_o[0] = k
    v_o[0] = v
    vt_s[...] = v.T

    def queries(b, carry):
        rows = pl.ds(pl.multiple_of(b * 256, 256), 256)
        for head in range(H3):
            lanes = slice(head // 2 * 128, head // 2 * 128 + 128)
            key = half_of(k_o[0, :, lanes], head % 2)
            scores = nt(key, q_o[0, rows, lanes]) * SCALE
            soft = softmax_rows0(scores).astype(BF)
            p_o[0, head, :, rows] = soft
            mix_o[0, head * 64 : head * 64 + 64, rows] = nn(vt_s[head * 64 : head * 64 + 64, :], soft).astype(BF)
        x1_o[0, rows, :] = x0_s[rows, :] + tn(mix_o[0, :, rows], mat3[0:C3, 3 * C3P : 3 * C3P + C3])
        return carry

    lax.fori_loop(0, 4, queries, 0)


def feed3(x1, tall3, mat3, depth, norms, n_o, hid_o, slope_o, act_o, x2_o, plain, moved):
    @pl.when(pl.program_id(0) == 0)
    def _():
        for ref in (plain, moved):
            ref[:, 0:1] = jnp.zeros((ref.shape[0], 1, 8, LC), F32)
            ref[:, 17:18] = jnp.zeros((ref.shape[0], 1, 8, LC), F32)

    for b in range(4):
        rows = pl.ds(b * 256, 256)
        n_o[0, rows, :] = (normalize(x1[0, rows, :])[0] * norms[6:7] + norms[7:8]).astype(BF)

    def chunk(j, carry):
        wide = pl.ds(pl.multiple_of(j * LC, LC), LC)
        w1 = mat3[:, pl.ds(pl.multiple_of(4 * C3P + j * LC, LC), LC)]
        for plane in range(4):
            rows = pl.ds(plane * 256, 256)
            value = nn(n_o[0, rows, :], w1)
            hid_o[0, rows, wide] = value.astype(BF)
            store3(plain, moved, plane, value)
        for lt in range(LC // 128):
            lanes = pl.ds(lt * 128, 128)
            out_lanes = pl.ds(pl.multiple_of(j * LC + lt * 128, 128), 128)
            kernel = depth[:, out_lanes]
            for py in range(2):
                for xm in range(4):
                    total = None
                    for t, dy, dx in TAPS:
                        term = tap3(plain, moved, py, xm, dy, dx, lanes) * kernel[t : t + 1][None]
                        total = term if total is None else total + term
                    act, slope = gelu_both(total)
                    rows = pl.ds(class3(py, xm) * 128, 128)
                    act_o[0, rows, out_lanes] = act.reshape(128, 128).astype(BF)
                    slope_o[0, rows, out_lanes] = slope.reshape(128, 128).astype(BF)
        return carry

    lax.fori_loop(0, F3 // LC, chunk, 0)
    for b in range(4):
        rows = pl.ds(b * 256, 256)
        x2_o[0, rows, :] = (x1[0, rows, :] + nn(act_o[0, rows, :], tall3[PATCH + 4 * C3 :])).astype(BF)


def section4(
    labels, valid, inv_count, x2, mat4, tall4, depth, norms,
    dx2_o, gm_o, gt_o, gd_o, gn_o, loss_o,
    first, y1_s, y2_s, h_s, qkv_s, p_s, mix_s, n_s, hid_s, slope_s, act_s, plain, moved, gd_s,
):
    for ref in (plain, moved):
        for at in (0, 17):
            ref[:, :, at : at + 1] = jnp.zeros((IMGS, 2, 1, 8, LC), F32)

    w1_at = 4 * C4
    wc_at = 4 * C4 + F4

    for i in range(IMGS):
        rows = pl.ds(i * TOK4, TOK4)
        prod = None
        for plane in range(4):
            part = nn(x2[i, plane * 256 : plane * 256 + 256, :], tall4[plane * C3 : plane * C3 + C3, :])
            prod = part if prod is None else prod + part
        first[rows, :] = prod
        y0 = normalize(prod)[0] * norms[0:1] + norms[1:2]
        y1_s[rows, :] = y0
        h_s[rows, :] = (normalize(y0)[0] * norms[2:3] + norms[3:4]).astype(BF)
    for j in range(3):
        wide = slice(j * C4, j * C4 + C4)
        qkv_s[:, wide] = nn(h_s[...], mat4[:, wide]).astype(BF)

    def attend(i, carry):
        rows = pl.ds(pl.multiple_of(i * TOK4, TOK4), TOK4)
        for head in range(H4):
            pair = head // 2 * 128
            key = half_of(qkv_s[rows, C4 + pair : C4 + pair + 128], head % 2)
            scores = nt(key, qkv_s[rows, pair : pair + 128]) * SCALE
            soft = softmax_rows0(scores).astype(BF)
            p_s[i * H4 + head] = soft
            if head % 2 == 0:
                vt = qkv_s[rows, 2 * C4 + pair : 2 * C4 + pair + 128].T
            half = vt[0:64] if head % 2 == 0 else vt[64:128]
            mix_s[head * 64 : head * 64 + 64, rows] = nn(half, soft).astype(BF)
        return carry

    lax.fori_loop(0, IMGS, attend, 0)

    for i in range(IMGS):
        rows = pl.ds(i * TOK4, TOK4)
        y1 = y1_s[rows, :] + tn(mix_s[:, i * TOK4 : i * TOK4 + TOK4], mat4[:, 3 * C4 : 4 * C4])
        y1_s[rows, :] = y1
        n_s[rows, :] = (normalize(y1)[0] * norms[4:5] + norms[5:6]).astype(BF)

    def feed(j, carry):
        wide = pl.ds(pl.multiple_of(j * LC, LC), LC)
        w1 = mat4[:, pl.ds(pl.multiple_of(w1_at + j * LC, LC), LC)]
        for i in range(IMGS):
            rows = pl.ds(i * TOK4, TOK4)
            value = nn(n_s[rows, :], w1)
            hid_s[rows, wide] = value.astype(BF)
            store4(plain, moved, i, value)
        for lt in range(LC // 128):
            lanes = pl.ds(lt * 128, 128)
            out_lanes = pl.ds(pl.multiple_of(j * LC + lt * 128, 128), 128)
            kernel = depth[:, out_lanes]
            for i in range(IMGS):
                for qx in range(2):
                    total = None
                    for t, dy, dx in TAPS:
                        term = tap4(plain, moved, i, qx, dy, dx, lanes) * kernel[t : t + 1][None]
                        total = term if total is None else total + term
                    act, slope = gelu_both(total)
                    rows = pl.ds(i * TOK4 + qx * 128, 128)
                    act_s[rows, out_lanes] = act.reshape(128, 128).astype(BF)
                    slope_s[rows, out_lanes] = slope.reshape(128, 128).astype(BF)
        return carry

    lax.fori_loop(0, F4 // LC, feed, 0)

    pools = []
    hat_means = []
    for i in range(IMGS):
        rows = pl.ds(i * TOK4, TOK4)
        y2 = y1_s[rows, :] + nn(act_s[rows, :], tall4[4 * C3 :, :])
        y2_s[rows, :] = y2
        hat_mean = jnp.mean(normalize(y2)[0], axis=0, keepdims=True)
        hat_means.append(hat_mean)
        pools.append(hat_mean * norms[6:7] + norms[7:8])
    pooled = jnp.concatenate(pools + [jnp.zeros((8 - IMGS, C4), F32)], axis=0).astype(BF)
    logits = nn(pooled, mat4[:, wc_at:])

    row = lax.broadcasted_iota(jnp.int32, (8, CLASSES), 0)
    column = lax.broadcasted_iota(jnp.int32, (8, CLASSES), 1)
    target = jnp.full((8, CLASSES), -1, jnp.int32)
    present = jnp.zeros((8, CLASSES), F32)
    for i in range(IMGS):
        target = jnp.where(row == i, labels[i], target)
        present = jnp.where(row == i, valid[i].astype(F32), present)
    goal = (1.0 - SMOOTHING) * (column == target).astype(F32) + SMOOTHING / CLASSES
    shifted = logits - jnp.max(logits, axis=-1, keepdims=True)
    exponent = jnp.exp(shifted)
    mass = jnp.sum(exponent, axis=-1, keepdims=True)
    log_probs = shifted - jnp.log(mass)
    ce = -jnp.sum(goal * log_probs, axis=-1, keepdims=True)
    loss_o[...] = jnp.broadcast_to(jnp.sum(present[:, 0:1] * ce, axis=0, keepdims=True), (8, 128))
    dlogits = (present * inv_count[0] * (exponent / mass - goal)).astype(BF)

    gm_o[:, wc_at:] = tn(pooled, dlogits).astype(gm_o.dtype)
    dpool = nt(dlogits, mat4[:, wc_at:])
    dgain = None
    for i in range(IMGS):
        rows = pl.ds(i * TOK4, TOK4)
        one = dpool[i : i + 1]
        part = one * hat_means[i]
        dgain = part if dgain is None else dgain + part
        xhat, rstd = normalize(y2_s[rows, :])
        dy2 = norm_grad(jnp.broadcast_to(one * (1.0 / TOK4), (TOK4, C4)), xhat, rstd, norms[6:7])
        y2_s[rows, :] = dy2
    gn_o[6:7] = dgain
    gn_o[7:8] = column_sum(dpool)

    dy = y2_s[...].astype(BF)
    gt_o[4 * C3 :, :] = tn(act_s[...], dy).astype(gt_o.dtype)
    act_s[:, 0:C4] = dy
    act_s[:, C4 : 2 * C4] = jnp.zeros((IMGS * TOK4, C4), BF)
    gd_s[...] = jnp.zeros_like(gd_s)
    nt_val = n_s[...].T

    def feed_back(j, total):
        wide = pl.ds(pl.multiple_of(j * LC, LC), LC)
        w1_wide = pl.ds(pl.multiple_of(w1_at + j * LC, LC), LC)
        w2 = tall4[pl.ds(pl.multiple_of(4 * C3 + j * LC, LC), LC), :]
        for i in range(IMGS):
            rows = pl.ds(i * TOK4, TOK4)
            value = nt(act_s[rows, 0:C4], w2) * slope_s[rows, wide].astype(F32)
            store4(plain, moved, i, value)
        for lt in range(LC // 128):
            lanes = pl.ds(lt * 128, 128)
            out_lanes = pl.ds(pl.multiple_of(j * LC + lt * 128, 128), 128)
            kernel = depth[:, out_lanes]
            sums = [None] * 9
            for i in range(IMGS):
                for qx in range(2):
                    rows = pl.ds(i * TOK4 + qx * 128, 128)
                    base = hid_s[rows, out_lanes].astype(F32).reshape(16, 8, 128)
                    out = None
                    for t, dy, dx in TAPS:
                        value = tap4(plain, moved, i, qx, -dy, -dx, lanes)
                        term = value * kernel[t : t + 1][None]
                        out = term if out is None else out + term
                        part = jnp.sum(value * base, axis=0)
                        sums[t] = part if sums[t] is None else sums[t] + part
                    hid_s[rows, out_lanes] = out.reshape(128, 128).astype(BF)
            for t in range(9):
                gd_s[t, :, out_lanes] = sums[t]
        dhid = hid_s[:, wide]
        gm_o[:, w1_wide] = nn(nt_val, dhid).astype(gm_o.dtype)
        return carry_none

    carry_none = 0
    lax.fori_loop(0, F4 // LC, feed_back, 0)
    for t in range(9):
        gd_o[t : t + 1, :] = column_sum(gd_s[t])

    for ref_at in (2, 4, 0):
        pass
    dgain = dshift = None
    for i in range(IMGS):
        rows = pl.ds(i * TOK4, TOK4)
        dn = nt(hid_s[rows, :], mat4[:, w1_at : w1_at + F4])
        xhat, rstd = normalize(y1_s[rows, :])
        part_g, part_s = column_sum(dn * xhat), column_sum(dn)
        dgain = part_g if dgain is None else dgain + part_g
        dshift = part_s if dshift is None else dshift + part_s
        y2_s[rows, :] = y2_s[rows, :] + norm_grad(dn, xhat, rstd, norms[4:5])
    gn_o[4:5] = dgain
    gn_o[5:6] = dshift

    dprod = y2_s[...].astype(BF)
    gm_o[:, 3 * C4 : 4 * C4] = nn(mix_s[...], dprod).astype(gm_o.dtype)
    n_s[...] = nt(dprod, mat4[:, 3 * C4 : 4 * C4]).astype(BF)

    def attend_back(i, carry):
        rows = pl.ds(pl.multiple_of(i * TOK4, TOK4), TOK4)
        lane = lax.broadcasted_iota(jnp.int32, (TOK4, 128), 1)
        for pair in range(H4 // 2):
            at = pair * 128
            q = qkv_s[rows, at : at + 128]
            k = qkv_s[rows, C4 + at : C4 + at + 128]
            v = qkv_s[rows, 2 * C4 + at : 2 * C4 + at + 128]
            do = n_s[rows, at : at + 128]
            kt = k.T
            dqts, dks, dvs = [], [], []
            for half in range(2):
                soft = p_s[i * H4 + pair * 2 + half]
                dp = nt(half_of(v, half), do)
                wide_soft = soft.astype(F32)
                ds = wide_soft * (dp - jnp.sum(dp * wide_soft, axis=0, keepdims=True))
                ds = ds.astype(BF)
                dvs.append(nn(soft, do))
                dks.append(nn(ds, q))
                dqts.append(nn(kt[half * 64 : half * 64 + 64], ds))
            dqt = (jnp.concatenate(dqts, axis=0) * SCALE).astype(BF)
            qkv_s[rows, at : at + 128] = dqt.T
            qkv_s[rows, C4 + at : C4 + at + 128] = (jnp.where(lane < 64, dks[0], dks[1]) * SCALE).astype(BF)
            qkv_s[rows, 2 * C4 + at : 2 * C4 + at + 128] = jnp.where(lane < 64, dvs[0], dvs[1]).astype(BF)
        return carry

    lax.fori_loop(0, IMGS, attend_back, 0)
    ht = h_s[...].T
    for j in range(3):
        wide = slice(j * C4, j * C4 + C4)
        gm_o[:, wide] = nn(ht, qkv_s[:, wide]).astype(gm_o.dtype)

    sums = [None] * 4
    for i in range(IMGS):
        rows = pl.ds(i * TOK4, TOK4)
        dh = nt(qkv_s[rows, :], mat4[:, 0 : 3 * C4])
        hat0, rstd0 = normalize(first[rows, :])
        hat1, rstd1 = normalize(hat0 * norms[0:1] + norms[1:2])
        dy0 = y2_s[rows, :] + norm_grad(dh, hat1, rstd1, norms[2:3])
        dprod0 = norm_grad(dy0, hat0, rstd0, norms[0:1]).astype(BF)
        n_s[rows, :] = dprod0
        parts = [column_sum(dy0 * hat0), column_sum(dy0), column_sum(dh * hat1), column_sum(dh)]
        sums = [part if old is None else old + part for old, part in zip(sums, parts)]
        for plane in range(4):
            dx2_o[i, plane * 256 : plane * 256 + 256, :] = nt(dprod0, tall4[plane * C3 : plane * C3 + C3, :]).astype(BF)
    gn_o[0:4] = jnp.concatenate(sums, axis=0)
    for plane in range(4):
        total = None
        for i in range(IMGS):
            part = tn(x2[i, plane * 256 : plane * 256 + 256, :], n_s[i * TOK4 : i * TOK4 + TOK4, :])
            total = part if total is None else total + part
        gt_o[plane * C3 : plane * C3 + C3, :] = total.astype(gt_o.dtype)


def feed3_back(dx2, x1, n, hid, slope, act, tall3, mat3, depth, norms, dx1_o, g1_o, g2_o, gd_o, gn_o,
               acc1, acc2, accd, accn, plain, moved, dy_s, dyt_s, nt_s, da_s):
    step = pl.program_id(0)

    @pl.when(step == 0)
    def _():
        for ref in (plain, moved):
            ref[:, 0:1] = jnp.zeros((ref.shape[0], 1, 8, LC), F32)
            ref[:, 17:18] = jnp.zeros((ref.shape[0], 1, 8, LC), F32)
        for ref in (acc1, acc2, accd, accn):
            ref[...] = jnp.zeros_like(ref)

    dy = dx2[0]
    dy_s[...] = dy
    dyt_s[...] = dy.T
    nt_s[...] = n[0].T

    def chunk(j, carry):
        wide = pl.ds(pl.multiple_of(j * LC, LC), LC)
        w2 = tall3[pl.ds(pl.multiple_of(PATCH + 4 * C3 + j * LC, LC), LC), :]
        for plane in range(4):
            rows = pl.ds(plane * 256, 256)
            value = nt(dy_s[rows, :], w2) * slope[0, rows, wide].astype(F32)
            store3(plain, moved, plane, value)
        for lt in range(LC // 128):
            lanes = pl.ds(lt * 128, 128)
            out_lanes = pl.ds(pl.multiple_of(j * LC + lt * 128, 128), 128)
            kernel = depth[:, out_lanes]
            sums = [None] * 9
            for py in range(2):
                for xm in range(4):
                    rows = pl.ds(class3(py, xm) * 128, 128)
                    base = hid[0, rows, out_lanes].astype(F32).reshape(16, 8, 128)
                    out = None
                    for t, dy, dx in TAPS:
                        value = tap3(plain, moved, py, xm, -dy, -dx, lanes)
                        term = value * kernel[t : t + 1][None]
                        out = term if out is None else out + term
                        part = jnp.sum(value * base, axis=0)
                        sums[t] = part if sums[t] is None else sums[t] + part
                    da_s[rows, out_lanes] = out.reshape(128, 128).astype(BF)
            for t in range(9):
                accd[t, :, out_lanes] += sums[t]
        da = da_s[:, wide]
        acc1[:, wide] += nn(nt_s[...], da)
        acc2[:, wide] += nn(dyt_s[...], act[0, :, wide])
        return carry

    lax.fori_loop(0, F3 // LC, chunk, 0)
    for b in range(4):
        rows = pl.ds(b * 256, 256)
        dn = nt(da_s[rows, :], mat3[:, 4 * C3P :])
        xhat, rstd = normalize(x1[0, rows, :])
        accn[0:1] += column_sum(dn * xhat)
        accn[1:2] += column_sum(dn)
        dx1_o[0, rows, :] = dx2[0, rows, :].astype(F32) + norm_grad(dn, xhat, rstd, norms[6:7])

    @pl.when(step == IMGS - 1)
    def _():
        g1_o[...] = acc1[...].astype(g1_o.dtype)
        g2_o[...] = acc2[...].T.astype(g2_o.dtype)
        gn_o[...] = accn[...]
        for t in range(9):
            gd_o[t : t + 1, :] = column_sum(accd[t])


def attend3_back(dx1, z, h, red, q, k, v, p, mix, patches, tall3, mat3, norms, ge_o, gr_o, gm_o, gn_o,
                 acce, accr, accq, acck, accv, acco, accn, dk_s, dv_s, kt_s, dqt_s, dr_s):
    step = pl.program_id(0)

    @pl.when(step == 0)
    def _():
        for ref in (acce, accr, accq, acck, accv, acco, accn):
            ref[...] = jnp.zeros_like(ref)

    kt_s[...] = k[0].T
    dk_s[...] = jnp.zeros_like(dk_s)
    dv_s[...] = jnp.zeros_like(dv_s)
    wo = mat3[0:C3, 3 * C3P : 3 * C3P + C3]
    lane = lax.broadcasted_iota(jnp.int32, (256, 128), 1)

    def queries(b, carry):
        rows = pl.ds(pl.multiple_of(b * 256, 256), 256)
        dprod = dx1[0, rows, :].astype(BF)
        acco[...] += nn(mix[0, :, rows], dprod)
        dmix = nt(dprod, wo).astype(BF)
        dmix = jnp.concatenate([dmix, jnp.zeros((256, C3P - C3), BF)], axis=1)
        for pair in range(3):
            lanes = slice(pair * 128, pair * 128 + 128)
            do = dmix[:, lanes]
            qp = q[0, rows, lanes]
            dks, dvs = [], []
            for half in range(2 if pair < 2 else 1):
                head = pair * 2 + half
                soft = p[0, head, :, rows]
                dp = nt(half_of(v[0, :, lanes], half), do)
                wide_soft = soft.astype(F32)
                ds = wide_soft * (dp - jnp.sum(dp * wide_soft, axis=0, keepdims=True))
                ds = ds.astype(BF)
                dvs.append(nn(soft, do))
                dks.append(nn(ds, qp))
                dqt = nn(kt_s[head * 64 : head * 64 + 64, :], ds) * SCALE
                dqt_s[head * 64 : head * 64 + 64, rows] = dqt.astype(BF)
            if len(dks) == 2:
                dk_s[:, lanes] += jnp.where(lane < 64, dks[0], dks[1])
                dv_s[:, lanes] += jnp.where(lane < 64, dvs[0], dvs[1])
            else:
                dk_s[:, lanes] += dks[0]
                dv_s[:, lanes] += dvs[0]
        return carry

    lax.fori_loop(0, 4, queries, 0)

    dk = (dk_s[...] * SCALE).astype(BF)
    dv = dv_s[...].astype(BF)
    hat_r, rstd_r = normalize(red[0])
    r = (hat_r * norms[4:5] + norms[5:6]).astype(BF)
    acck[...] += tn(r, dk)
    accv[...] += tn(r, dv)
    dr = nt(dk, mat3[:, C3P : 2 * C3P]) + nt(dv, mat3[:, 2 * C3P : 3 * C3P])
    accn[4:5] += column_sum(dr * hat_r)
    accn[5:6] += column_sum(dr)
    dred = norm_grad(dr, hat_r, rstd_r, norms[4:5]).astype(BF)
    accq[...] += nn(dqt_s[...], h[0])
    for b in range(4):
        rows = pl.ds(b * 256, 256)
        wr = tall3[PATCH + C3 * b : PATCH + C3 * (b + 1)]
        accr[C3 * b : C3 * (b + 1)] += tn(h[0, rows, :], dred)
        dh = tn(dqt_s[:, rows], mat3[:, 0:C3].T) + nt(dred, wr)
        hat0, rstd0 = normalize(z[0, rows, :])
        hat1, rstd1 = normalize(hat0 * norms[0:1] + norms[1:2])
        accn[2:3] += column_sum(dh * hat1)
        accn[3:4] += column_sum(dh)
        dx0 = dx1[0, rows, :] + norm_grad(dh, hat1, rstd1, norms[2:3])
        accn[0:1] += column_sum(dx0 * hat0)
        accn[1:2] += column_sum(dx0)
        dz = norm_grad(dx0, hat0, rstd0, norms[0:1]).astype(BF)
        acce[...] += tn(dz, patches[0, rows, :])

    @pl.when(step == IMGS - 1)
    def _():
        ge_o[...] = acce[...].T.astype(ge_o.dtype)
        gr_o[...] = accr[...].astype(gr_o.dtype)
        gm_o[:, 0:C3] = accq[...].T.astype(gm_o.dtype)
        gm_o[:, C3P : 2 * C3P] = acck[...].astype(gm_o.dtype)
        gm_o[:, 2 * C3P : 3 * C3P] = accv[...].astype(gm_o.dtype)
        gm_o[:, 3 * C3P : 3 * C3P + C3] = acco[...].astype(gm_o.dtype)
        gn_o[...] = accn[...]


def whole(shape, dtype=None):
    return pl.BlockSpec(shape, lambda i: (0,) * len(shape), pipeline_mode=pl.Buffered(1))


def per_image(*shape):
    return pl.BlockSpec((1,) + shape, lambda i: (i,) + (0,) * len(shape))


def sds(*shape, dtype=F32):
    return jax.ShapeDtypeStruct(shape, dtype)


PARAMS = pltpu.CompilerParams(vmem_limit_bytes=VMEM_BYTES, dimension_semantics=("arbitrary",))


def run_embed_attend(patches, tall3, mat3, norms3):
    return pl.pallas_call(
        embed_attend,
        grid=(IMGS,),
        in_specs=[per_image(TOK3, PATCH), whole(tall3.shape), whole(mat3.shape), whole(norms3.shape)],
        out_specs=[
            per_image(TOK3, C3), per_image(TOK3, C3), per_image(256, C3), per_image(TOK3, C3P), per_image(256, C3P),
            per_image(256, C3P), per_image(H3, 256, TOK3), per_image(C3, TOK3), per_image(TOK3, C3),
        ],
        out_shape=[
            sds(IMGS, TOK3, C3), sds(IMGS, TOK3, C3, dtype=BF), sds(IMGS, 256, C3), sds(IMGS, TOK3, C3P, dtype=BF),
            sds(IMGS, 256, C3P, dtype=BF), sds(IMGS, 256, C3P, dtype=BF), sds(IMGS, H3, 256, TOK3, dtype=BF),
            sds(IMGS, C3, TOK3, dtype=BF), sds(IMGS, TOK3, C3),
        ],
        scratch_shapes=[pltpu.VMEM((TOK3, C3), F32), pltpu.VMEM((C3P, 256), BF)],
        compiler_params=PARAMS,
        name="embed_attend",
    )(patches, tall3, mat3, norms3)


def run_feed3(x1, tall3, mat3, depth, norms3):
    return pl.pallas_call(
        feed3,
        grid=(IMGS,),
        in_specs=[per_image(TOK3, C3), whole(tall3.shape), whole(mat3.shape), whole(depth.shape), whole(norms3.shape)],
        out_specs=[per_image(TOK3, C3), per_image(TOK3, F3), per_image(TOK3, F3), per_image(TOK3, F3), per_image(TOK3, C3)],
        out_shape=[
            sds(IMGS, TOK3, C3, dtype=BF), sds(IMGS, TOK3, F3, dtype=BF), sds(IMGS, TOK3, F3, dtype=BF),
            sds(IMGS, TOK3, F3, dtype=BF), sds(IMGS, TOK3, C3, dtype=BF),
        ],
        scratch_shapes=[pltpu.VMEM((8, 18, 8, LC), F32), pltpu.VMEM((4, 18, 8, LC), F32)],
        compiler_params=PARAMS,
        name="feed3",
    )(x1, tall3, mat3, depth, norms3)


def run_section4(labels, valid, inv_count, x2, mat4, tall4, depth, norms4):
    vm = pl.BlockSpec(memory_space=pltpu.VMEM)
    sm = pl.BlockSpec(memory_space=pltpu.SMEM)
    rows = IMGS * TOK4
    return pl.pallas_call(
        section4,
        in_specs=[sm, sm, sm, vm, vm, vm, vm, vm],
        out_specs=[vm] * 6,
        out_shape=[
            sds(IMGS, TOK3, C3, dtype=BF), sds(*mat4.shape, dtype=BF), sds(*tall4.shape, dtype=BF), sds(9, F4), sds(8, C4),
            sds(8, 128),
        ],
        scratch_shapes=[
            pltpu.VMEM((rows, C4), F32), pltpu.VMEM((rows, C4), F32), pltpu.VMEM((rows, C4), F32),
            pltpu.VMEM((rows, C4), BF), pltpu.VMEM((rows, 3 * C4), BF), pltpu.VMEM((IMGS * H4, 256, 256), BF),
            pltpu.VMEM((C4, rows), BF), pltpu.VMEM((rows, C4), BF), pltpu.VMEM((rows, F4), BF),
            pltpu.VMEM((rows, F4), BF), pltpu.VMEM((rows, F4), BF), pltpu.VMEM((IMGS, 2, 18, 8, LC), F32),
            pltpu.VMEM((IMGS, 2, 18, 8, LC), F32), pltpu.VMEM((9, 8, F4), F32),
        ],
        compiler_params=pltpu.CompilerParams(vmem_limit_bytes=VMEM_BYTES),
        name="section4",
    )(labels, valid, inv_count, x2, mat4, tall4, depth, norms4)


def run_feed3_back(dx2, x1, n, hid, slope, act, tall3, mat3, depth, norms3):
    return pl.pallas_call(
        feed3_back,
        grid=(IMGS,),
        in_specs=[
            per_image(TOK3, C3), per_image(TOK3, C3), per_image(TOK3, C3), per_image(TOK3, F3), per_image(TOK3, F3),
            per_image(TOK3, F3), whole(tall3.shape), whole(mat3.shape), whole(depth.shape), whole(norms3.shape),
        ],
        out_specs=[per_image(TOK3, C3), whole((C3, F3)), whole((F3, C3)), whole((9, F3)), whole((2, C3))],
        out_shape=[sds(IMGS, TOK3, C3), sds(C3, F3, dtype=BF), sds(F3, C3, dtype=BF), sds(9, F3), sds(2, C3)],
        scratch_shapes=[
            pltpu.VMEM((C3, F3), F32), pltpu.VMEM((C3, F3), F32), pltpu.VMEM((9, 8, F3), F32), pltpu.VMEM((2, C3), F32),
            pltpu.VMEM((8, 18, 8, LC), F32), pltpu.VMEM((4, 18, 8, LC), F32), pltpu.VMEM((TOK3, C3), BF),
            pltpu.VMEM((C3, TOK3), BF), pltpu.VMEM((C3, TOK3), BF), pltpu.VMEM((TOK3, F3), BF),
        ],
        compiler_params=PARAMS,
        name="feed3_back",
    )(dx2, x1, n, hid, slope, act, tall3, mat3, depth, norms3)


def run_attend3_back(dx1, z, h, red, q, k, v, p, mix, patches, tall3, mat3, norms3):
    return pl.pallas_call(
        attend3_back,
        grid=(IMGS,),
        in_specs=[
            per_image(TOK3, C3), per_image(TOK3, C3), per_image(TOK3, C3), per_image(256, C3), per_image(TOK3, C3P),
            per_image(256, C3P), per_image(256, C3P), per_image(H3, 256, TOK3), per_image(C3, TOK3),
            per_image(TOK3, PATCH), whole(tall3.shape), whole(mat3.shape), whole(norms3.shape),
        ],
        out_specs=[whole((PATCH, C3)), whole((4 * C3, C3)), whole((C3, 4 * C3P)), whole((6, C3))],
        out_shape=[sds(PATCH, C3, dtype=BF), sds(4 * C3, C3, dtype=BF), sds(C3, 4 * C3P, dtype=BF), sds(6, C3)],
        scratch_shapes=[
            pltpu.VMEM((C3, PATCH), F32), pltpu.VMEM((4 * C3, C3), F32), pltpu.VMEM((C3, C3), F32),
            pltpu.VMEM((C3, C3P), F32), pltpu.VMEM((C3, C3P), F32), pltpu.VMEM((C3, C3), F32), pltpu.VMEM((6, C3), F32),
            pltpu.VMEM((256, C3P), F32), pltpu.VMEM((256, C3P), F32), pltpu.VMEM((C3P, 256), BF),
            pltpu.VMEM((C3, TOK3), BF), pltpu.VMEM((256, C3), F32),
        ],
        compiler_params=PARAMS,
        name="attend3_back",
    )(dx1, z, h, red, q, k, v, p, mix, patches, tall3, mat3, norms3)


def pad_mat3(mat):
    pieces = [mat[:, at * C3 : at * C3 + C3] for at in range(4)]
    pieces = [jnp.pad(piece, ((0, 0), (0, C3P - C3))) for piece in pieces]
    return jnp.concatenate(pieces + [mat[:, 4 * C3 :]], axis=1)


def reorder(patches):
    count = patches.shape[0]
    grid = patches.reshape(count, 16, 2, 8, 2, 2, patches.shape[-1])
    return grid.transpose(0, 2, 5, 4, 1, 3, 6).reshape(patches.shape)


def local_gradients(patches, labels, valid, inv_count, mat3, tall3, mat4, tall4, depth, norms3, norms4):
    z, h, red, q, k, v, p, mix, x1 = run_embed_attend(patches, tall3, mat3, norms3)
    n, hid, slope, act, x2 = run_feed3(x1, tall3, mat3, depth[:, :F3], norms3)
    dx2, gm4, gt4, gd4, gn4, loss = run_section4(labels, valid, inv_count, x2, mat4, tall4, depth[:, F3:], norms4)
    dx1, g1, g2, gd3, gn3b = run_feed3_back(dx2, x1, n, hid, slope, act, tall3, mat3, depth[:, :F3], norms3)
    ge, gr, gm3, gn3a = run_attend3_back(dx1, z, h, red, q, k, v, p, mix, patches, tall3, mat3, norms3)
    return loss, gm4, gt4, gd4, gn4, g1, g2, gd3, gn3b, ge, gr, gm3, gn3a


def adamw(master, moment, second, gradient, is_norm):
    step_rate = 0.5 if is_norm else 0.05
    decay_now = 0.0 if is_norm else 0.05
    first = 0.9 * moment + 0.1 * gradient
    second_new = 0.999 * second + 0.001 * gradient * gradient
    first_hat = first / (1.0 - 0.9**STEP)
    second_hat = second_new / (1.0 - 0.999**STEP)
    updated = master - step_rate * (first_hat / (jnp.sqrt(second_hat) + 1e-08) + decay_now * master)
    return (updated, first, second_new)


def body(patches, labels, valid, *state):
    masters, moments, seconds = state[0:7], state[7:14], state[14:21]
    both = ("dp", "fsdp")
    image_count = lax.psum(jnp.sum(valid).astype(F32), both)
    inv_count = (1.0 / image_count).reshape(1)

    mat3, tall3, mat4, tall4, depth, norms3, norms4 = [master.astype(BF) for master in masters]
    small = [jnp.pad(piece.T, ((0, 0), (0, 16 - piece.shape[0]))) for piece in (depth, norms3, norms4)]
    sizes = [piece.shape[0] for piece in small]
    small = lax.all_gather(jnp.concatenate(small, axis=0), "fsdp", axis=0)
    edges = [0, sizes[0], sizes[0] + sizes[1], sum(sizes)]
    parts = [small[:, edges[at] : edges[at + 1]].reshape(-1, 16).T.astype(F32) for at in range(3)]
    depth_all, norms3_all, norms4_all = parts[0][:9], parts[1][:8], parts[2][:8]
    tall3_all = lax.all_gather(tall3, "fsdp", axis=0, tiled=True)
    mat3_all = lax.all_gather(pad_mat3(mat3), "fsdp", axis=0, tiled=True)
    tall4_all = lax.all_gather(tall4, "fsdp", axis=0, tiled=True)
    mat4_all = lax.all_gather(mat4, "fsdp", axis=0, tiled=True)

    loss, gm4, gt4, gd4, gn4, g1, g2, gd3, gn3b, ge, gr, gm3, gn3a = local_gradients(
        reorder(patches.reshape(IMGS, TOK3, PATCH)), labels.reshape(IMGS), valid.reshape(IMGS), inv_count,
        mat3_all, tall3_all, mat4_all, tall4_all, depth_all, norms3_all, norms4_all,
    )

    def share(piece):
        return lax.psum(lax.psum_scatter(piece, "fsdp", scatter_dimension=0, tiled=True).astype(F32), "dp")

    grad_mat4 = share(gm4)
    grad_tall4 = share(gt4)
    grad_feed = share(g1)
    grad_mix = share(gm3)
    grad_tall3 = share(jnp.concatenate([ge, gr, g2], axis=0))
    grad_mat3 = jnp.concatenate([grad_mix[:, at * C3P : at * C3P + C3] for at in range(4)] + [grad_feed], axis=1)
    flat = [gd3.reshape(-1), gd4.reshape(-1), gn3a.reshape(-1), gn3b.reshape(-1), gn4.reshape(-1)]
    flat = lax.psum(jnp.concatenate(flat), both)
    me = lax.axis_index("fsdp")
    ends = [0]
    for size in (9 * F3, 9 * F4, 6 * C3, 2 * C3, 8 * C4):
        ends.append(ends[-1] + size)
    cut = [flat[ends[at] : ends[at + 1]] for at in range(5)]
    full = [
        jnp.concatenate([cut[0].reshape(9, F3), cut[1].reshape(9, F4)], axis=1),
        jnp.concatenate([cut[2].reshape(6, C3), cut[3].reshape(2, C3)], axis=0),
        cut[4].reshape(8, C4),
    ]
    own = [
        lax.dynamic_slice_in_dim(piece, me * master.shape[1], master.shape[1], 1)
        for piece, master in zip(full, masters[4:])
    ]
    group = [grad_mat3, grad_tall3, grad_mat4, grad_tall4] + own

    square = jnp.float32(0.0)
    for shard in group:
        square = square + jnp.sum(shard * shard)
    dp_count = lax.axis_size("dp")
    totals = lax.psum(jnp.stack([square / dp_count, loss[0, 0]]), both)
    grad_norm = jnp.sqrt(totals[0])
    clip_factor = jnp.minimum(1.0, CLIP_LEVEL / (grad_norm + 1e-06))
    results = [
        adamw(masters[at], moments[at], seconds[at], clip_factor * group[at], at >= 5) for at in range(7)
    ]
    return (
        *[result[0] for result in results],
        *[result[1] for result in results],
        *[result[2] for result in results],
        totals[1],
        image_count,
        grad_norm,
    )


def solution(mesh):
    rows, columns = P("fsdp", None), P(None, "fsdp")
    weights = (rows,) * 4 + (columns,) * 3
    images = P(None, ("dp", "fsdp"))
    in_specs = (P(None, ("dp", "fsdp"), None, None), images, images) + weights * 3
    out_specs = weights * 3 + (P(), P(), P())
    return jax.shard_map(body, mesh=mesh, in_specs=in_specs, out_specs=out_specs, check_vma=False)
```

```python
import functools

import jax
import jax.numpy as jnp
from jax import lax
from jax.experimental import pallas as pl
from jax.experimental.pallas import tpu as pltpu
from jax.sharding import PartitionSpec as P

BF = jnp.bfloat16
F32 = jnp.float32
C3 = 320
C3P = 384
H3 = 5
F3 = 1280
C4 = 512
H4 = 8
F4 = 2048
CLASSES = 1000
PATCH = 768
STEP = 10
IMGS = 4
TOK3 = 1024
TOK4 = 256
LC = 256
EPS = 1e-06
SMOOTHING = 0.1
CLIP_LEVEL = 0.001
SCALE = 0.125
VMEM_BYTES = 63 * 2**20


def contract(a, b, ca, cb):
    return lax.dot_general(a, b, (((ca,), (cb,)), ((), ())), preferred_element_type=F32)


def nn(a, b):
    return contract(a, b, 1, 0)


def nt(a, b):
    return contract(a, b, 1, 1)


def tn(a, b):
    return contract(a, b, 0, 0)


def normalize(x):
    centred = x - jnp.mean(x, axis=-1, keepdims=True)
    rstd = lax.rsqrt(jnp.mean(centred * centred, axis=-1, keepdims=True) + EPS)
    return centred * rstd, rstd


def norm_grad(dy, xhat, rstd, gain):
    dx = dy * gain
    return rstd * (dx - jnp.mean(dx, axis=-1, keepdims=True) - xhat * jnp.mean(dx * xhat, axis=-1, keepdims=True))


def column_sum(x):
    return jnp.sum(x, axis=0, keepdims=True)


def half_of(x, half):
    lane = lax.broadcasted_iota(jnp.int32, x.shape, 1)
    keep = (lane < 64) if half == 0 else (lane >= 64)
    return jnp.where(keep, x, jnp.zeros_like(x))


def softmax_rows0(scores):
    top = jnp.max(scores, axis=0, keepdims=True)
    exponent = jnp.exp(scores - top)
    return exponent * (1.0 / jnp.sum(exponent, axis=0, keepdims=True))


def gelu_both(c):
    k0 = 0.7978845608028654
    k1 = 0.044715 * k0
    c2 = c * c
    t = jnp.tanh(c * (k1 * c2 + k0))
    half = 0.5 * t + 0.5
    slope = half + c * (half - half * half) * (6.0 * k1 * c2 + 2.0 * k0)
    return c * half, slope


def shift_down(v):
    lane = lax.broadcasted_iota(jnp.int32, v.shape, 1)
    return jnp.where(lane == 0, 0.0, pltpu.roll(v, 1, 1))


def shift_up(v):
    lane = lax.broadcasted_iota(jnp.int32, v.shape, 1)
    return jnp.where(lane == 7, 0.0, pltpu.roll(v, 7, 1))


def class3(py, xm):
    return py * 4 + (xm & 1) * 2 + (xm >> 1)


def store3(plain, moved, plane, value):
    py, px = plane // 2, plane % 2
    value = value.reshape(2, 16, 8, value.shape[-1])
    for qx in range(2):
        plain[plane * 2 + qx, 1:17] = value[qx]
    if px == 1:
        moved[py * 2, 1:17] = shift_down(value[1])
    else:
        moved[py * 2 + 1, 1:17] = shift_up(value[0])


def tap3(plain, moved, py, xm, dy, dx, lanes):
    row = (py + dy) % 2
    start = 1 + (py + dy) // 2
    at = xm + dx
    if at == -1:
        return moved[row * 2, start : start + 16, :, lanes]
    if at == 4:
        return moved[row * 2 + 1, start : start + 16, :, lanes]
    return plain[class3(row, at), start : start + 16, :, lanes]


def store4(plain, moved, image, value):
    value = value.reshape(2, 16, 8, value.shape[-1])
    for qx in range(2):
        plain[image, qx, 1:17] = value[qx]
    moved[image, 0, 1:17] = shift_down(value[1])
    moved[image, 1, 1:17] = shift_up(value[0])


def tap4(plain, moved, image, qx, dy, dx, lanes):
    start = 1 + dy
    at = qx + dx
    if at == -1:
        return moved[image, 0, start : start + 16, :, lanes]
    if at == 2:
        return moved[image, 1, start : start + 16, :, lanes]
    return plain[image, at, start : start + 16, :, lanes]


def up(value, unit):
    return -(-value // unit) * unit


def rows4(shards, groups):
    return up(10 * (C4 // shards) + (4 * C3 + F4) // shards, 8 * groups)


def places3(shards, groups):
    tall = (PATCH + 4 * C3 + F3) // shards // 2
    mats = up(tall, 16)
    slot = up(C3 // shards, 8)
    flat = up(mats + 4 * slot, 16)
    flat_rows = -(-(9 * (F3 + F4) + 2 * C3 + 8 * C4) // (shards * 2 * C3))
    last = flat + up(flat_rows, 8)
    return mats, slot, flat, flat_rows, last, up(last + 8, 8 * groups)


def send_off(out, keep, send, sems, core):
    def move(at, target):
        return pltpu.make_async_copy(out.at[at], target.at[at // 2], sems.at[at])

    for at in range(out.shape[0]):

        @pl.when(core == at % 2)
        def _():
            move(at, keep).start()

        @pl.when(core != at % 2)
        def _():
            move(at, send).start()

    for at in range(out.shape[0]):
        move(at, keep).wait()


def store_columns4(out, value, column):
    size = C4 // out.shape[0]
    block, lane = column // C4, column % C4
    start = block * size
    lanes = slice(lane, lane + value.shape[1])
    if not isinstance(column, int):
        start = pl.multiple_of(start, size)
        lanes = pl.ds(pl.multiple_of(lane, LC), value.shape[1])
    for at in range(out.shape[0]):
        out[at, pl.ds(start, size), lanes] = value[at * size : at * size + size].astype(BF)


def store_rows(out, value, row, size, offset):
    at = row
    while at < row + value.shape[0]:
        shard = at // size
        end = min((shard + 1) * size, row + value.shape[0])
        start = offset + at - shard * size
        out[shard, start : start + end - at, :] = value[at - row : end - row].astype(BF)
        at = end


TAPS = [(t, t // 3 - 1, t % 3 - 1) for t in range(9)]


def embed_attend(patches, tall3, mat3, norms, z_o, h_o, red_o, q_o, k_o, v_o, p_o, mix_o, x1_o, x0_s, vt_s):
    we = tall3[0:PATCH]
    reduced = None
    for b in range(4):
        rows = pl.ds(b * 256, 256)
        z = nn(patches[0, rows, :], we)
        z_o[0, rows, :] = z
        x0 = normalize(z)[0] * norms[0:1] + norms[1:2]
        x0_s[rows, :] = x0
        h = (normalize(x0)[0] * norms[2:3] + norms[3:4]).astype(BF)
        h_o[0, rows, :] = h
        q_o[0, rows, :] = nn(h, mat3[:, 0:C3P]).astype(BF)
        part = nn(h, tall3[PATCH + C3 * b : PATCH + C3 * (b + 1)])
        reduced = part if reduced is None else reduced + part
    red_o[0] = reduced
    r = (normalize(reduced)[0] * norms[4:5] + norms[5:6]).astype(BF)
    k = nn(r, mat3[:, C3P : 2 * C3P]).astype(BF)
    v = nn(r, mat3[:, 2 * C3P : 3 * C3P]).astype(BF)
    k_o[0] = k
    v_o[0] = v
    vt_s[...] = v.T

    def queries(b, carry):
        rows = pl.ds(pl.multiple_of(b * 256, 256), 256)
        for head in range(H3):
            lanes = slice(head // 2 * 128, head // 2 * 128 + 128)
            key = half_of(k_o[0, :, lanes], head % 2)
            scores = nt(key, q_o[0, rows, lanes]) * SCALE
            soft = softmax_rows0(scores).astype(BF)
            p_o[0, head, :, rows] = soft
            mix_o[0, head * 64 : head * 64 + 64, rows] = nn(vt_s[head * 64 : head * 64 + 64, :], soft).astype(BF)
        x1_o[0, rows, :] = x0_s[rows, :] + tn(mix_o[0, :, rows], mat3[0:C3, 3 * C3P : 3 * C3P + C3])
        return carry

    lax.fori_loop(0, 4, queries, 0)


def feed3(x1, tall3, mat3, depth, norms, n_o, hid_o, slope_o, act_o, x2_o, plain, moved):
    @pl.when(pl.program_id(0) == 0)
    def _():
        for ref in (plain, moved):
            ref[:, 0:1] = jnp.zeros((ref.shape[0], 1, 8, LC), F32)
            ref[:, 17:18] = jnp.zeros((ref.shape[0], 1, 8, LC), F32)

    for b in range(4):
        rows = pl.ds(b * 256, 256)
        n_o[0, rows, :] = (normalize(x1[0, rows, :])[0] * norms[6:7] + norms[7:8]).astype(BF)

    def chunk(j, carry):
        wide = pl.ds(pl.multiple_of(j * LC, LC), LC)
        w1 = mat3[:, pl.ds(pl.multiple_of(4 * C3P + j * LC, LC), LC)]
        for plane in range(4):
            rows = pl.ds(plane * 256, 256)
            value = nn(n_o[0, rows, :], w1)
            hid_o[0, rows, wide] = value.astype(BF)
            store3(plain, moved, plane, value)
        for lt in range(LC // 128):
            lanes = pl.ds(lt * 128, 128)
            out_lanes = pl.ds(pl.multiple_of(j * LC + lt * 128, 128), 128)
            kernel = depth[:, out_lanes]
            for py in range(2):
                for xm in range(4):
                    total = None
                    for t, dy, dx in TAPS:
                        term = tap3(plain, moved, py, xm, dy, dx, lanes) * kernel[t : t + 1][None]
                        total = term if total is None else total + term
                    act, slope = gelu_both(total)
                    rows = pl.ds(class3(py, xm) * 128, 128)
                    act_o[0, rows, out_lanes] = act.reshape(128, 128).astype(BF)
                    slope_o[0, rows, out_lanes] = slope.reshape(128, 128).astype(BF)
        return carry

    lax.fori_loop(0, F3 // LC, chunk, 0)
    for b in range(4):
        rows = pl.ds(b * 256, 256)
        x2_o[0, rows, :] = (x1[0, rows, :] + nn(act_o[0, rows, :], tall3[PATCH + 4 * C3 :])).astype(BF)


def section4(
    labels, valid, inv_count, core, x2, mat4, tall4, depth, norms,
    dx2_o, keep, send, gd_o, gn_o, loss_o,
    out, sems, first, y1_s, y2_s, h_s, qkv_s, p_s, mix_s, n_s, hid_s, slope_s, act_s, plain, moved, gd_s,
):
    for ref in (plain, moved):
        for at in (0, 17):
            ref[:, :, at : at + 1] = jnp.zeros((IMGS, 2, 1, 8, LC), F32)

    w1_at = 4 * C4
    wc_at = 4 * C4 + F4
    shards = out.shape[0]
    tall_rows = (4 * C3 + F4) // shards
    tall_at = 10 * (C4 // shards)

    for i in range(IMGS):
        rows = pl.ds(i * TOK4, TOK4)
        prod = None
        for plane in range(4):
            part = nn(x2[i, plane * 256 : plane * 256 + 256, :], tall4[plane * C3 : plane * C3 + C3, :])
            prod = part if prod is None else prod + part
        first[rows, :] = prod
        y0 = normalize(prod)[0] * norms[0:1] + norms[1:2]
        y1_s[rows, :] = y0
        h_s[rows, :] = (normalize(y0)[0] * norms[2:3] + norms[3:4]).astype(BF)
    for j in range(3):
        wide = slice(j * C4, j * C4 + C4)
        for i in range(IMGS):
            rows = pl.ds(i * TOK4, TOK4)
            qkv_s[rows, wide] = nn(h_s[rows, :], mat4[:, wide]).astype(BF)

    def attend(i, carry):
        rows = pl.ds(pl.multiple_of(i * TOK4, TOK4), TOK4)
        for head in range(H4):
            pair = head // 2 * 128
            key = half_of(qkv_s[rows, C4 + pair : C4 + pair + 128], head % 2)
            scores = nt(key, qkv_s[rows, pair : pair + 128]) * SCALE
            soft = softmax_rows0(scores).astype(BF)
            p_s[i * H4 + head] = soft
            if head % 2 == 0:
                vt = qkv_s[rows, 2 * C4 + pair : 2 * C4 + pair + 128].T
            half = vt[0:64] if head % 2 == 0 else vt[64:128]
            mix_s[head * 64 : head * 64 + 64, rows] = nn(half, soft).astype(BF)
        return carry

    lax.fori_loop(0, IMGS, attend, 0)

    for i in range(IMGS):
        rows = pl.ds(i * TOK4, TOK4)
        y1 = y1_s[rows, :] + tn(mix_s[:, i * TOK4 : i * TOK4 + TOK4], mat4[:, 3 * C4 : 4 * C4])
        y1_s[rows, :] = y1
        n_s[rows, :] = (normalize(y1)[0] * norms[4:5] + norms[5:6]).astype(BF)

    def feed(j, carry):
        wide = pl.ds(pl.multiple_of(j * LC, LC), LC)
        w1 = mat4[:, pl.ds(pl.multiple_of(w1_at + j * LC, LC), LC)]
        for i in range(IMGS):
            rows = pl.ds(i * TOK4, TOK4)
            value = nn(n_s[rows, :], w1)
            hid_s[rows, wide] = value.astype(BF)
            store4(plain, moved, i, value)
        for lt in range(LC // 128):
            lanes = pl.ds(lt * 128, 128)
            out_lanes = pl.ds(pl.multiple_of(j * LC + lt * 128, 128), 128)
            kernel = depth[:, out_lanes]
            for i in range(IMGS):
                for qx in range(2):
                    total = None
                    for t, dy, dx in TAPS:
                        term = tap4(plain, moved, i, qx, dy, dx, lanes) * kernel[t : t + 1][None]
                        total = term if total is None else total + term
                    act, slope = gelu_both(total)
                    rows = pl.ds(i * TOK4 + qx * 128, 128)
                    act_s[rows, out_lanes] = act.reshape(128, 128).astype(BF)
                    slope_s[rows, out_lanes] = slope.reshape(128, 128).astype(BF)
        return carry

    lax.fori_loop(0, F4 // LC, feed, 0)

    pools = []
    hat_means = []
    for i in range(IMGS):
        rows = pl.ds(i * TOK4, TOK4)
        y2 = y1_s[rows, :] + nn(act_s[rows, :], tall4[4 * C3 :, :])
        y2_s[rows, :] = y2
        hat_mean = jnp.mean(normalize(y2)[0], axis=0, keepdims=True)
        hat_means.append(hat_mean)
        pools.append(hat_mean * norms[6:7] + norms[7:8])
    pooled = jnp.concatenate(pools + [jnp.zeros((8 - IMGS, C4), F32)], axis=0).astype(BF)
    logits = nn(pooled, mat4[:, wc_at:])

    row = lax.broadcasted_iota(jnp.int32, (8, CLASSES), 0)
    column = lax.broadcasted_iota(jnp.int32, (8, CLASSES), 1)
    target = jnp.full((8, CLASSES), -1, jnp.int32)
    present = jnp.zeros((8, CLASSES), F32)
    for i in range(IMGS):
        target = jnp.where(row == i, labels[i], target)
        present = jnp.where(row == i, valid[i].astype(F32), present)
    goal = (1.0 - SMOOTHING) * (column == target).astype(F32) + SMOOTHING / CLASSES
    shifted = logits - jnp.max(logits, axis=-1, keepdims=True)
    exponent = jnp.exp(shifted)
    mass = jnp.sum(exponent, axis=-1, keepdims=True)
    log_probs = shifted - jnp.log(mass)
    ce = -jnp.sum(goal * log_probs, axis=-1, keepdims=True)
    loss_o[...] = jnp.broadcast_to(jnp.sum(present[:, 0:1] * ce, axis=0, keepdims=True), (8, 128))
    dlogits = (present * inv_count[0] * (exponent / mass - goal)).astype(BF)

    dclass = tn(pooled, dlogits)
    store_columns4(out, dclass[:, :C4], wc_at)
    store_columns4(out, jnp.concatenate([dclass[:, C4:], jnp.zeros((C4, 2 * C4 - CLASSES), F32)], axis=1), wc_at + C4)
    if tall_at + tall_rows < out.shape[1]:
        out[:, tall_at + tall_rows :, :] = jnp.zeros((shards, out.shape[1] - tall_at - tall_rows, C4), BF)
    dpool = nt(dlogits, mat4[:, wc_at:])
    dgain = None
    for i in range(IMGS):
        rows = pl.ds(i * TOK4, TOK4)
        one = dpool[i : i + 1]
        part = one * hat_means[i]
        dgain = part if dgain is None else dgain + part
        xhat, rstd = normalize(y2_s[rows, :])
        dy2 = norm_grad(jnp.broadcast_to(one * (1.0 / TOK4), (TOK4, C4)), xhat, rstd, norms[6:7])
        y2_s[rows, :] = dy2
    gn_o[6:7] = dgain
    gn_o[7:8] = column_sum(dpool)

    dy = y2_s[...].astype(BF)
    for at in range(0, F4, 512):
        store_rows(out, tn(act_s[:, at : at + 512], dy), 4 * C3 + at, tall_rows, tall_at)
    act_s[:, 0:C4] = dy
    gd_s[...] = jnp.zeros_like(gd_s)
    nt_val = n_s[...].T

    def feed_back(j, total):
        wide = pl.ds(pl.multiple_of(j * LC, LC), LC)
        w2 = tall4[pl.ds(pl.multiple_of(4 * C3 + j * LC, LC), LC), :]
        for i in range(IMGS):
            rows = pl.ds(i * TOK4, TOK4)
            value = nt(act_s[rows, 0:C4], w2) * slope_s[rows, wide].astype(F32)
            store4(plain, moved, i, value)
        for lt in range(LC // 128):
            lanes = pl.ds(lt * 128, 128)
            out_lanes = pl.ds(pl.multiple_of(j * LC + lt * 128, 128), 128)
            kernel = depth[:, out_lanes]
            sums = [None] * 9
            for i in range(IMGS):
                for qx in range(2):
                    rows = pl.ds(i * TOK4 + qx * 128, 128)
                    base = hid_s[rows, out_lanes].astype(F32).reshape(16, 8, 128)
                    acc = None
                    for t, dy, dx in TAPS:
                        value = tap4(plain, moved, i, qx, -dy, -dx, lanes)
                        term = value * kernel[t : t + 1][None]
                        acc = term if acc is None else acc + term
                        part = jnp.sum(value * base, axis=0)
                        sums[t] = part if sums[t] is None else sums[t] + part
                    hid_s[rows, out_lanes] = acc.reshape(128, 128).astype(BF)
            for t in range(9):
                gd_s[t, :, out_lanes] = sums[t]
        dhid = hid_s[:, wide]
        store_columns4(out, nn(nt_val, dhid), w1_at + j * LC)
        return total

    lax.fori_loop(0, F4 // LC, feed_back, 0)
    for t in range(9):
        gd_o[t : t + 1, :] = column_sum(gd_s[t])

    dgain = dshift = None
    for i in range(IMGS):
        rows = pl.ds(i * TOK4, TOK4)
        dn = nt(hid_s[rows, :], mat4[:, w1_at : w1_at + F4])
        xhat, rstd = normalize(y1_s[rows, :])
        part_g, part_s = column_sum(dn * xhat), column_sum(dn)
        dgain = part_g if dgain is None else dgain + part_g
        dshift = part_s if dshift is None else dshift + part_s
        y2_s[rows, :] = y2_s[rows, :] + norm_grad(dn, xhat, rstd, norms[4:5])
    gn_o[4:5] = dgain
    gn_o[5:6] = dshift

    dprod = y2_s[...].astype(BF)
    store_columns4(out, nn(mix_s[...], dprod), 3 * C4)
    for i in range(IMGS):
        rows = pl.ds(i * TOK4, TOK4)
        n_s[rows, :] = nt(dprod[i * TOK4 : i * TOK4 + TOK4], mat4[:, 3 * C4 : 4 * C4]).astype(BF)

    def attend_back(i, carry):
        rows = pl.ds(pl.multiple_of(i * TOK4, TOK4), TOK4)
        lane = lax.broadcasted_iota(jnp.int32, (TOK4, 128), 1)
        for pair in range(H4 // 2):
            at = pair * 128
            q = qkv_s[rows, at : at + 128]
            k = qkv_s[rows, C4 + at : C4 + at + 128]
            v = qkv_s[rows, 2 * C4 + at : 2 * C4 + at + 128]
            do = n_s[rows, at : at + 128]
            kt = k.T
            dqts, dks, dvs = [], [], []
            for half in range(2):
                soft = p_s[i * H4 + pair * 2 + half]
                dp = nt(half_of(v, half), do)
                wide_soft = soft.astype(F32)
                ds = wide_soft * (dp - jnp.sum(dp * wide_soft, axis=0, keepdims=True))
                ds = ds.astype(BF)
                dvs.append(nn(soft, do))
                dks.append(nn(ds, q))
                dqts.append(nn(kt[half * 64 : half * 64 + 64], ds))
            dqt = (jnp.concatenate(dqts, axis=0) * SCALE).astype(BF)
            qkv_s[rows, at : at + 128] = dqt.T
            qkv_s[rows, C4 + at : C4 + at + 128] = (jnp.where(lane < 64, dks[0], dks[1]) * SCALE).astype(BF)
            qkv_s[rows, 2 * C4 + at : 2 * C4 + at + 128] = jnp.where(lane < 64, dvs[0], dvs[1]).astype(BF)
        return carry

    lax.fori_loop(0, IMGS, attend_back, 0)
    ht = h_s[...].T
    for j in range(3):
        wide = slice(j * C4, j * C4 + C4)
        store_columns4(out, nn(ht, qkv_s[:, wide]), j * C4)

    sums = [None] * 4
    for i in range(IMGS):
        rows = pl.ds(i * TOK4, TOK4)
        dh = nt(qkv_s[rows, :], mat4[:, 0 : 3 * C4])
        hat0, rstd0 = normalize(first[rows, :])
        hat1, rstd1 = normalize(hat0 * norms[0:1] + norms[1:2])
        dy0 = y2_s[rows, :] + norm_grad(dh, hat1, rstd1, norms[2:3])
        dprod0 = norm_grad(dy0, hat0, rstd0, norms[0:1]).astype(BF)
        n_s[rows, :] = dprod0
        parts = [column_sum(dy0 * hat0), column_sum(dy0), column_sum(dh * hat1), column_sum(dh)]
        sums = [part if old is None else old + part for old, part in zip(sums, parts)]
        for plane in range(4):
            dx2_o[i, plane * 256 : plane * 256 + 256, :] = nt(dprod0, tall4[plane * C3 : plane * C3 + C3, :]).astype(BF)
    gn_o[0:4] = jnp.concatenate(sums, axis=0)
    for plane in range(4):
        total = None
        for i in range(IMGS):
            part = tn(x2[i, plane * 256 : plane * 256 + 256, :], n_s[i * TOK4 : i * TOK4 + TOK4, :])
            total = part if total is None else total + part
        store_rows(out, total, plane * C3, tall_rows, tall_at)
    send_off(out, keep, send, sems, core[0])


def feed3_back(dx2, x1, n, hid, slope, act, tall3, mat3, depth, norms, dx1_o, g1_o, g2_o, gd_o, gn_o,
               acc1, acc2, accd, accn, plain, moved, dy_s, dyt_s, nt_s, da_s):
    step = pl.program_id(0)

    @pl.when(step == 0)
    def _():
        for ref in (plain, moved):
            ref[:, 0:1] = jnp.zeros((ref.shape[0], 1, 8, LC), F32)
            ref[:, 17:18] = jnp.zeros((ref.shape[0], 1, 8, LC), F32)
        for ref in (acc1, acc2, accd, accn):
            ref[...] = jnp.zeros_like(ref)

    dy = dx2[0]
    dy_s[...] = dy
    dyt_s[...] = dy.T
    nt_s[...] = n[0].T

    def chunk(j, carry):
        wide = pl.ds(pl.multiple_of(j * LC, LC), LC)
        w2 = tall3[pl.ds(pl.multiple_of(PATCH + 4 * C3 + j * LC, LC), LC), :]
        for plane in range(4):
            rows = pl.ds(plane * 256, 256)
            value = nt(dy_s[rows, :], w2) * slope[0, rows, wide].astype(F32)
            store3(plain, moved, plane, value)
        for lt in range(LC // 128):
            lanes = pl.ds(lt * 128, 128)
            out_lanes = pl.ds(pl.multiple_of(j * LC + lt * 128, 128), 128)
            kernel = depth[:, out_lanes]
            sums = [None] * 9
            for py in range(2):
                for xm in range(4):
                    rows = pl.ds(class3(py, xm) * 128, 128)
                    base = hid[0, rows, out_lanes].astype(F32).reshape(16, 8, 128)
                    out = None
                    for t, dy, dx in TAPS:
                        value = tap3(plain, moved, py, xm, -dy, -dx, lanes)
                        term = value * kernel[t : t + 1][None]
                        out = term if out is None else out + term
                        part = jnp.sum(value * base, axis=0)
                        sums[t] = part if sums[t] is None else sums[t] + part
                    da_s[rows, out_lanes] = out.reshape(128, 128).astype(BF)
            for t in range(9):
                accd[t, :, out_lanes] += sums[t]
        da = da_s[:, wide]
        acc1[:, wide] += nn(nt_s[...], da)
        acc2[:, wide] += nn(dyt_s[...], act[0, :, wide])
        return carry

    lax.fori_loop(0, F3 // LC, chunk, 0)
    for b in range(4):
        rows = pl.ds(b * 256, 256)
        dn = nt(da_s[rows, :], mat3[:, 4 * C3P :])
        xhat, rstd = normalize(x1[0, rows, :])
        accn[0:1] += column_sum(dn * xhat)
        accn[1:2] += column_sum(dn)
        dx1_o[0, rows, :] = dx2[0, rows, :].astype(F32) + norm_grad(dn, xhat, rstd, norms[6:7])

    @pl.when(step == IMGS - 1)
    def _():
        g1_o[...] = acc1[...].astype(g1_o.dtype)
        g2_o[...] = acc2[...].T.astype(g2_o.dtype)
        gn_o[...] = accn[...]
        for t in range(9):
            gd_o[t : t + 1, :] = column_sum(accd[t])


def attend3_back(groups, core, dx1, z, h, red, q, k, v, p, mix, patches, tall3, mat3, norms, g1, g2, flat, keep, send, out, sems,
                 tall_s, acce, accr, accq, acck, accv, acco, accn, dk_s, dv_s, kt_s, dqt_s, dr_s):
    step = pl.program_id(0)

    @pl.when(step == 0)
    def _():
        for ref in (acce, accr, accq, acck, accv, acco, accn):
            ref[...] = jnp.zeros_like(ref)

    kt_s[...] = k[0].T
    dk_s[...] = jnp.zeros_like(dk_s)
    dv_s[...] = jnp.zeros_like(dv_s)
    wo = mat3[0:C3, 3 * C3P : 3 * C3P + C3]
    lane = lax.broadcasted_iota(jnp.int32, (256, 128), 1)

    def queries(b, carry):
        rows = pl.ds(pl.multiple_of(b * 256, 256), 256)
        dprod = dx1[0, rows, :].astype(BF)
        acco[...] += nn(mix[0, :, rows], dprod)
        dmix = nt(dprod, wo).astype(BF)
        dmix = jnp.concatenate([dmix, jnp.zeros((256, C3P - C3), BF)], axis=1)
        for pair in range(3):
            lanes = slice(pair * 128, pair * 128 + 128)
            do = dmix[:, lanes]
            qp = q[0, rows, lanes]
            dks, dvs = [], []
            for half in range(2 if pair < 2 else 1):
                head = pair * 2 + half
                soft = p[0, head, :, rows]
                dp = nt(half_of(v[0, :, lanes], half), do)
                wide_soft = soft.astype(F32)
                ds = wide_soft * (dp - jnp.sum(dp * wide_soft, axis=0, keepdims=True))
                ds = ds.astype(BF)
                dvs.append(nn(soft, do))
                dks.append(nn(ds, qp))
                dqt = nn(kt_s[head * 64 : head * 64 + 64, :], ds) * SCALE
                dqt_s[head * 64 : head * 64 + 64, rows] = dqt.astype(BF)
            if len(dks) == 2:
                dk_s[:, lanes] += jnp.where(lane < 64, dks[0], dks[1])
                dv_s[:, lanes] += jnp.where(lane < 64, dvs[0], dvs[1])
            else:
                dk_s[:, lanes] += dks[0]
                dv_s[:, lanes] += dvs[0]
        return carry

    lax.fori_loop(0, 4, queries, 0)

    dk = (dk_s[...] * SCALE).astype(BF)
    dv = dv_s[...].astype(BF)
    hat_r, rstd_r = normalize(red[0])
    r = (hat_r * norms[4:5] + norms[5:6]).astype(BF)
    acck[...] += tn(r, dk)
    accv[...] += tn(r, dv)
    dr = nt(dk, mat3[:, C3P : 2 * C3P]) + nt(dv, mat3[:, 2 * C3P : 3 * C3P])
    accn[4:5] += column_sum(dr * hat_r)
    accn[5:6] += column_sum(dr)
    dred = norm_grad(dr, hat_r, rstd_r, norms[4:5]).astype(BF)
    accq[...] += nn(dqt_s[...], h[0])
    for b in range(4):
        rows = pl.ds(b * 256, 256)
        wr = tall3[PATCH + C3 * b : PATCH + C3 * (b + 1)]
        accr[C3 * b : C3 * (b + 1)] += tn(h[0, rows, :], dred)
        dh = tn(dqt_s[:, rows], mat3[:, 0:C3].T) + nt(dred, wr)
        hat0, rstd0 = normalize(z[0, rows, :])
        hat1, rstd1 = normalize(hat0 * norms[0:1] + norms[1:2])
        accn[2:3] += column_sum(dh * hat1)
        accn[3:4] += column_sum(dh)
        dx0 = dx1[0, rows, :] + norm_grad(dh, hat1, rstd1, norms[2:3])
        accn[0:1] += column_sum(dx0 * hat0)
        accn[1:2] += column_sum(dx0)
        dz = norm_grad(dx0, hat0, rstd0, norms[0:1]).astype(BF)
        acce[...] += tn(dz, patches[0, rows, :])

    @pl.when(step == IMGS - 1)
    def _():
        shards = out.shape[0]
        mats, slot, flat_at, flat_rows, last, total_rows = places3(shards, groups)
        mat_rows = C3 // shards
        tall = (PATCH + 4 * C3 + F3) // shards // 2
        out[:, mats:, :] = jnp.zeros((shards, total_rows - mats, 2 * C3), BF)
        if tall < mats:
            out[:, tall:mats, :] = jnp.zeros((shards, mats - tall, 2 * C3), BF)
        tall_s[0:PATCH] = acce[...].T
        tall_s[PATCH : PATCH + 4 * C3] = accr[...]
        tall_s[PATCH + 4 * C3 :] = g2[...].astype(F32)
        accq[...] = accq[...].T
        for at in range(shards):
            rows = slice(at * mat_rows, at * mat_rows + mat_rows)
            pieces = [accq[rows, :], acck[rows, 0:C3], accv[rows, 0:C3], acco[rows, :]]
            start = at * 2 * tall
            pairs = [tall_s[start : start + tall], tall_s[start + tall : start + 2 * tall]]
            out[at, 0:tall, :] = jnp.concatenate(pairs, axis=1).astype(BF)
            for b in range(2):
                pair = jnp.concatenate(pieces[2 * b : 2 * b + 2], axis=1)
                out[at, mats + b * slot : mats + b * slot + mat_rows, :] = pair.astype(BF)
                feed = g1[rows, b * 2 * C3 : b * 2 * C3 + 2 * C3]
                out[at, mats + (b + 2) * slot : mats + (b + 2) * slot + mat_rows, :] = feed.astype(BF)
            out[at, flat_at : flat_at + flat_rows, :] = flat[at]
            out[at, last : last + 6, 0:mat_rows] = accn[:, rows].astype(BF)
        send_off(out, keep, send, sems, core[0])


def whole(shape, dtype=None):
    return pl.BlockSpec(shape, lambda i: (0,) * len(shape), pipeline_mode=pl.Buffered(1))


def per_image(*shape):
    return pl.BlockSpec((1,) + shape, lambda i: (i,) + (0,) * len(shape))


def sds(*shape, dtype=F32):
    return jax.ShapeDtypeStruct(shape, dtype)


def work(microseconds):
    return pl.CostEstimate(flops=microseconds * 10**9, bytes_accessed=microseconds * 3 * 10**6, transcendentals=0)


PARAMS = pltpu.CompilerParams(vmem_limit_bytes=VMEM_BYTES, dimension_semantics=("arbitrary",))


def run_embed_attend(patches, tall3, mat3, norms3):
    return pl.pallas_call(
        embed_attend,
        grid=(IMGS,),
        in_specs=[per_image(TOK3, PATCH), whole(tall3.shape), whole(mat3.shape), whole(norms3.shape)],
        out_specs=[
            per_image(TOK3, C3), per_image(TOK3, C3), per_image(256, C3), per_image(TOK3, C3P), per_image(256, C3P),
            per_image(256, C3P), per_image(H3, 256, TOK3), per_image(C3, TOK3), per_image(TOK3, C3),
        ],
        out_shape=[
            sds(IMGS, TOK3, C3), sds(IMGS, TOK3, C3, dtype=BF), sds(IMGS, 256, C3), sds(IMGS, TOK3, C3P, dtype=BF),
            sds(IMGS, 256, C3P, dtype=BF), sds(IMGS, 256, C3P, dtype=BF), sds(IMGS, H3, 256, TOK3, dtype=BF),
            sds(IMGS, C3, TOK3, dtype=BF), sds(IMGS, TOK3, C3),
        ],
        scratch_shapes=[pltpu.VMEM((TOK3, C3), F32), pltpu.VMEM((C3P, 256), BF)],
        compiler_params=PARAMS,
        name="embed_attend",
        cost_estimate=work(58),
    )(patches, tall3, mat3, norms3)


def run_feed3(x1, tall3, mat3, depth, norms3):
    return pl.pallas_call(
        feed3,
        grid=(IMGS,),
        in_specs=[per_image(TOK3, C3), whole(tall3.shape), whole(mat3.shape), whole(depth.shape), whole(norms3.shape)],
        out_specs=[per_image(TOK3, C3), per_image(TOK3, F3), per_image(TOK3, F3), per_image(TOK3, F3), per_image(TOK3, C3)],
        out_shape=[
            sds(IMGS, TOK3, C3, dtype=BF), sds(IMGS, TOK3, F3, dtype=BF), sds(IMGS, TOK3, F3, dtype=BF),
            sds(IMGS, TOK3, F3, dtype=BF), sds(IMGS, TOK3, C3, dtype=BF),
        ],
        scratch_shapes=[pltpu.VMEM((8, 18, 8, LC), F32), pltpu.VMEM((4, 18, 8, LC), F32)],
        compiler_params=PARAMS,
        name="feed3",
        cost_estimate=work(47),
    )(x1, tall3, mat3, depth, norms3)


def run_section4(labels, valid, inv_count, core, x2, mat4, tall4, depth, norms4, shards, groups):
    vm = pl.BlockSpec(memory_space=pltpu.VMEM)
    sm = pl.BlockSpec(memory_space=pltpu.SMEM)
    hbm = pl.BlockSpec(memory_space=pl.ANY)
    rows = IMGS * TOK4
    half = sds(shards // 2, rows4(shards, groups), C4, dtype=BF)
    return pl.pallas_call(
        section4,
        in_specs=[sm, sm, sm, sm, vm, vm, vm, vm, vm],
        out_specs=[vm, hbm, hbm, vm, vm, vm],
        out_shape=[
            sds(IMGS, TOK3, C3, dtype=BF), half, half, sds(9, F4), sds(8, C4),
            sds(8, 128),
        ],
        scratch_shapes=[
            pltpu.VMEM((shards,) + half.shape[1:], BF), pltpu.SemaphoreType.DMA((shards,)),
            pltpu.VMEM((rows, C4), F32), pltpu.VMEM((rows, C4), F32), pltpu.VMEM((rows, C4), F32),
            pltpu.VMEM((rows, C4), BF), pltpu.VMEM((rows, 3 * C4), BF), pltpu.VMEM((IMGS * H4, 256, 256), BF),
            pltpu.VMEM((C4, rows), BF), pltpu.VMEM((rows, C4), BF), pltpu.VMEM((rows, F4), BF),
            pltpu.VMEM((rows, F4), BF), pltpu.VMEM((rows, F4), BF), pltpu.VMEM((IMGS, 2, 18, 8, LC), F32),
            pltpu.VMEM((IMGS, 2, 18, 8, LC), F32), pltpu.VMEM((9, 8, F4), F32),
        ],
        compiler_params=pltpu.CompilerParams(vmem_limit_bytes=VMEM_BYTES),
        name="section4",
        cost_estimate=work(90),
    )(labels, valid, inv_count, core, x2, mat4, tall4, depth, norms4)


def run_feed3_back(dx2, x1, n, hid, slope, act, tall3, mat3, depth, norms3):
    return pl.pallas_call(
        feed3_back,
        grid=(IMGS,),
        in_specs=[
            per_image(TOK3, C3), per_image(TOK3, C3), per_image(TOK3, C3), per_image(TOK3, F3), per_image(TOK3, F3),
            per_image(TOK3, F3), whole(tall3.shape), whole(mat3.shape), whole(depth.shape), whole(norms3.shape),
        ],
        out_specs=[per_image(TOK3, C3), whole((C3, F3)), whole((F3, C3)), whole((9, F3)), whole((2, C3))],
        out_shape=[sds(IMGS, TOK3, C3), sds(C3, F3), sds(F3, C3, dtype=BF), sds(9, F3), sds(2, C3)],
        scratch_shapes=[
            pltpu.VMEM((C3, F3), F32), pltpu.VMEM((C3, F3), F32), pltpu.VMEM((9, 8, F3), F32), pltpu.VMEM((2, C3), F32),
            pltpu.VMEM((8, 18, 8, LC), F32), pltpu.VMEM((4, 18, 8, LC), F32), pltpu.VMEM((TOK3, C3), BF),
            pltpu.VMEM((C3, TOK3), BF), pltpu.VMEM((C3, TOK3), BF), pltpu.VMEM((TOK3, F3), BF),
        ],
        compiler_params=PARAMS,
        name="feed3_back",
        cost_estimate=work(68),
    )(dx2, x1, n, hid, slope, act, tall3, mat3, depth, norms3)


def run_attend3_back(core, dx1, z, h, red, q, k, v, p, mix, patches, tall3, mat3, norms3, g1, g2, flat, groups):
    shards = flat.shape[0]
    total_rows = places3(shards, groups)[-1]
    return pl.pallas_call(
        functools.partial(attend3_back, groups),
        grid=(IMGS,),
        in_specs=[
            pl.BlockSpec(memory_space=pltpu.SMEM),
            per_image(TOK3, C3), per_image(TOK3, C3), per_image(TOK3, C3), per_image(256, C3), per_image(TOK3, C3P),
            per_image(256, C3P), per_image(256, C3P), per_image(H3, 256, TOK3), per_image(C3, TOK3),
            per_image(TOK3, PATCH), whole(tall3.shape), whole(mat3.shape), whole(norms3.shape),
            whole(g1.shape), whole(g2.shape), whole(flat.shape),
        ],
        out_specs=[pl.BlockSpec(memory_space=pl.ANY)] * 2,
        out_shape=[sds(shards // 2, total_rows, 2 * C3, dtype=BF)] * 2,
        scratch_shapes=[
            pltpu.VMEM((shards, total_rows, 2 * C3), BF), pltpu.SemaphoreType.DMA((shards,)),
            pltpu.VMEM((PATCH + 4 * C3 + F3, C3), F32),
            pltpu.VMEM((C3, PATCH), F32), pltpu.VMEM((4 * C3, C3), F32), pltpu.VMEM((C3, C3), F32),
            pltpu.VMEM((C3, C3P), F32), pltpu.VMEM((C3, C3P), F32), pltpu.VMEM((C3, C3), F32), pltpu.VMEM((6, C3), F32),
            pltpu.VMEM((256, C3P), F32), pltpu.VMEM((256, C3P), F32), pltpu.VMEM((C3P, 256), BF),
            pltpu.VMEM((C3, TOK3), BF), pltpu.VMEM((256, C3), F32),
        ],
        compiler_params=PARAMS,
        name="attend3_back",
        cost_estimate=work(65),
    )(core, dx1, z, h, red, q, k, v, p, mix, patches, tall3, mat3, norms3, g1, g2, flat)


def pad_mat3(mat):
    pieces = [mat[:, at * C3 : at * C3 + C3] for at in range(4)]
    pieces = [jnp.pad(piece, ((0, 0), (0, C3P - C3))) for piece in pieces]
    return jnp.concatenate(pieces + [mat[:, 4 * C3 :]], axis=1)


def reorder(patches):
    count = patches.shape[0]
    grid = patches.reshape(count, 16, 2, 8, 2, 2, patches.shape[-1])
    return grid.transpose(0, 2, 5, 4, 1, 3, 6).reshape(patches.shape)


def swap(value, axis, mask):
    return lax.ppermute(value, axis, [(at, at ^ mask) for at in range(lax.axis_size(axis))])


def pick(value, index, axis=0):
    return lax.dynamic_index_in_dim(value, index, axis, keepdims=False)


def add_all(own, parts):
    total = own.astype(F32)
    for part in parts:
        total = total + part.astype(F32)
    return total


def chip_sends(keep, got):
    chip = lax.axis_index("fsdp") // 2
    sums = [add_all(pick(keep, chip ^ mask), [pick(got, chip ^ mask)]) for mask in range(keep.shape[0])]
    return sums[0], [one.astype(BF) for one in sums[1:]]


def depth_sends(shard):
    count, me = lax.axis_size("dp"), lax.axis_index("dp")
    cut = shard.reshape(count, shard.shape[0] // count, shard.shape[1])
    return pick(cut, me), [pick(cut, me ^ mask).astype(BF) for mask in range(1, count)]


def exchange(sends, axis, unit):
    return [swap(send, axis, unit * (at + 1)) for at, send in enumerate(sends)]


def depth_gather(piece):
    count, me = lax.axis_size("dp"), lax.axis_index("dp")
    narrow = piece.astype(BF)
    parts = [narrow] + [swap(narrow, "dp", mask) for mask in range(1, count)]
    placed = [lax.select_n(me, *[parts[at ^ other] for other in range(count)]) for at in range(count)]
    return jnp.concatenate(placed, axis=0).astype(F32)


def total_over(axis, value):
    mask = 1
    while mask < lax.axis_size(axis):
        value = value + swap(value, axis, mask)
        mask *= 2
    return value


def total_over_all(row):
    count = lax.axis_size("dp") * lax.axis_size("fsdp")
    rows = jnp.broadcast_to(row, (count, row.shape[1]))
    return jnp.sum(lax.all_to_all(rows, ("dp", "fsdp"), 0, 0, tiled=True), axis=0, keepdims=True)


def adamw(master, moment, second, gradient, is_norm):
    step_rate = 0.5 if is_norm else 0.05
    decay_now = 0.0 if is_norm else 0.05
    first = 0.9 * moment + 0.1 * gradient
    second_new = 0.999 * second + 0.001 * gradient * gradient
    first_hat = first / (1.0 - 0.9**STEP)
    second_hat = second_new / (1.0 - 0.999**STEP)
    updated = master - step_rate * (first_hat / (jnp.sqrt(second_hat) + 1e-08) + decay_now * master)
    return (updated, first, second_new)


def body(patches, labels, valid, *state):
    masters, moments, seconds = state[0:7], state[7:14], state[14:21]
    shards, groups = lax.axis_size("fsdp"), lax.axis_size("dp")
    mat3, tall3, mat4, tall4, depth, norms3, norms4 = [master.astype(BF) for master in masters]
    half, m_rows = tall3.shape[0] // 2, mat3.shape[0]
    pack = [jnp.concatenate([tall3[:half], tall3[half:]], axis=1)]
    pack += [mat3[:, at * 2 * C3 : at * 2 * C3 + 2 * C3] for at in range(4)]
    pack = lax.all_gather(jnp.concatenate(pack, axis=0), "fsdp", axis=0)

    small = [jnp.pad(piece.T, ((0, 0), (0, 16 - piece.shape[0]))) for piece in (depth, norms3, norms4)]
    small.append(jnp.full((8, 16), jnp.sum(valid)).astype(BF))
    sizes = [piece.shape[0] for piece in small]
    small = lax.all_gather(jnp.concatenate(small, axis=0), "fsdp", axis=0)
    edges = [0, sizes[0], sizes[0] + sizes[1], sum(sizes[:3])]
    parts = [small[:, edges[at] : edges[at + 1]].reshape(-1, 16).T.astype(F32) for at in range(3)]
    depth_all, norms3_all, norms4_all = parts[0][:9], parts[1][:8], parts[2][:8]
    present = jnp.full((8, 128), jnp.sum(small[:, edges[3], 0].astype(F32)))
    image_count = total_over("dp", present)[0, 0]
    inv_count = (1.0 / image_count).reshape(1)

    tall3_all = jnp.concatenate([pack[:, :half, :C3], pack[:, :half, C3:]], axis=1).reshape(-1, C3)
    mats = pack[:, half:].reshape(shards, 4, m_rows, 2 * C3).transpose(1, 0, 2, 3).reshape(4, C3, 2 * C3)
    mat3_all = [mats[at // 2, :, at % 2 * C3 : at % 2 * C3 + C3] for at in range(4)]
    mat3_all = [jnp.pad(piece, ((0, 0), (0, C3P - C3))) for piece in mat3_all]
    mat3_all = jnp.concatenate(mat3_all + [mats[2], mats[3]], axis=1)
    tall4_all = lax.all_gather(tall4, "fsdp", axis=0, tiled=True)
    mat4_all = lax.all_gather(mat4, "fsdp", axis=0, tiled=True)

    patches = reorder(patches.reshape(IMGS, TOK3, PATCH))
    depth3, depth4 = depth_all[:, :F3], depth_all[:, F3:]
    z, h, red, q, k, v, p, mix, x1 = run_embed_attend(patches, tall3_all, mat3_all, norms3_all)
    n, hid, slope, act, x2 = run_feed3(x1, tall3_all, mat3_all, depth3, norms3_all)
    core = (lax.axis_index("fsdp") % 2).reshape(1)
    dx2, keep4, send4, gd4, gn4, loss = run_section4(
        labels.reshape(IMGS), valid.reshape(IMGS), inv_count, core, x2, mat4_all, tall4_all, depth4, norms4_all,
        shards, groups,
    )

    own4, sends4 = chip_sends(keep4, swap(send4, "fsdp", 1))
    dx2, own4, sends4 = lax.optimization_barrier((dx2, own4, sends4))
    got4 = exchange(sends4, "fsdp", 2)
    dx1, g1, g2, gd3, gn3b = run_feed3_back(dx2, x1, n, hid, slope, act, tall3_all, mat3_all, depth3, norms3_all)
    dx1, own4, got4 = lax.optimization_barrier((dx1, own4, got4))
    own4, sends4 = depth_sends(add_all(own4, got4))

    def by_columns(grad):
        return grad.reshape(grad.shape[0], shards, -1).transpose(1, 0, 2).reshape(shards, -1)

    _, slot, flat_at, flat_rows, last, _ = places3(shards, groups)
    flat = jnp.concatenate([by_columns(grad) for grad in (jnp.concatenate([gd3, gd4], axis=1), gn3b, gn4)], axis=1)
    flat = jnp.pad(flat, ((0, 0), (0, flat_rows * 2 * C3 - flat.shape[1])))
    flat = flat.reshape(shards, flat_rows, 2 * C3).astype(BF)
    dx1, own4, sends4, flat = lax.optimization_barrier((dx1, own4, sends4, flat))
    got4 = exchange(sends4, "dp", 1)
    keep3, send3 = run_attend3_back(
        core, dx1, z, h, red, q, k, v, p, mix, patches, tall3_all, mat3_all, norms3_all, g1, g2, flat, groups
    )
    keep3, send3, got4 = lax.optimization_barrier((keep3, send3, got4))
    piece4 = add_all(own4, got4)
    own3, sends3 = chip_sends(keep3, swap(send3, "fsdp", 1))
    own3, sends3, piece4 = lax.optimization_barrier((own3, sends3, piece4))
    got3 = exchange(sends3, "fsdp", 2)
    grads4 = depth_gather(piece4)
    own3, got3, grads4 = lax.optimization_barrier((own3, got3, grads4))
    own3, sends3 = depth_sends(add_all(own3, got3))
    piece3 = add_all(own3, exchange(sends3, "dp", 1))
    square = jnp.sum(piece4 * piece4) + jnp.sum(piece3 * piece3)
    lane = lax.broadcasted_iota(jnp.int32, (1, 128), 1)
    totals = total_over_all(jnp.where(lane == 0, square, loss[0:1]))
    grads3 = depth_gather(piece3)

    m_rows, t_rows = C4 // shards, masters[3].shape[0]
    blocks4 = [grads4[at * m_rows : at * m_rows + m_rows] for at in range(10)]
    grad_mat4 = jnp.concatenate(blocks4, axis=1)[:, : masters[2].shape[1]]
    grad_tall4 = grads4[10 * m_rows : 10 * m_rows + t_rows]
    t_rows, m_rows = masters[1].shape[0], masters[0].shape[0]
    mats_at, half = up(t_rows // 2, 16), t_rows // 2
    grad_tall3 = jnp.concatenate([grads3[:half, :C3], grads3[:half, C3:]], axis=0)
    grad_mat3 = jnp.concatenate([grads3[mats_at + at * slot : mats_at + at * slot + m_rows] for at in range(4)], axis=1)
    flat = grads3[flat_at : flat_at + flat_rows].reshape(-1)
    sizes = [9 * t_rows, 2 * m_rows, masters[6].size]
    grad_depth = flat[: sizes[0]].reshape(9, t_rows)
    grad_norms3 = jnp.concatenate(
        [grads3[last : last + 6, :m_rows], flat[sizes[0] : sizes[0] + sizes[1]].reshape(2, m_rows)], axis=0
    )
    grad_norms4 = flat[sizes[0] + sizes[1] : sum(sizes)].reshape(masters[6].shape)
    group = [grad_mat3, grad_tall3, grad_mat4, grad_tall4, grad_depth, grad_norms3, grad_norms4]

    grad_norm = jnp.sqrt(totals[0, 0])
    clip_factor = jnp.minimum(1.0, CLIP_LEVEL / (grad_norm + 1e-06))
    results = [adamw(masters[at], moments[at], seconds[at], clip_factor * group[at], at >= 5) for at in range(7)]
    return (
        *[result[0] for result in results],
        *[result[1] for result in results],
        *[result[2] for result in results],
        totals[0, 1],
        image_count,
        grad_norm,
    )


def solution(mesh):
    rows, columns = P("fsdp", None), P(None, "fsdp")
    weights = (rows,) * 4 + (columns,) * 3
    images = P(None, ("dp", "fsdp"))
    in_specs = (P(None, ("dp", "fsdp"), None, None), images, images) + weights * 3
    out_specs = weights * 3 + (P(), P(), P())
    return jax.shard_map(body, mesh=mesh, in_specs=in_specs, out_specs=out_specs, check_vma=False)
```

```python
import functools
import math

import jax
import jax.numpy as jnp
from jax import lax
from jax.experimental import pallas as pl
from jax.experimental.pallas import tpu as pltpu
from jax.sharding import PartitionSpec as P

BF = jnp.bfloat16
F32 = jnp.float32
C3 = 320
C3P = 384
H3 = 5
F3 = 1280
C4 = 512
H4 = 8
F4 = 2048
CLASSES = 1000
PATCH = 768
STEP = 10
IMGS = 4
TOK3 = 1024
TOK4 = 256
LC = 256
PART = 8
EPS = 1e-06
SMOOTHING = 0.1
CLIP_LEVEL = 0.001
SCALE = 0.125
LOG2_E = 1.4426950408889634
VMEM_BYTES = 63 * 2**20


def contract(a, b, ca, cb):
    return lax.dot_general(a, b, (((ca,), (cb,)), ((), ())), preferred_element_type=F32)


def nn(a, b):
    return contract(a, b, 1, 0)


def nt(a, b):
    return contract(a, b, 1, 1)


def tn(a, b):
    return contract(a, b, 0, 0)


def normalize(x):
    centred = x - jnp.mean(x, axis=-1, keepdims=True)
    rstd = lax.rsqrt(jnp.mean(centred * centred, axis=-1, keepdims=True) + EPS)
    return centred * rstd, rstd


def norm_grad(dy, xhat, rstd, gain):
    dx = dy * gain
    return rstd * (dx - jnp.mean(dx, axis=-1, keepdims=True) - xhat * jnp.mean(dx * xhat, axis=-1, keepdims=True))


def fold(x, op):
    x = x.reshape(x.shape[0] // 8, 8, x.shape[1])
    while x.shape[0] > 1:
        half = x.shape[0] // 2
        x = op(x[:half], x[half:])
    return x[0]


def column_sum(x):
    return jnp.sum(fold(x, jnp.add), axis=0, keepdims=True)


def half_of(x, half):
    lane = lax.broadcasted_iota(jnp.int32, x.shape, 1)
    keep = (lane < 64) if half == 0 else (lane >= 64)
    return jnp.where(keep, x, jnp.zeros_like(x))


def softmax_rows0(scores):
    top = jnp.max(fold(scores, jnp.maximum), axis=0, keepdims=True)
    exponent = jnp.exp2((scores - top) * (SCALE * LOG2_E))
    return exponent * (1.0 / column_sum(exponent))


def softmax_grad(soft, grad):
    mean = column_sum(grad * soft) / column_sum(soft)
    return soft * (grad - mean)


def gelu_both(c):
    k0 = 0.7978845608028654
    k1 = 0.044715 * k0
    c2 = c * c
    t = jnp.tanh(c * (k1 * c2 + k0))
    half = 0.5 * t + 0.5
    slope = half + c * (half - half * half) * (6.0 * k1 * c2 + 2.0 * k0)
    return c * half, slope


def shift_down(v):
    lane = lax.broadcasted_iota(jnp.int32, v.shape, 1)
    return jnp.where(lane == 0, 0.0, pltpu.roll(v, 1, 1))


def shift_up(v):
    lane = lax.broadcasted_iota(jnp.int32, v.shape, 1)
    return jnp.where(lane == 7, 0.0, pltpu.roll(v, 7, 1))


def class3(py, xm):
    return py * 4 + (xm & 1) * 2 + (xm >> 1)


def store3(plain, moved, plane, value):
    py, px = plane // 2, plane % 2
    value = value.reshape(2, 16, 8, value.shape[-1])
    for qx in range(2):
        plain[plane * 2 + qx, 1:17] = value[qx]
    if px == 1:
        moved[py * 2, 1:17] = shift_down(value[1])
    else:
        moved[py * 2 + 1, 1:17] = shift_up(value[0])


def tap3(plain, moved, py, xm, dy, dx, part, lanes):
    row = (py + dy) % 2
    start = 1 + (py + dy) // 2 + part * PART
    at = xm + dx
    if at == -1:
        return moved[row * 2, start : start + PART, :, lanes]
    if at == 4:
        return moved[row * 2 + 1, start : start + PART, :, lanes]
    return plain[class3(row, at), start : start + PART, :, lanes]


def store4(plain, moved, image, value):
    value = value.reshape(2, 16, 8, value.shape[-1])
    for qx in range(2):
        plain[image, qx, 1:17] = value[qx]
    moved[image, 0, 1:17] = shift_down(value[1])
    moved[image, 1, 1:17] = shift_up(value[0])


def tap4(plain, moved, image, qx, dy, dx, part, lanes):
    start = 1 + dy + part * PART
    at = qx + dx
    if at == -1:
        return moved[image, 0, start : start + PART, :, lanes]
    if at == 2:
        return moved[image, 1, start : start + PART, :, lanes]
    return plain[image, at, start : start + PART, :, lanes]


def up(value, unit):
    return -(-value // unit) * unit


def rows4(shards, groups):
    return up(10 * (C4 // shards) + (4 * C3 + F4) // shards, math.lcm(16, groups))


def places3(shards, groups):
    tall = (PATCH + 4 * C3 + F3) // shards // 2
    mats = up(tall, 16)
    slot = up(C3 // shards, 8)
    flat = up(mats + 4 * slot, 16)
    flat_rows = -(-(9 * (F3 + F4) + 2 * C3 + 8 * C4) // (shards * 2 * C3))
    last = flat + up(flat_rows, 8)
    return mats, slot, flat, flat_rows, last, up(last + 8, 8 * groups)


def piece_copy(out, target, sems, piece, at):
    shard, start, end = piece
    rows = pl.ds(start, end - start)
    return pltpu.make_async_copy(out.at[shard, rows], target.at[shard // 2, rows], sems.at[at])


def send_off(out, keep, send, sems, core, pieces, base):
    for at, piece in enumerate(pieces):

        @pl.when(core == piece[0] % 2)
        def _():
            piece_copy(out, keep, sems, piece, base + at).start()

        @pl.when(core != piece[0] % 2)
        def _():
            piece_copy(out, send, sems, piece, base + at).start()


def arrived(out, keep, sems, pieces, base):
    for at, piece in enumerate(pieces):
        piece_copy(out, keep, sems, piece, base + at).wait()


def store_columns4(out, value, column):
    size = C4 // out.shape[0]
    block, lane = column // C4, column % C4
    start = block * size
    lanes = slice(lane, lane + value.shape[1])
    if not isinstance(column, int):
        start = pl.multiple_of(start, size)
        lanes = pl.ds(pl.multiple_of(lane, LC), value.shape[1])
    for at in range(out.shape[0]):
        out[at, pl.ds(start, size), lanes] = value[at * size : at * size + size].astype(BF)


def store_rows(out, value, row, size, offset):
    at = row
    while at < row + value.shape[0]:
        shard = at // size
        end = min((shard + 1) * size, row + value.shape[0])
        start = offset + at - shard * size
        out[shard, start : start + end - at, :] = value[at - row : end - row].astype(BF)
        at = end


def alternate(many, few):
    done = 0
    for at, one in enumerate(many):
        one()
        while done < len(few) and (done + 1) * len(many) <= (at + 1) * len(few):
            few[done]()
            done += 1


TAPS = [(t, t // 3 - 1, t % 3 - 1) for t in range(9)]


def embed_attend(patches, tall3, mat3, norms, z_o, h_o, red_o, q_o, k_o, v_o, p_o, mix_o, x1_o, x0_s, vt_s):
    def embed(b):
        return nn(patches[0, b * 256 : b * 256 + 256, :], tall3[0:PATCH])

    def project(b, h):
        q_o[0, b * 256 : b * 256 + 256, :] = nn(h, mat3[:, 0:C3P]).astype(BF)
        return nn(h, tall3[PATCH + C3 * b : PATCH + C3 * (b + 1)])

    reduced = None
    later = embed(0)
    for b in range(4):
        rows = pl.ds(b * 256, 256)
        z = later
        if b < 3:
            later = embed(b + 1)
        z_o[0, rows, :] = z
        x0 = normalize(z)[0] * norms[0:1] + norms[1:2]
        x0_s[rows, :] = x0
        h = (normalize(x0)[0] * norms[2:3] + norms[3:4]).astype(BF)
        h_o[0, rows, :] = h
        if b > 0:
            part = project(b - 1, before)
            reduced = part if reduced is None else reduced + part
        before = h
    reduced = reduced + project(3, before)
    red_o[0] = reduced
    r = (normalize(reduced)[0] * norms[4:5] + norms[5:6]).astype(BF)
    k = nn(r, mat3[:, C3P : 2 * C3P]).astype(BF)
    v = nn(r, mat3[:, 2 * C3P : 3 * C3P]).astype(BF)
    k_o[0] = k
    v_o[0] = v
    vt_s[...] = v.T

    def queries(b, carry):
        rows = pl.ds(pl.multiple_of(b * 256, 256), 256)
        def raw(head):
            lanes = slice(head // 2 * 128, head // 2 * 128 + 128)
            return nt(half_of(k_o[0, :, lanes], head % 2), q_o[0, rows, lanes])

        def mix(head, soft):
            mix_o[0, head * 64 : head * 64 + 64, rows] = nn(vt_s[head * 64 : head * 64 + 64, :], soft).astype(BF)

        later = raw(0)
        before = None
        for head in range(H3):
            scores = later
            if head + 1 < H3:
                later = raw(head + 1)
            soft = softmax_rows0(scores).astype(BF)
            p_o[0, head, :, rows] = soft
            if head > 0:
                mix(head - 1, before)
            before = soft
        mix(H3 - 1, before)
        x1_o[0, rows, :] = x0_s[rows, :] + tn(mix_o[0, :, rows], mat3[0:C3, 3 * C3P : 3 * C3P + C3])
        return carry

    lax.fori_loop(0, 4, queries, 0)


def feed3(x1, tall3, mat3, depth, norms, n_o, hid_o, slope_o, act_o, x2_o, plain, moved, stage, cur, prev, total):
    @pl.when(pl.program_id(0) == 0)
    def _():
        for ref in (plain, moved):
            ref[:, 0:1] = jnp.zeros((ref.shape[0], 1, 8, LC), F32)
            ref[:, 17:18] = jnp.zeros((ref.shape[0], 1, 8, LC), F32)

    for b in range(4):
        rows = pl.ds(b * 256, 256)
        n_o[0, rows, :] = (normalize(x1[0, rows, :])[0] * norms[6:7] + norms[7:8]).astype(BF)

    chunks = F3 // LC

    def lanes_of(j):
        return pl.ds(pl.multiple_of(j * LC, LC), LC)

    def hidden(j, plane):
        rows = pl.ds(plane * 256, 256)
        stage[rows, :] = nn(n_o[0, rows, :], mat3[:, pl.ds(pl.multiple_of(4 * C3P + j * LC, LC), LC)])

    def spread(j):
        for plane in range(4):
            rows = pl.ds(plane * 256, 256)
            value = stage[rows, :]
            hid_o[0, rows, lanes_of(j)] = value.astype(BF)
            store3(plain, moved, plane, value)

    def second(j, b):
        rows = pl.ds(b * 256, 256)
        return total[rows, :] + nn(prev[rows, :], tall3[pl.ds(pl.multiple_of(PATCH + 4 * C3 + j * LC, LC), LC), :])

    for plane in range(4):
        hidden(0, plane)
    spread(0)
    total[...] = x1[0]
    prev[...] = jnp.zeros_like(prev)

    def chunk(j, carry):
        later = jnp.minimum(j + 1, chunks - 1)
        previous = jnp.maximum(j - 1, 0)
        kernels = [depth[:, pl.ds(pl.multiple_of(j * LC + lt * 128, 128), 128)] for lt in range(LC // 128)]

        def convolve(lt, py, xm, part):
            lanes = pl.ds(lt * 128, 128)
            out_lanes = pl.ds(pl.multiple_of(j * LC + lt * 128, 128), 128)
            out = None
            for t, dy, dx in TAPS:
                term = tap3(plain, moved, py, xm, dy, dx, part, lanes) * kernels[lt][t : t + 1][None]
                out = term if out is None else out + term
            activated, slope = gelu_both(out)
            rows = pl.ds(class3(py, xm) * 128 + part * PART * 8, PART * 8)
            cur[rows, lanes] = activated.reshape(PART * 8, 128).astype(BF)
            slope_o[0, rows, out_lanes] = slope.reshape(PART * 8, 128).astype(BF)

        def accumulate(b):
            total[b * 256 : b * 256 + 256, :] = second(previous, b)

        products = []
        for b in range(4):
            products += [functools.partial(hidden, later, b), functools.partial(accumulate, b)]
        alternate(
            [
                functools.partial(convolve, lt, py, xm, part)
                for lt in range(LC // 128)
                for py in range(2)
                for xm in range(4)
                for part in range(16 // PART)
            ],
            products,
        )
        prev[...] = cur[...]
        act_o[0, :, lanes_of(j)] = cur[...]
        spread(later)
        return carry

    lax.fori_loop(0, chunks, chunk, 0)
    for b in range(4):
        x2_o[0, b * 256 : b * 256 + 256, :] = second(chunks - 1, b).astype(BF)


def section4(
    labels, valid, inv_count, core, x2_h, mat4_h, tall4_h, depth, norms,
    dx2_h, keep, send, gd_o, gn_o, loss_o,
    x2, mat4, tall4, sems, out, first, y1_s, y2_s, h_s, qkv_s, p_s, mix_s, n_s, nt_s, hid_s, slope_s, act_s, plain,
    moved, gd_s, stage, cur, prev,
):
    def load(source, target, at):
        return pltpu.make_async_copy(source, target, sems.at[at])

    loads = [load(tall4_h.at[0 : 4 * C3], tall4.at[0 : 4 * C3], 0)]
    loads += [load(x2_h.at[i], x2.at[i], 1 + i) for i in range(IMGS)]
    loads += [load(mat4_h, mat4, 5), load(tall4_h.at[4 * C3 :], tall4.at[4 * C3 :], 6)]
    for one in loads:
        one.start()
    for ref in (plain, moved):
        for at in (0, 17):
            ref[:, :, at : at + 1] = jnp.zeros((IMGS, 2, 1, 8, LC), F32)

    w1_at = 4 * C4
    wc_at = 4 * C4 + F4
    shards = out.shape[0]
    tall_rows = (4 * C3 + F4) // shards
    tall_at = 10 * (C4 // shards)

    loads[0].wait()
    def downsample(i):
        loads[1 + i].wait()
        prod = None
        for plane in range(4):
            part = nn(x2[i, plane * 256 : plane * 256 + 256, :], tall4[plane * C3 : plane * C3 + C3, :])
            prod = part if prod is None else prod + part
        return prod

    def project(i):
        rows = pl.ds(i * TOK4, TOK4)
        for j in range(3):
            wide = slice(j * C4, j * C4 + C4)
            qkv_s[rows, wide] = nn(h_s[rows, :], mat4[:, wide]).astype(BF)

    later = downsample(0)
    for i in range(IMGS):
        rows = pl.ds(i * TOK4, TOK4)
        prod = later
        if i + 1 < IMGS:
            later = downsample(i + 1)
        first[rows, :] = prod
        y0 = normalize(prod)[0] * norms[0:1] + norms[1:2]
        y1_s[rows, :] = y0
        if i == 1:
            loads[5].wait()
        if i > 0:
            project(i - 1)
        h_s[rows, :] = (normalize(y0)[0] * norms[2:3] + norms[3:4]).astype(BF)
    project(IMGS - 1)

    def attend(i, carry):
        rows = pl.ds(pl.multiple_of(i * TOK4, TOK4), TOK4)
        def raw(head):
            pair = head // 2 * 128
            key = half_of(qkv_s[rows, C4 + pair : C4 + pair + 128], head % 2)
            return nt(key, qkv_s[rows, pair : pair + 128])

        def mix(head, soft):
            at = 2 * C4 + head // 2 * 128
            if head % 2 == 0:
                values.append(qkv_s[rows, at : at + 128].T)
            half = values[-1][head % 2 * 64 : head % 2 * 64 + 64]
            mix_s[head * 64 : head * 64 + 64, rows] = nn(half, soft).astype(BF)

        values = []
        later = raw(0)
        before = None
        for head in range(H4):
            scores = later
            if head + 1 < H4:
                later = raw(head + 1)
            soft = softmax_rows0(scores).astype(BF)
            p_s[i * H4 + head] = soft
            if head > 0:
                mix(head - 1, before)
            before = soft
        mix(H4 - 1, before)
        return carry

    lax.fori_loop(0, IMGS, attend, 0)

    def output(i):
        return tn(mix_s[:, i * TOK4 : i * TOK4 + TOK4], mat4[:, 3 * C4 : 4 * C4])

    later = output(0)
    for i in range(IMGS):
        rows = pl.ds(i * TOK4, TOK4)
        y1 = y1_s[rows, :] + later
        if i + 1 < IMGS:
            later = output(i + 1)
        y1_s[rows, :] = y1
        y2_s[rows, :] = y1
        n_s[rows, :] = (normalize(y1)[0] * norms[4:5] + norms[5:6]).astype(BF)
    loads[6].wait()

    chunks = F4 // LC
    blocks = [(lt, i, qx, p) for lt in range(LC // 128) for i in range(IMGS) for qx in range(2) for p in range(16 // PART)]

    def lanes_of(j):
        return pl.ds(pl.multiple_of(j * LC, LC), LC)

    def second_rows(j):
        return tall4[pl.ds(pl.multiple_of(4 * C3 + j * LC, LC), LC), :]

    def taps_of(j):
        return [depth[:, pl.ds(pl.multiple_of(j * LC + lt * 128, 128), 128)] for lt in range(LC // 128)]

    def image_rows(i):
        return pl.ds(i * TOK4, TOK4)

    def hidden(j, i):
        stage[image_rows(i), :] = nn(n_s[image_rows(i), :], mat4[:, pl.ds(pl.multiple_of(w1_at + j * LC, LC), LC)])

    def spread(j):
        for i in range(IMGS):
            value = stage[image_rows(i), :]
            hid_s[image_rows(i), lanes_of(j)] = value.astype(BF)
            store4(plain, moved, i, value)

    def accumulate(j, i):
        y2_s[image_rows(i), :] += nn(prev[image_rows(i), :], second_rows(j))

    for i in range(IMGS):
        hidden(0, i)
    spread(0)
    prev[...] = jnp.zeros_like(prev)

    def feed(j, carry):
        later, previous = jnp.minimum(j + 1, chunks - 1), jnp.maximum(j - 1, 0)
        kernels = taps_of(j)

        def convolve(lt, i, qx, part):
            lanes = pl.ds(lt * 128, 128)
            total = None
            for t, dy, dx in TAPS:
                term = tap4(plain, moved, i, qx, dy, dx, part, lanes) * kernels[lt][t : t + 1][None]
                total = term if total is None else total + term
            activated, slope = gelu_both(total)
            rows = pl.ds(i * TOK4 + qx * 128 + part * PART * 8, PART * 8)
            cur[rows, lanes] = activated.reshape(PART * 8, 128).astype(BF)
            out_lanes = pl.ds(pl.multiple_of(j * LC + lt * 128, 128), 128)
            slope_s[rows, out_lanes] = slope.reshape(PART * 8, 128).astype(BF)

        products = []
        for i in range(IMGS):
            products += [functools.partial(hidden, later, i), functools.partial(accumulate, previous, i)]
        alternate([functools.partial(convolve, *block) for block in blocks], products)
        prev[...] = cur[...]
        act_s[:, lanes_of(j)] = cur[...]
        spread(later)
        return carry

    lax.fori_loop(0, chunks, feed, 0)

    pools = []
    hat_means = []
    for i in range(IMGS):
        accumulate(chunks - 1, i)
    for i in range(IMGS):
        hat_mean = jnp.mean(normalize(y2_s[image_rows(i), :])[0], axis=0, keepdims=True)
        hat_means.append(hat_mean)
        pools.append(hat_mean * norms[6:7] + norms[7:8])
    pooled = jnp.concatenate(pools + [jnp.zeros((8 - IMGS, C4), F32)], axis=0).astype(BF)
    logits = nn(pooled, mat4[:, wc_at:])

    row = lax.broadcasted_iota(jnp.int32, (8, CLASSES), 0)
    column = lax.broadcasted_iota(jnp.int32, (8, CLASSES), 1)
    target = jnp.full((8, CLASSES), -1, jnp.int32)
    present = jnp.zeros((8, CLASSES), F32)
    for i in range(IMGS):
        target = jnp.where(row == i, labels[i], target)
        present = jnp.where(row == i, valid[i].astype(F32), present)
    goal = (1.0 - SMOOTHING) * (column == target).astype(F32) + SMOOTHING / CLASSES
    shifted = logits - jnp.max(logits, axis=-1, keepdims=True)
    exponent = jnp.exp(shifted)
    mass = jnp.sum(exponent, axis=-1, keepdims=True)
    log_probs = shifted - jnp.log(mass)
    ce = -jnp.sum(goal * log_probs, axis=-1, keepdims=True)
    loss_o[...] = jnp.broadcast_to(jnp.sum(present[:, 0:1] * ce, axis=0, keepdims=True), (8, 128))
    dlogits = (present * inv_count[0] * (exponent / mass - goal)).astype(BF)

    dclass = tn(pooled, dlogits)
    store_columns4(out, dclass[:, :C4], wc_at)
    store_columns4(out, jnp.concatenate([dclass[:, C4:], jnp.zeros((C4, 2 * C4 - CLASSES), F32)], axis=1), wc_at + C4)
    if tall_at + tall_rows < out.shape[1]:
        out[:, tall_at + tall_rows :, :] = jnp.zeros((shards, out.shape[1] - tall_at - tall_rows, C4), BF)
    dpool = nt(dlogits, mat4[:, wc_at:])
    dgain = None
    for i in range(IMGS):
        rows = pl.ds(i * TOK4, TOK4)
        one = dpool[i : i + 1]
        part = one * hat_means[i]
        dgain = part if dgain is None else dgain + part
        xhat, rstd = normalize(y2_s[rows, :])
        dy2 = norm_grad(jnp.broadcast_to(one * (1.0 / TOK4), (TOK4, C4)), xhat, rstd, norms[6:7])
        y2_s[rows, :] = dy2
    gn_o[6:7] = dgain
    gn_o[7:8] = column_sum(dpool)

    for i in range(IMGS):
        nt_s[:, i * TOK4 : i * TOK4 + TOK4] = n_s[image_rows(i), :].T
        n_s[image_rows(i), :] = y2_s[image_rows(i), :].astype(BF)

    def hidden_grad(j, i):
        stage[image_rows(i), :] = nt(n_s[image_rows(i), :], second_rows(j))

    def spread_grad(j):
        for i in range(IMGS):
            store4(plain, moved, i, stage[image_rows(i), :] * slope_s[image_rows(i), lanes_of(j)].astype(F32))

    def first_grad(j):
        store_columns4(out, nn(nt_s[...], hid_s[:, lanes_of(j)]), w1_at + j * LC)

    for i in range(IMGS):
        hidden_grad(0, i)
    spread_grad(0)

    def feed_back(j, carry):
        later, previous = jnp.minimum(j + 1, chunks - 1), jnp.maximum(j - 1, 0)
        kernels = taps_of(j)
        sums = [[None] * 9 for _ in kernels]

        def convolve(lt, i, qx, part):
            lanes = pl.ds(lt * 128, 128)
            out_lanes = pl.ds(pl.multiple_of(j * LC + lt * 128, 128), 128)
            rows = pl.ds(i * TOK4 + qx * 128 + part * PART * 8, PART * 8)
            base = hid_s[rows, out_lanes].astype(F32).reshape(PART, 8, 128)
            acc = None
            for t, dy, dx in TAPS:
                value = tap4(plain, moved, i, qx, -dy, -dx, part, lanes)
                term = value * kernels[lt][t : t + 1][None]
                acc = term if acc is None else acc + term
                tap_sum = jnp.sum(value * base, axis=0)
                sums[lt][t] = tap_sum if sums[lt][t] is None else sums[lt][t] + tap_sum
            cur[rows, lanes] = acc.reshape(PART * 8, 128).astype(BF)

        def second_grad():
            grad = tn(act_s[:, lanes_of(j)], n_s[...]).astype(BF)
            act_s[0:LC, lanes_of(j)] = grad[:, 0:LC]
            act_s[LC : 2 * LC, lanes_of(j)] = grad[:, LC:]

        products = [functools.partial(hidden_grad, later, i) for i in range(IMGS)]
        products = products[:2] + [functools.partial(first_grad, previous)] + products[2:] + [second_grad]
        alternate([functools.partial(convolve, *block) for block in blocks], products)
        for lt in range(LC // 128):
            for t in range(9):
                gd_s[t, :, pl.ds(pl.multiple_of(j * LC + lt * 128, 128), 128)] = sums[lt][t]
        hid_s[:, lanes_of(j)] = cur[...]
        spread_grad(later)
        return carry

    lax.fori_loop(0, chunks, feed_back, 0)
    first_grad(chunks - 1)
    for j in range(chunks):
        wide = slice(j * LC, j * LC + LC)
        grad = jnp.concatenate([act_s[0:LC, wide], act_s[LC : 2 * LC, wide]], axis=1)
        store_rows(out, grad, 4 * C3 + j * LC, tall_rows, tall_at)
    for t in range(9):
        gd_o[t : t + 1, :] = column_sum(gd_s[t])

    mats_done, tall_done = 4 * (C4 // shards), up(4 * C3, tall_rows) // tall_rows
    early = [(at, mats_done, tall_at) for at in range(shards)]
    early += [(at, tall_at, out.shape[1]) for at in range(tall_done, shards)]
    send_off(out, keep, send, sems, core[0], early, 8)

    def normed_grad(i):
        return nt(hid_s[image_rows(i), :], mat4[:, w1_at : w1_at + F4])

    dgain = dshift = None
    later = normed_grad(0)
    for i in range(IMGS):
        rows = image_rows(i)
        dn = later
        if i + 1 < IMGS:
            later = normed_grad(i + 1)
        xhat, rstd = normalize(y1_s[rows, :])
        part_g, part_s = column_sum(dn * xhat), column_sum(dn)
        dgain = part_g if dgain is None else dgain + part_g
        dshift = part_s if dshift is None else dshift + part_s
        y2_s[rows, :] = y2_s[rows, :] + norm_grad(dn, xhat, rstd, norms[4:5])
    gn_o[4:5] = dgain
    gn_o[5:6] = dshift

    dprod = y2_s[...].astype(BF)
    store_columns4(out, nn(mix_s[...], dprod), 3 * C4)
    for i in range(IMGS):
        rows = pl.ds(i * TOK4, TOK4)
        n_s[rows, :] = nt(dprod[i * TOK4 : i * TOK4 + TOK4], mat4[:, 3 * C4 : 4 * C4]).astype(BF)

    d_s = slope_s

    def attend_back(i, carry):
        rows = pl.ds(pl.multiple_of(i * TOK4, TOK4), TOK4)
        lane = lax.broadcasted_iota(jnp.int32, (TOK4, 128), 1)
        dqts, dks, dvs, keys = [], [], [], []

        def at(head):
            return head // 2 * 128

        def first(head):
            start = 2 * C4 + at(head)
            return nt(half_of(qkv_s[rows, start : start + 128], head % 2), n_s[rows, at(head) : at(head) + 128])

        def last(head, ds):
            dks.append(nn(ds, qkv_s[rows, at(head) : at(head) + 128]))
            if head % 2 == 0:
                keys.append(qkv_s[rows, C4 + at(head) : C4 + at(head) + 128].T)
            dqts.append(nn(keys[-1][head % 2 * 64 : head % 2 * 64 + 64], ds))
            if head % 2 == 1:
                start = at(head)
                dqt = (jnp.concatenate(dqts[-2:], axis=0) * SCALE).astype(BF)
                dk = (jnp.where(lane < 64, dks[-2], dks[-1]) * SCALE).astype(BF)
                dv = jnp.where(lane < 64, dvs[head - 1], dvs[head]).astype(BF)
                d_s[rows, start : start + 128] = dqt.T
                d_s[rows, C4 + start : C4 + start + 128] = dk
                d_s[rows, 2 * C4 + start : 2 * C4 + start + 128] = dv

        later = first(0)
        before = None
        for head in range(H4):
            dp = later
            if head + 1 < H4:
                later = first(head + 1)
            soft = p_s[i * H4 + head]
            dvs.append(nn(soft, n_s[rows, at(head) : at(head) + 128]))
            ds = softmax_grad(soft.astype(F32), dp).astype(BF)
            if head > 0:
                last(head - 1, before)
            before = ds
        last(H4 - 1, before)
        return carry

    lax.fori_loop(0, IMGS, attend_back, 0)
    ht = h_s[...].T
    for j in range(3):
        wide = slice(j * C4, j * C4 + C4)
        store_columns4(out, nn(ht, d_s[:, wide]), j * C4)

    def normed_grad0(i):
        return nt(d_s[image_rows(i), 0 : 3 * C4], mat4[:, 0 : 3 * C4])

    sums = [None] * 4
    later = normed_grad0(0)
    for i in range(IMGS):
        rows = image_rows(i)
        dh = later
        if i + 1 < IMGS:
            later = normed_grad0(i + 1)
        hat0, rstd0 = normalize(first[rows, :])
        hat1, rstd1 = normalize(hat0 * norms[0:1] + norms[1:2])
        dy0 = y2_s[rows, :] + norm_grad(dh, hat1, rstd1, norms[2:3])
        n_s[rows, :] = norm_grad(dy0, hat0, rstd0, norms[0:1]).astype(BF)
        parts = [column_sum(dy0 * hat0), column_sum(dy0), column_sum(dh * hat1), column_sum(dh)]
        sums = [part if old is None else old + part for old, part in zip(sums, parts)]
    gn_o[0:4] = jnp.concatenate(sums, axis=0)
    for plane in range(4):
        total = None
        for i in range(IMGS):
            part = tn(x2[i, plane * 256 : plane * 256 + 256, :], n_s[image_rows(i), :])
            total = part if total is None else total + part
        store_rows(out, total, plane * C3, tall_rows, tall_at)
    late = [(at, 0, mats_done) for at in range(shards)] + [(at, tall_at, out.shape[1]) for at in range(tall_done)]
    send_off(out, keep, send, sems, core[0], late, 8 + len(early))
    stores = [load(x2.at[i], dx2_h.at[i], 1 + i) for i in range(IMGS)]
    for i in range(IMGS):
        for plane in range(4):
            grad = nt(n_s[image_rows(i), :], tall4[plane * C3 : plane * C3 + C3, :])
            x2[i, plane * 256 : plane * 256 + 256, :] = grad.astype(BF)
        stores[i].start()
    for one in stores:
        one.wait()
    arrived(out, keep, sems, early, 8)
    arrived(out, keep, sems, late, 8 + len(early))


def feed3_back(dx2, x1, n, hid, slope, act, tall3, mat3, depth, norms, dx1_o, g1_o, g2_o, gd_o, gn_o,
               acc1, acc2, accd, accn, plain, moved, dy_s, dyt_s, nt_s, da_s, stage, cur):
    step = pl.program_id(0)

    @pl.when(step == 0)
    def _():
        for ref in (plain, moved):
            ref[:, 0:1] = jnp.zeros((ref.shape[0], 1, 8, LC), F32)
            ref[:, 17:18] = jnp.zeros((ref.shape[0], 1, 8, LC), F32)
        for ref in (acc1, acc2, accd, accn):
            ref[...] = jnp.zeros_like(ref)

    dy = dx2[0]
    dy_s[...] = dy
    dyt_s[...] = dy.T
    nt_s[...] = n[0].T

    chunks = F3 // LC

    def lanes_of(j):
        return pl.ds(pl.multiple_of(j * LC, LC), LC)

    def hidden_grad(j, plane):
        rows = pl.ds(plane * 256, 256)
        w2 = tall3[pl.ds(pl.multiple_of(PATCH + 4 * C3 + j * LC, LC), LC), :]
        stage[rows, :] = nt(dy_s[rows, :], w2)

    def spread(j):
        for plane in range(4):
            rows = pl.ds(plane * 256, 256)
            store3(plain, moved, plane, stage[rows, :] * slope[0, rows, lanes_of(j)].astype(F32))

    def first_grad(j):
        acc1[:, lanes_of(j)] += nn(nt_s[...], da_s[:, lanes_of(j)])

    for plane in range(4):
        hidden_grad(0, plane)
    spread(0)

    def chunk(j, carry):
        later = jnp.minimum(j + 1, chunks - 1)
        previous = jnp.where(j > 0, j - 1, chunks)
        kernels, sums = [], []
        for lt in range(LC // 128):
            kernels.append(depth[:, pl.ds(pl.multiple_of(j * LC + lt * 128, 128), 128)])
            sums.append([None] * 9)

        def convolve(lt, py, xm, part):
            lanes = pl.ds(lt * 128, 128)
            out_lanes = pl.ds(pl.multiple_of(j * LC + lt * 128, 128), 128)
            rows = pl.ds(class3(py, xm) * 128 + part * PART * 8, PART * 8)
            base = hid[0, rows, out_lanes].astype(F32).reshape(PART, 8, 128)
            out = None
            for t, dy, dx in TAPS:
                value = tap3(plain, moved, py, xm, -dy, -dx, part, lanes)
                term = value * kernels[lt][t : t + 1][None]
                out = term if out is None else out + term
                tap_sum = jnp.sum(value * base, axis=0)
                sums[lt][t] = tap_sum if sums[lt][t] is None else sums[lt][t] + tap_sum
            cur[rows, lanes] = out.reshape(PART * 8, 128).astype(BF)

        def second_grad():
            acc2[:, lanes_of(j)] += nn(dyt_s[...], act[0, :, lanes_of(j)])

        products = [functools.partial(hidden_grad, later, plane) for plane in range(4)]
        products = products[:2] + [functools.partial(first_grad, previous)] + products[2:] + [second_grad]
        alternate(
            [
                functools.partial(convolve, lt, py, xm, part)
                for lt in range(LC // 128)
                for py in range(2)
                for xm in range(4)
                for part in range(16 // PART)
            ],
            products,
        )
        for lt in range(LC // 128):
            for t in range(9):
                accd[t, :, pl.ds(pl.multiple_of(j * LC + lt * 128, 128), 128)] += sums[lt][t]
        da_s[:, lanes_of(j)] = cur[...]
        spread(later)
        return carry

    lax.fori_loop(0, chunks, chunk, 0)
    first_grad(chunks - 1)

    def normed_grad(b):
        return nt(da_s[b * 256 : b * 256 + 256, 0:F3], mat3[:, 4 * C3P :])

    later = normed_grad(0)
    for b in range(4):
        rows = pl.ds(b * 256, 256)
        dn = later
        if b < 3:
            later = normed_grad(b + 1)
        xhat, rstd = normalize(x1[0, rows, :])
        accn[0:1] += column_sum(dn * xhat)
        accn[1:2] += column_sum(dn)
        dx1_o[0, rows, :] = dx2[0, rows, :].astype(F32) + norm_grad(dn, xhat, rstd, norms[6:7])

    @pl.when(step == IMGS - 1)
    def _():
        g1_o[...] = acc1[:, 0:F3]
        g2_o[...] = acc2[...].T.astype(g2_o.dtype)
        gn_o[...] = accn[...]
        for t in range(9):
            gd_o[t : t + 1, :] = column_sum(accd[t])


def attend3_back(groups, core, dx1, z, h, red, q, k, v, p, mix, patches, tall3, mat3, norms, g1, g2, flat, keep, send, out, sems,
                 tall_s, acce, accr, accq, acck, accv, acco, accn, dk_s, dv_s, kt_s, dqt_s, dr_s):
    step = pl.program_id(0)

    @pl.when(step == 0)
    def _():
        for ref in (acce, accr, accq, acck, accv, acco, accn):
            ref[...] = jnp.zeros_like(ref)

    kt_s[...] = k[0].T
    dk_s[...] = jnp.zeros_like(dk_s)
    dv_s[...] = jnp.zeros_like(dv_s)
    wo = mat3[0:C3, 3 * C3P : 3 * C3P + C3]
    lane = lax.broadcasted_iota(jnp.int32, (256, 128), 1)

    def queries(b, carry):
        rows = pl.ds(pl.multiple_of(b * 256, 256), 256)
        dprod = dx1[0, rows, :].astype(BF)
        acco[...] += nn(mix[0, :, rows], dprod)
        dmix = nt(dprod, wo).astype(BF)
        dmix = jnp.concatenate([dmix, jnp.zeros((256, C3P - C3), BF)], axis=1)
        lanes = [slice(pair * 128, pair * 128 + 128) for pair in range(3)]
        dks, dvs = [], []

        def first(head):
            return nt(half_of(v[0, :, lanes[head // 2]], head % 2), dmix[:, lanes[head // 2]])

        def last(head, ds):
            dks.append(nn(ds, q[0, rows, lanes[head // 2]]))
            dqt = nn(kt_s[head * 64 : head * 64 + 64, :], ds) * SCALE
            dqt_s[head * 64 : head * 64 + 64, rows] = dqt.astype(BF)

        later = first(0)
        before = None
        for head in range(H3):
            dp = later
            if head + 1 < H3:
                later = first(head + 1)
            soft = p[0, head, :, rows]
            dvs.append(nn(soft, dmix[:, lanes[head // 2]]))
            ds = softmax_grad(soft.astype(F32), dp).astype(BF)
            if head > 0:
                last(head - 1, before)
            before = ds
        last(H3 - 1, before)
        for pair in range(2):
            dk_s[:, lanes[pair]] += jnp.where(lane < 64, dks[2 * pair], dks[2 * pair + 1])
            dv_s[:, lanes[pair]] += jnp.where(lane < 64, dvs[2 * pair], dvs[2 * pair + 1])
        dk_s[:, lanes[2]] += dks[4]
        dv_s[:, lanes[2]] += dvs[4]
        return carry

    lax.fori_loop(0, 4, queries, 0)

    dk = (dk_s[...] * SCALE).astype(BF)
    dv = dv_s[...].astype(BF)
    hat_r, rstd_r = normalize(red[0])
    r = (hat_r * norms[4:5] + norms[5:6]).astype(BF)
    acck[...] += tn(r, dk)
    accv[...] += tn(r, dv)
    dr = nt(dk, mat3[:, C3P : 2 * C3P]) + nt(dv, mat3[:, 2 * C3P : 3 * C3P])
    accn[4:5] += column_sum(dr * hat_r)
    accn[5:6] += column_sum(dr)
    dred = norm_grad(dr, hat_r, rstd_r, norms[4:5]).astype(BF)
    accq[...] += nn(dqt_s[...], h[0])

    def input_grad(b):
        rows = slice(b * 256, b * 256 + 256)
        wr = tall3[PATCH + C3 * b : PATCH + C3 * (b + 1)]
        return contract(dqt_s[:, rows], mat3[:, 0:C3], 0, 1) + nt(dred, wr)

    def weight_grads(b, dz):
        rows = slice(b * 256, b * 256 + 256)
        accr[C3 * b : C3 * (b + 1)] += tn(h[0, rows, :], dred)
        acce[...] += tn(dz, patches[0, rows, :])

    later = input_grad(0)
    before = None
    for b in range(4):
        rows = pl.ds(b * 256, 256)
        dh = later
        if b < 3:
            later = input_grad(b + 1)
        hat0, rstd0 = normalize(z[0, rows, :])
        hat1, rstd1 = normalize(hat0 * norms[0:1] + norms[1:2])
        accn[2:3] += column_sum(dh * hat1)
        accn[3:4] += column_sum(dh)
        dx0 = dx1[0, rows, :] + norm_grad(dh, hat1, rstd1, norms[2:3])
        accn[0:1] += column_sum(dx0 * hat0)
        accn[1:2] += column_sum(dx0)
        dz = norm_grad(dx0, hat0, rstd0, norms[0:1]).astype(BF)
        if b > 0:
            weight_grads(b - 1, before)
        before = dz
    weight_grads(3, before)

    @pl.when(step == IMGS - 1)
    def _():
        shards = out.shape[0]
        mats, slot, flat_at, flat_rows, last, total_rows = places3(shards, groups)
        mat_rows = C3 // shards
        tall = (PATCH + 4 * C3 + F3) // shards // 2
        out[:, mats:, :] = jnp.zeros((shards, total_rows - mats, 2 * C3), BF)
        if tall < mats:
            out[:, tall:mats, :] = jnp.zeros((shards, mats - tall, 2 * C3), BF)
        tall_s[0:PATCH] = acce[...].T
        tall_s[PATCH : PATCH + 4 * C3] = accr[...]
        tall_s[PATCH + 4 * C3 :] = g2[...].astype(F32)
        accq[...] = accq[...].T
        for at in range(shards):
            rows = slice(at * mat_rows, at * mat_rows + mat_rows)
            pieces = [accq[rows, :], acck[rows, 0:C3], accv[rows, 0:C3], acco[rows, :]]
            start = at * 2 * tall
            pairs = [tall_s[start : start + tall], tall_s[start + tall : start + 2 * tall]]
            out[at, 0:tall, :] = jnp.concatenate(pairs, axis=1).astype(BF)
            for b in range(2):
                pair = jnp.concatenate(pieces[2 * b : 2 * b + 2], axis=1)
                out[at, mats + b * slot : mats + b * slot + mat_rows, :] = pair.astype(BF)
                feed = g1[rows, b * 2 * C3 : b * 2 * C3 + 2 * C3]
                out[at, mats + (b + 2) * slot : mats + (b + 2) * slot + mat_rows, :] = feed.astype(BF)
            out[at, flat_at : flat_at + flat_rows, :] = flat[at]
            out[at, last : last + 6, 0:mat_rows] = accn[:, rows].astype(BF)
        pieces = [(at, 0, total_rows) for at in range(shards)]
        send_off(out, keep, send, sems, core[0], pieces, 0)
        arrived(out, keep, sems, pieces, 0)


def whole(shape, dtype=None):
    return pl.BlockSpec(shape, lambda i: (0,) * len(shape), pipeline_mode=pl.Buffered(1))


def per_image(*shape):
    return pl.BlockSpec((1,) + shape, lambda i: (i,) + (0,) * len(shape))


def sds(*shape, dtype=F32):
    return jax.ShapeDtypeStruct(shape, dtype)


def work(microseconds):
    return pl.CostEstimate(flops=microseconds * 10**9, bytes_accessed=microseconds * 3 * 10**6, transcendentals=0)


PARAMS = pltpu.CompilerParams(vmem_limit_bytes=VMEM_BYTES, dimension_semantics=("arbitrary",))


def unpack3(pack, tall3, mat3):
    half = tall3.shape[0] // pack.shape[0] // 2
    size = C3 // pack.shape[0]
    for at in range(pack.shape[0]):
        start = at * 2 * half
        tall3[start : start + half, :] = pack[at, 0:half, 0:C3]
        tall3[start + half : start + 2 * half, :] = pack[at, 0:half, C3:]
        rows = slice(at * size, at * size + size)
        for b in range(2):
            piece = pack[at, half + b * size : half + (b + 1) * size, :]
            blank = jnp.zeros((size, C3P - C3), BF)
            wide = jnp.concatenate([piece[:, :C3], blank, piece[:, C3:], blank], axis=1)
            mat3[rows, b * 2 * C3P : (b + 1) * 2 * C3P] = wide
            feed = pack[at, half + (b + 2) * size : half + (b + 3) * size, :]
            mat3[rows, 4 * C3P + b * 2 * C3 : 4 * C3P + (b + 1) * 2 * C3] = feed


def forward3(packed, *refs):
    if packed:
        pack, patches, depth, norms, tall3, mat3 = refs[:6]

        @pl.when(pl.program_id(0) == 0)
        def _():
            unpack3(pack, tall3, mat3)

    else:
        tall3, mat3, patches, depth, norms = refs[:5]
    refs = refs[6 if packed else 5 :]
    x1 = refs[8]
    embed_attend(patches, tall3, mat3, norms, *refs[:9], *refs[14:16])
    feed3(x1, tall3, mat3, depth, norms, *refs[9:14], *refs[16:])


def run_forward3(weights, patches, depth, norms3):
    packed = len(weights) == 1
    tall_shape, mat_shape = (PATCH + 4 * C3 + F3, C3), (C3, 4 * C3P + F3)
    full = [whole(tall_shape), whole(mat_shape)] if packed else []
    full_shapes = [sds(*tall_shape, dtype=BF), sds(*mat_shape, dtype=BF)] if packed else []
    weight_specs = [whole(weight.shape) for weight in weights]
    image_specs = [per_image(TOK3, PATCH), whole(depth.shape), whole(norms3.shape)]
    outs = pl.pallas_call(
        functools.partial(forward3, packed),
        grid=(IMGS,),
        in_specs=weight_specs + image_specs,
        out_specs=full + [
            per_image(TOK3, C3), per_image(TOK3, C3), per_image(256, C3), per_image(TOK3, C3P), per_image(256, C3P),
            per_image(256, C3P), per_image(H3, 256, TOK3), per_image(C3, TOK3), per_image(TOK3, C3),
            per_image(TOK3, C3), per_image(TOK3, F3), per_image(TOK3, F3), per_image(TOK3, F3), per_image(TOK3, C3),
        ],
        out_shape=full_shapes + [
            sds(IMGS, TOK3, C3), sds(IMGS, TOK3, C3, dtype=BF), sds(IMGS, 256, C3), sds(IMGS, TOK3, C3P, dtype=BF),
            sds(IMGS, 256, C3P, dtype=BF), sds(IMGS, 256, C3P, dtype=BF), sds(IMGS, H3, 256, TOK3, dtype=BF),
            sds(IMGS, C3, TOK3, dtype=BF), sds(IMGS, TOK3, C3),
            sds(IMGS, TOK3, C3, dtype=BF), sds(IMGS, TOK3, F3, dtype=BF), sds(IMGS, TOK3, F3, dtype=BF),
            sds(IMGS, TOK3, F3, dtype=BF), sds(IMGS, TOK3, C3, dtype=BF),
        ],
        scratch_shapes=[
            pltpu.VMEM((TOK3, C3), F32), pltpu.VMEM((C3P, 256), BF),
            pltpu.VMEM((8, 18, 8, LC), F32), pltpu.VMEM((4, 18, 8, LC), F32), pltpu.VMEM((TOK3, LC), F32),
            pltpu.VMEM((TOK3, LC), BF), pltpu.VMEM((TOK3, LC), BF), pltpu.VMEM((TOK3, C3), F32),
        ],
        compiler_params=PARAMS,
        name="forward3",
        cost_estimate=work(85),
    )(*weights, patches, depth, norms3)
    return outs if packed else [*weights, *outs]


def run_section4(labels, valid, inv_count, core, x2, mat4, tall4, depth, norms4, shards, groups):
    vm = pl.BlockSpec(memory_space=pltpu.VMEM)
    sm = pl.BlockSpec(memory_space=pltpu.SMEM)
    hbm = pl.BlockSpec(memory_space=pl.ANY)
    rows = IMGS * TOK4
    half = sds(shards // 2, rows4(shards, groups), C4, dtype=BF)
    return pl.pallas_call(
        section4,
        in_specs=[sm, sm, sm, sm, hbm, hbm, hbm, vm, vm],
        out_specs=[hbm, hbm, hbm, vm, vm, vm],
        out_shape=[
            sds(IMGS, TOK3, C3, dtype=BF), half, half, sds(9, F4), sds(8, C4),
            sds(8, 128),
        ],
        scratch_shapes=[
            pltpu.VMEM(x2.shape, BF), pltpu.VMEM(mat4.shape, BF), pltpu.VMEM(tall4.shape, BF),
            pltpu.SemaphoreType.DMA((8 + 3 * shards,)), pltpu.VMEM((shards,) + half.shape[1:], BF),
            pltpu.VMEM((rows, C4), F32), pltpu.VMEM((rows, C4), F32), pltpu.VMEM((rows, C4), F32),
            pltpu.VMEM((rows, C4), BF), pltpu.VMEM((rows, 3 * C4), BF), pltpu.VMEM((IMGS * H4, 256, 256), BF),
            pltpu.VMEM((C4, rows), BF), pltpu.VMEM((rows, C4), BF), pltpu.VMEM((C4, rows), BF), pltpu.VMEM((rows, F4), BF),
            pltpu.VMEM((rows, F4), BF), pltpu.VMEM((rows, F4), BF), pltpu.VMEM((IMGS, 2, 18, 8, LC), F32),
            pltpu.VMEM((IMGS, 2, 18, 8, LC), F32), pltpu.VMEM((9, 8, F4), F32),
            pltpu.VMEM((rows, LC), F32), pltpu.VMEM((rows, LC), BF), pltpu.VMEM((rows, LC), BF),
        ],
        compiler_params=pltpu.CompilerParams(vmem_limit_bytes=VMEM_BYTES),
        name="section4",
        cost_estimate=work(90),
    )(labels, valid, inv_count, core, x2, mat4, tall4, depth, norms4)


def run_feed3_back(dx2, x1, n, hid, slope, act, tall3, mat3, depth, norms3):
    return pl.pallas_call(
        feed3_back,
        grid=(IMGS,),
        in_specs=[
            per_image(TOK3, C3), per_image(TOK3, C3), per_image(TOK3, C3), per_image(TOK3, F3), per_image(TOK3, F3),
            per_image(TOK3, F3), whole(tall3.shape), whole(mat3.shape), whole(depth.shape), whole(norms3.shape),
        ],
        out_specs=[per_image(TOK3, C3), whole((C3, F3)), whole((F3, C3)), whole((9, F3)), whole((2, C3))],
        out_shape=[sds(IMGS, TOK3, C3), sds(C3, F3), sds(F3, C3, dtype=BF), sds(9, F3), sds(2, C3)],
        scratch_shapes=[
            pltpu.VMEM((C3, F3 + LC), F32), pltpu.VMEM((C3, F3), F32), pltpu.VMEM((9, 8, F3), F32), pltpu.VMEM((2, C3), F32),
            pltpu.VMEM((8, 18, 8, LC), F32), pltpu.VMEM((4, 18, 8, LC), F32), pltpu.VMEM((TOK3, C3), BF),
            pltpu.VMEM((C3, TOK3), BF), pltpu.VMEM((C3, TOK3), BF), pltpu.VMEM((TOK3, F3 + LC), BF),
            pltpu.VMEM((TOK3, LC), F32), pltpu.VMEM((TOK3, LC), BF),
        ],
        compiler_params=PARAMS,
        name="feed3_back",
        cost_estimate=work(68),
    )(dx2, x1, n, hid, slope, act, tall3, mat3, depth, norms3)


def run_attend3_back(core, dx1, z, h, red, q, k, v, p, mix, patches, tall3, mat3, norms3, g1, g2, flat, groups):
    shards = flat.shape[0]
    total_rows = places3(shards, groups)[-1]
    return pl.pallas_call(
        functools.partial(attend3_back, groups),
        grid=(IMGS,),
        in_specs=[
            pl.BlockSpec(memory_space=pltpu.SMEM),
            per_image(TOK3, C3), per_image(TOK3, C3), per_image(TOK3, C3), per_image(256, C3), per_image(TOK3, C3P),
            per_image(256, C3P), per_image(256, C3P), per_image(H3, 256, TOK3), per_image(C3, TOK3),
            per_image(TOK3, PATCH), whole(tall3.shape), whole(mat3.shape), whole(norms3.shape),
            whole(g1.shape), whole(g2.shape), whole(flat.shape),
        ],
        out_specs=[pl.BlockSpec(memory_space=pl.ANY)] * 2,
        out_shape=[sds(shards // 2, total_rows, 2 * C3, dtype=BF)] * 2,
        scratch_shapes=[
            pltpu.VMEM((shards, total_rows, 2 * C3), BF), pltpu.SemaphoreType.DMA((shards,)),
            pltpu.VMEM((PATCH + 4 * C3 + F3, C3), F32),
            pltpu.VMEM((C3, PATCH), F32), pltpu.VMEM((4 * C3, C3), F32), pltpu.VMEM((C3, C3), F32),
            pltpu.VMEM((C3, C3P), F32), pltpu.VMEM((C3, C3P), F32), pltpu.VMEM((C3, C3), F32), pltpu.VMEM((6, C3), F32),
            pltpu.VMEM((256, C3P), F32), pltpu.VMEM((256, C3P), F32), pltpu.VMEM((C3P, 256), BF),
            pltpu.VMEM((C3, TOK3), BF), pltpu.VMEM((256, C3), F32),
        ],
        compiler_params=PARAMS,
        name="attend3_back",
        cost_estimate=work(65),
    )(core, dx1, z, h, red, q, k, v, p, mix, patches, tall3, mat3, norms3, g1, g2, flat)


def pad_mat3(mat):
    pieces = [mat[:, at * C3 : at * C3 + C3] for at in range(4)]
    pieces = [jnp.pad(piece, ((0, 0), (0, C3P - C3))) for piece in pieces]
    return jnp.concatenate(pieces + [mat[:, 4 * C3 :]], axis=1)


def reorder(patches):
    count = patches.shape[0]
    grid = patches.reshape(count, 16, 2, 8, 2, 2, patches.shape[-1])
    return grid.transpose(0, 2, 5, 4, 1, 3, 6).reshape(patches.shape)


def swap(value, axis, mask):
    return lax.ppermute(value, axis, [(at, at ^ mask) for at in range(lax.axis_size(axis))])


def pick(value, index, axis=0):
    return lax.dynamic_index_in_dim(value, index, axis, keepdims=False)


def add_all(own, parts):
    total = own.astype(F32)
    for part in parts:
        total = total + part.astype(F32)
    return total


def chip_sends(keep, got):
    chip = lax.axis_index("fsdp") // 2
    sums = [add_all(pick(keep, chip ^ mask), [pick(got, chip ^ mask)]) for mask in range(keep.shape[0])]
    return sums[0], [one.astype(BF) for one in sums[1:]]


def depth_sends(shard):
    count, me = lax.axis_size("dp"), lax.axis_index("dp")
    cut = shard.reshape(count, shard.shape[0] // count, shard.shape[1])
    return pick(cut, me), [pick(cut, me ^ mask).astype(BF) for mask in range(1, count)]


def exchange(sends, axis, unit):
    return [swap(send, axis, unit * (at + 1)) for at, send in enumerate(sends)]


def depth_gather(piece):
    count, me = lax.axis_size("dp"), lax.axis_index("dp")
    narrow = piece.astype(BF)
    parts = [narrow] + [swap(narrow, "dp", mask) for mask in range(1, count)]
    placed = [lax.select_n(me, *[parts[at ^ other] for other in range(count)]) for at in range(count)]
    return jnp.concatenate(placed, axis=0).astype(F32)


def total_over_all(row):
    count = lax.axis_size("dp") * lax.axis_size("fsdp")
    rows = jnp.broadcast_to(row, (count, row.shape[1]))
    return jnp.sum(lax.all_to_all(rows, ("dp", "fsdp"), 0, 0, tiled=True), axis=0, keepdims=True)


def adamw(master, moment, second, gradient, is_norm):
    step_rate = 0.5 if is_norm else 0.05
    decay_now = 0.0 if is_norm else 0.05
    first = 0.9 * moment + 0.1 * gradient
    second_new = 0.999 * second + 0.001 * gradient * gradient
    first_hat = first / (1.0 - 0.9**STEP)
    second_hat = second_new / (1.0 - 0.999**STEP)
    updated = master - step_rate * (first_hat / (jnp.sqrt(second_hat) + 1e-08) + decay_now * master)
    return (updated, first, second_new)


def body(patches, labels, valid, *state):
    masters, moments, seconds = state[0:7], state[7:14], state[14:21]
    shards, groups = lax.axis_size("fsdp"), lax.axis_size("dp")
    mat3, tall3, mat4, tall4, depth, norms3, norms4 = [master.astype(BF) for master in masters]
    half, m_rows = tall3.shape[0] // 2, mat3.shape[0]
    pack = [jnp.concatenate([tall3[:half], tall3[half:]], axis=1)]
    pack += [mat3[:, at * 2 * C3 : at * 2 * C3 + 2 * C3] for at in range(4)]
    pack = lax.all_gather(jnp.concatenate(pack, axis=0), "fsdp", axis=0)

    small = [jnp.pad(piece.T, ((0, 0), (0, 16 - piece.shape[0]))) for piece in (depth, norms3, norms4)]
    small.append(jnp.full((8, 16), jnp.sum(valid)).astype(BF))
    sizes = [piece.shape[0] for piece in small]
    small = lax.all_gather(jnp.concatenate(small, axis=0), "fsdp", axis=0)
    edges = [0, sizes[0], sizes[0] + sizes[1], sum(sizes[:3])]
    parts = [small[:, edges[at] : edges[at + 1]].reshape(-1, 16).T.astype(F32) for at in range(3)]
    depth_all, norms3_all, norms4_all = parts[0][:9], parts[1][:8], parts[2][:8]
    present = jnp.full((8, 128), jnp.sum(small[:, edges[3], 0].astype(F32)))
    others = exchange([present] * (groups - 1), "dp", 1)

    weights3 = [pack]
    if half % 8 or m_rows % 8:
        tall3_all = jnp.concatenate([pack[:, :half, :C3], pack[:, :half, C3:]], axis=1).reshape(-1, C3)
        mats = pack[:, half:].reshape(shards, 4, m_rows, 2 * C3).transpose(1, 0, 2, 3).reshape(4, C3, 2 * C3)
        mat3_all = [mats[at // 2, :, at % 2 * C3 : at % 2 * C3 + C3] for at in range(4)]
        mat3_all = [jnp.pad(piece, ((0, 0), (0, C3P - C3))) for piece in mat3_all]
        weights3 = [tall3_all, jnp.concatenate(mat3_all + [mats[2], mats[3]], axis=1)]
    tall4_all = lax.all_gather(tall4, "fsdp", axis=0, tiled=True)
    mat4_all = lax.all_gather(mat4, "fsdp", axis=0, tiled=True)

    patches = reorder(patches.reshape(IMGS, TOK3, PATCH))
    depth3, depth4 = depth_all[:, :F3], depth_all[:, F3:]
    tall3_all, mat3_all, z, h, red, q, k, v, p, mix, x1, n, hid, slope, act, x2 = run_forward3(
        weights3, patches, depth3, norms3_all
    )
    x2, others = lax.optimization_barrier((x2, others))
    image_count = add_all(present, others)[0, 0]
    inv_count = (1.0 / image_count).reshape(1)
    core = (lax.axis_index("fsdp") % 2).reshape(1)
    dx2, keep4, send4, gd4, gn4, loss = run_section4(
        labels.reshape(IMGS), valid.reshape(IMGS), inv_count, core, x2, mat4_all, tall4_all, depth4, norms4_all,
        shards, groups,
    )

    own4, sends4 = chip_sends(keep4, swap(send4, "fsdp", 1))
    dx2, own4, sends4 = lax.optimization_barrier((dx2, own4, sends4))
    got4 = exchange(sends4, "fsdp", 2)
    dx1, g1, g2, gd3, gn3b = run_feed3_back(dx2, x1, n, hid, slope, act, tall3_all, mat3_all, depth3, norms3_all)
    dx1, own4, got4 = lax.optimization_barrier((dx1, own4, got4))
    own4, sends4 = depth_sends(add_all(own4, got4))

    def by_columns(grad):
        return grad.reshape(grad.shape[0], shards, -1).transpose(1, 0, 2).reshape(shards, -1)

    _, slot, flat_at, flat_rows, last, _ = places3(shards, groups)
    flat = jnp.concatenate([by_columns(grad) for grad in (jnp.concatenate([gd3, gd4], axis=1), gn3b, gn4)], axis=1)
    flat = jnp.pad(flat, ((0, 0), (0, flat_rows * 2 * C3 - flat.shape[1])))
    flat = flat.reshape(shards, flat_rows, 2 * C3).astype(BF)
    dx1, own4, sends4, flat = lax.optimization_barrier((dx1, own4, sends4, flat))
    got4 = exchange(sends4, "dp", 1)
    keep3, send3 = run_attend3_back(
        core, dx1, z, h, red, q, k, v, p, mix, patches, tall3_all, mat3_all, norms3_all, g1, g2, flat, groups
    )
    keep3, send3, got4 = lax.optimization_barrier((keep3, send3, got4))
    piece4 = add_all(own4, got4)
    own3, sends3 = chip_sends(keep3, swap(send3, "fsdp", 1))
    own3, sends3, piece4 = lax.optimization_barrier((own3, sends3, piece4))
    got3 = exchange(sends3, "fsdp", 2)
    grads4 = depth_gather(piece4)
    own3, got3, grads4 = lax.optimization_barrier((own3, got3, grads4))
    own3, sends3 = depth_sends(add_all(own3, got3))
    piece3 = add_all(own3, exchange(sends3, "dp", 1))
    square = jnp.sum(piece4 * piece4) + jnp.sum(piece3 * piece3)
    lane = lax.broadcasted_iota(jnp.int32, (1, 128), 1)
    totals = total_over_all(jnp.where(lane == 0, square, loss[0:1]))
    grads3 = depth_gather(piece3)

    m_rows, t_rows = C4 // shards, masters[3].shape[0]
    blocks4 = [grads4[at * m_rows : at * m_rows + m_rows] for at in range(10)]
    grad_mat4 = jnp.concatenate(blocks4, axis=1)[:, : masters[2].shape[1]]
    grad_tall4 = grads4[10 * m_rows : 10 * m_rows + t_rows]
    t_rows, m_rows = masters[1].shape[0], masters[0].shape[0]
    mats_at, half = up(t_rows // 2, 16), t_rows // 2
    grad_tall3 = jnp.concatenate([grads3[:half, :C3], grads3[:half, C3:]], axis=0)
    grad_mat3 = jnp.concatenate([grads3[mats_at + at * slot : mats_at + at * slot + m_rows] for at in range(4)], axis=1)
    flat = grads3[flat_at : flat_at + flat_rows].reshape(-1)
    sizes = [9 * t_rows, 2 * m_rows, masters[6].size]
    grad_depth = flat[: sizes[0]].reshape(9, t_rows)
    grad_norms3 = jnp.concatenate(
        [grads3[last : last + 6, :m_rows], flat[sizes[0] : sizes[0] + sizes[1]].reshape(2, m_rows)], axis=0
    )
    grad_norms4 = flat[sizes[0] + sizes[1] : sum(sizes)].reshape(masters[6].shape)
    group = [grad_mat3, grad_tall3, grad_mat4, grad_tall4, grad_depth, grad_norms3, grad_norms4]

    grad_norm = jnp.sqrt(totals[0, 0])
    clip_factor = jnp.minimum(1.0, CLIP_LEVEL / (grad_norm + 1e-06))
    results = [adamw(masters[at], moments[at], seconds[at], clip_factor * group[at], at >= 5) for at in range(7)]
    return (
        *[result[0] for result in results],
        *[result[1] for result in results],
        *[result[2] for result in results],
        totals[0, 1],
        image_count,
        grad_norm,
    )


def solution(mesh):
    rows, columns = P("fsdp", None), P(None, "fsdp")
    weights = (rows,) * 4 + (columns,) * 3
    images = P(None, ("dp", "fsdp"))
    in_specs = (P(None, ("dp", "fsdp"), None, None), images, images) + weights * 3
    out_specs = weights * 3 + (P(), P(), P())
    return jax.shard_map(body, mesh=mesh, in_specs=in_specs, out_specs=out_specs, check_vma=False)
```

```python
import functools
import math

import jax
import jax.numpy as jnp
from jax import lax
from jax.experimental import pallas as pl
from jax.experimental.pallas import tpu as pltpu
from jax.sharding import PartitionSpec as P

BF = jnp.bfloat16
F32 = jnp.float32
C3 = 320
C3P = 384
H3 = 5
F3 = 1280
C4 = 512
H4 = 8
F4 = 2048
CLASSES = 1000
PATCH = 768
STEP = 10
IMGS = 4
TOK3 = 1024
TOK4 = 256
LC = 256
PART = 8
EPS = 1e-06
SMOOTHING = 0.1
CLIP_LEVEL = 0.001
SCALE = 0.125
LOG2_E = 1.4426950408889634
VMEM_BYTES = 63 * 2**20


def contract(a, b, ca, cb):
    return lax.dot_general(a, b, (((ca,), (cb,)), ((), ())), preferred_element_type=F32)


def nn(a, b):
    return contract(a, b, 1, 0)


def nt(a, b):
    return contract(a, b, 1, 1)


def tn(a, b):
    return contract(a, b, 0, 0)


def normalize(x):
    centred = x - jnp.mean(x, axis=-1, keepdims=True)
    rstd = lax.rsqrt(jnp.mean(centred * centred, axis=-1, keepdims=True) + EPS)
    return centred * rstd, rstd


def norm_grad(dy, xhat, rstd, gain):
    dx = dy * gain
    return rstd * (dx - jnp.mean(dx, axis=-1, keepdims=True) - xhat * jnp.mean(dx * xhat, axis=-1, keepdims=True))


def fold(x, op):
    x = x.reshape(x.shape[0] // 8, 8, x.shape[1])
    while x.shape[0] > 1:
        half = x.shape[0] // 2
        x = op(x[:half], x[half:])
    return x[0]


def column_sum(x):
    return jnp.sum(fold(x, jnp.add), axis=0, keepdims=True)


def half_of(x, half):
    lane = lax.broadcasted_iota(jnp.int32, x.shape, 1)
    keep = (lane < 64) if half == 0 else (lane >= 64)
    return jnp.where(keep, x, jnp.zeros_like(x))


def softmax_rows0(scores):
    top = jnp.max(fold(scores, jnp.maximum), axis=0, keepdims=True)
    exponent = jnp.exp2((scores - top) * (SCALE * LOG2_E))
    return exponent * (1.0 / column_sum(exponent))


def softmax_grad(soft, grad):
    mean = column_sum(grad * soft) / column_sum(soft)
    return soft * (grad - mean)


def gelu_both(c):
    k0 = 0.7978845608028654
    k1 = 0.044715 * k0
    c2 = c * c
    t = jnp.tanh(c * (k1 * c2 + k0))
    half = 0.5 * t + 0.5
    slope = half + c * (half - half * half) * (6.0 * k1 * c2 + 2.0 * k0)
    return c * half, slope


def shift_down(v):
    lane = lax.broadcasted_iota(jnp.int32, v.shape, 1)
    return jnp.where(lane == 0, 0.0, pltpu.roll(v, 1, 1))


def shift_up(v):
    lane = lax.broadcasted_iota(jnp.int32, v.shape, 1)
    return jnp.where(lane == 7, 0.0, pltpu.roll(v, 7, 1))


def class3(py, xm):
    return py * 4 + (xm & 1) * 2 + (xm >> 1)


def store3(plain, moved, plane, value):
    py, px = plane // 2, plane % 2
    value = value.reshape(2, 16, 8, value.shape[-1])
    for qx in range(2):
        plain[plane * 2 + qx, 1:17] = value[qx]
    if px == 1:
        moved[py * 2, 1:17] = shift_down(value[1])
    else:
        moved[py * 2 + 1, 1:17] = shift_up(value[0])


def tap3(plain, moved, py, xm, dy, dx, part, lanes):
    row = (py + dy) % 2
    start = 1 + (py + dy) // 2 + part * PART
    at = xm + dx
    if at == -1:
        return moved[row * 2, start : start + PART, :, lanes]
    if at == 4:
        return moved[row * 2 + 1, start : start + PART, :, lanes]
    return plain[class3(row, at), start : start + PART, :, lanes]


def store4(plain, moved, image, value):
    value = value.reshape(2, 16, 8, value.shape[-1])
    for qx in range(2):
        plain[image, qx, 1:17] = value[qx]
    moved[image, 0, 1:17] = shift_down(value[1])
    moved[image, 1, 1:17] = shift_up(value[0])


def tap4(plain, moved, image, qx, dy, dx, part, lanes):
    start = 1 + dy + part * PART
    at = qx + dx
    if at == -1:
        return moved[image, 0, start : start + PART, :, lanes]
    if at == 2:
        return moved[image, 1, start : start + PART, :, lanes]
    return plain[image, at, start : start + PART, :, lanes]


def up(value, unit):
    return -(-value // unit) * unit


def rows4(shards, groups):
    return up(10 * (C4 // shards) + (4 * C3 + F4) // shards, math.lcm(16, groups))


def places3(shards, groups):
    tall = (PATCH + 4 * C3 + F3) // shards // 2
    mats = up(tall, 16)
    slot = up(C3 // shards, 8)
    flat = up(mats + 4 * slot, 16)
    flat_rows = -(-(9 * (F3 + F4) + 2 * C3 + 8 * C4) // (shards * 2 * C3))
    last = flat + up(flat_rows, 8)
    return mats, slot, flat, flat_rows, last, up(last + 8, 8 * groups)


def piece_copy(out, target, sems, piece, at):
    shard, start, end = piece
    rows = pl.ds(start, end - start)
    return pltpu.make_async_copy(out.at[shard, rows], target.at[shard // 2, rows], sems.at[at])


def send_off(out, keep, send, sems, core, pieces, base):
    for at, piece in enumerate(pieces):

        @pl.when(core == piece[0] % 2)
        def _():
            piece_copy(out, keep, sems, piece, base + at).start()

        @pl.when(core != piece[0] % 2)
        def _():
            piece_copy(out, send, sems, piece, base + at).start()


def arrived(out, keep, sems, pieces, base):
    for at, piece in enumerate(pieces):
        piece_copy(out, keep, sems, piece, base + at).wait()


def store_columns4(out, value, column):
    size = C4 // out.shape[0]
    block, lane = column // C4, column % C4
    start = block * size
    lanes = slice(lane, lane + value.shape[1])
    if not isinstance(column, int):
        start = pl.multiple_of(start, size)
        lanes = pl.ds(pl.multiple_of(lane, LC), value.shape[1])
    for at in range(out.shape[0]):
        out[at, pl.ds(start, size), lanes] = value[at * size : at * size + size].astype(BF)


def store_rows(out, value, row, size, offset):
    at = row
    while at < row + value.shape[0]:
        shard = at // size
        end = min((shard + 1) * size, row + value.shape[0])
        start = offset + at - shard * size
        out[shard, start : start + end - at, :] = value[at - row : end - row].astype(BF)
        at = end


def alternate(many, few):
    done = 0
    for at, one in enumerate(many):
        one()
        while done < len(few) and (done + 1) * len(many) <= (at + 1) * len(few):
            few[done]()
            done += 1


TAPS = [(t, t // 3 - 1, t % 3 - 1) for t in range(9)]


def embed_attend(patches, tall3, mat3, norms, z_o, h_o, red_o, q_o, k_o, v_o, p_o, mix_o, x1_o, x0_s, vt_s):
    def embed(b):
        return nn(patches[0, b * 256 : b * 256 + 256, :], tall3[0:PATCH])

    def project(b, h):
        q_o[0, b * 256 : b * 256 + 256, :] = nn(h, mat3[:, 0:C3P]).astype(BF)
        return nn(h, tall3[PATCH + C3 * b : PATCH + C3 * (b + 1)])

    reduced = None
    later = embed(0)
    for b in range(4):
        rows = pl.ds(b * 256, 256)
        z = later
        if b < 3:
            later = embed(b + 1)
        z_o[0, rows, :] = z
        x0 = normalize(z)[0] * norms[0:1] + norms[1:2]
        x0_s[rows, :] = x0
        h = (normalize(x0)[0] * norms[2:3] + norms[3:4]).astype(BF)
        h_o[0, rows, :] = h
        if b > 0:
            part = project(b - 1, before)
            reduced = part if reduced is None else reduced + part
        before = h
    reduced = reduced + project(3, before)
    red_o[0] = reduced
    r = (normalize(reduced)[0] * norms[4:5] + norms[5:6]).astype(BF)
    k = nn(r, mat3[:, C3P : 2 * C3P]).astype(BF)
    v = nn(r, mat3[:, 2 * C3P : 3 * C3P]).astype(BF)
    k_o[0] = k
    v_o[0] = v
    vt_s[...] = v.T

    def queries():
        rows = [pl.ds(at * 256, 256) for at in range(4)]
        steps = [(rows[at], head) for at in range(4) for head in range(H3)]

        def raw(block, head):
            lanes = slice(head // 2 * 128, head // 2 * 128 + 128)
            return nt(half_of(k_o[0, :, lanes], head % 2), q_o[0, block, lanes])

        def mix(block, head, soft):
            mix_o[0, head * 64 : head * 64 + 64, block] = nn(vt_s[head * 64 : head * 64 + 64, :], soft).astype(BF)
            if head == H3 - 1:
                product = tn(mix_o[0, :, block], mat3[0:C3, 3 * C3P : 3 * C3P + C3])
                x1_o[0, block, :] = x0_s[block, :] + product

        later = raw(*steps[0])
        before = None
        for at, (block, head) in enumerate(steps):
            scores = later
            if at + 1 < len(steps):
                later = raw(*steps[at + 1])
            soft = softmax_rows0(scores).astype(BF)
            p_o[0, head, :, block] = soft
            if at > 0:
                mix(*steps[at - 1], before)
            before = soft
        mix(*steps[-1], before)

    queries()


def feed3(x1, tall3, mat3, depth, norms, n_o, hid_o, slope_o, act_o, x2_o, plain, moved, stage, cur, prev, total):
    @pl.when(pl.program_id(0) == 0)
    def _():
        for ref in (plain, moved):
            ref[:, 0:1] = jnp.zeros((ref.shape[0], 1, 8, LC), F32)
            ref[:, 17:18] = jnp.zeros((ref.shape[0], 1, 8, LC), F32)

    for b in range(4):
        rows = pl.ds(b * 256, 256)
        n_o[0, rows, :] = (normalize(x1[0, rows, :])[0] * norms[6:7] + norms[7:8]).astype(BF)

    chunks = F3 // LC

    def lanes_of(j):
        return pl.ds(pl.multiple_of(j * LC, LC), LC)

    def hidden(j, plane):
        rows = pl.ds(plane * 256, 256)
        stage[rows, :] = nn(n_o[0, rows, :], mat3[:, pl.ds(pl.multiple_of(4 * C3P + j * LC, LC), LC)])

    def spread(j):
        for plane in range(4):
            rows = pl.ds(plane * 256, 256)
            value = stage[rows, :]
            hid_o[0, rows, lanes_of(j)] = value.astype(BF)
            store3(plain, moved, plane, value)

    def second(j, b):
        rows = pl.ds(b * 256, 256)
        return total[rows, :] + nn(prev[rows, :], tall3[pl.ds(pl.multiple_of(PATCH + 4 * C3 + j * LC, LC), LC), :])

    for plane in range(4):
        hidden(0, plane)
    spread(0)
    total[...] = x1[0]
    prev[...] = jnp.zeros_like(prev)

    def chunk(j, carry):
        later = jnp.minimum(j + 1, chunks - 1)
        previous = jnp.maximum(j - 1, 0)
        kernels = [depth[:, pl.ds(pl.multiple_of(j * LC + lt * 128, 128), 128)] for lt in range(LC // 128)]

        def convolve(lt, py, xm, part):
            lanes = pl.ds(lt * 128, 128)
            out_lanes = pl.ds(pl.multiple_of(j * LC + lt * 128, 128), 128)
            out = None
            for t, dy, dx in TAPS:
                term = tap3(plain, moved, py, xm, dy, dx, part, lanes) * kernels[lt][t : t + 1][None]
                out = term if out is None else out + term
            activated, slope = gelu_both(out)
            rows = pl.ds(class3(py, xm) * 128 + part * PART * 8, PART * 8)
            cur[rows, lanes] = activated.reshape(PART * 8, 128).astype(BF)
            slope_o[0, rows, out_lanes] = slope.reshape(PART * 8, 128).astype(BF)

        def accumulate(b):
            total[b * 256 : b * 256 + 256, :] = second(previous, b)

        products = []
        for b in range(4):
            products += [functools.partial(hidden, later, b), functools.partial(accumulate, b)]
        alternate(
            [
                functools.partial(convolve, lt, py, xm, part)
                for lt in range(LC // 128)
                for py in range(2)
                for xm in range(4)
                for part in range(16 // PART)
            ],
            products,
        )
        prev[...] = cur[...]
        act_o[0, :, lanes_of(j)] = cur[...]
        spread(later)
        return carry

    lax.fori_loop(0, chunks, chunk, 0)
    for b in range(4):
        x2_o[0, b * 256 : b * 256 + 256, :] = second(chunks - 1, b).astype(BF)


def section4(
    labels, valid, inv_count, core, x2_h, mat4_h, tall4_h, depth, norms,
    dx2_h, keep, send, gd_o, gn_o, loss_o,
    x2, mat4, tall4, sems, out, first, y1_s, y2_s, h_s, qkv_s, p_s, mix_s, n_s, nt_s, hid_s, slope_s, act_s, plain,
    moved, gd_s, stage, cur, prev,
):
    def load(source, target, at):
        return pltpu.make_async_copy(source, target, sems.at[at])

    loads = [load(tall4_h.at[0 : 4 * C3], tall4.at[0 : 4 * C3], 0)]
    loads += [load(x2_h.at[i], x2.at[i], 1 + i) for i in range(IMGS)]
    loads += [load(mat4_h, mat4, 5), load(tall4_h.at[4 * C3 :], tall4.at[4 * C3 :], 6)]
    for one in loads:
        one.start()
    for ref in (plain, moved):
        for at in (0, 17):
            ref[:, :, at : at + 1] = jnp.zeros((IMGS, 2, 1, 8, LC), F32)

    w1_at = 4 * C4
    wc_at = 4 * C4 + F4
    shards = out.shape[0]
    tall_rows = (4 * C3 + F4) // shards
    tall_at = 10 * (C4 // shards)

    loads[0].wait()
    def downsample(i):
        loads[1 + i].wait()
        prod = None
        for plane in range(4):
            part = nn(x2[i, plane * 256 : plane * 256 + 256, :], tall4[plane * C3 : plane * C3 + C3, :])
            prod = part if prod is None else prod + part
        return prod

    def project(i):
        rows = pl.ds(i * TOK4, TOK4)
        for j in range(3):
            wide = slice(j * C4, j * C4 + C4)
            qkv_s[rows, wide] = nn(h_s[rows, :], mat4[:, wide]).astype(BF)

    later = downsample(0)
    for i in range(IMGS):
        rows = pl.ds(i * TOK4, TOK4)
        prod = later
        if i + 1 < IMGS:
            later = downsample(i + 1)
        first[rows, :] = prod
        y0 = normalize(prod)[0] * norms[0:1] + norms[1:2]
        y1_s[rows, :] = y0
        if i == 1:
            loads[5].wait()
        if i > 0:
            project(i - 1)
        h_s[rows, :] = (normalize(y0)[0] * norms[2:3] + norms[3:4]).astype(BF)
    project(IMGS - 1)

    def attend(pair, carry):
        steps = [(pair * 2 + at, head) for at in range(2) for head in range(H4)]

        def image(i):
            return pl.ds(pl.multiple_of(i * TOK4, TOK4), TOK4)

        def raw(i, head):
            at = head // 2 * 128
            key = half_of(qkv_s[image(i), C4 + at : C4 + at + 128], head % 2)
            return nt(key, qkv_s[image(i), at : at + 128])

        def mix(i, head, soft):
            at = 2 * C4 + head // 2 * 128
            if head % 2 == 0:
                values.append(qkv_s[image(i), at : at + 128].T)
            half = values[-1][head % 2 * 64 : head % 2 * 64 + 64]
            mix_s[head * 64 : head * 64 + 64, image(i)] = nn(half, soft).astype(BF)

        values = []
        later = raw(*steps[0])
        before = None
        for at, (i, head) in enumerate(steps):
            scores = later
            if at + 1 < len(steps):
                later = raw(*steps[at + 1])
            soft = softmax_rows0(scores).astype(BF)
            p_s[i * H4 + head] = soft
            if at > 0:
                mix(*steps[at - 1], before)
            before = soft
        mix(*steps[-1], before)
        return carry

    lax.fori_loop(0, IMGS // 2, attend, 0)

    def output(i):
        return tn(mix_s[:, i * TOK4 : i * TOK4 + TOK4], mat4[:, 3 * C4 : 4 * C4])

    later = output(0)
    for i in range(IMGS):
        rows = pl.ds(i * TOK4, TOK4)
        y1 = y1_s[rows, :] + later
        if i + 1 < IMGS:
            later = output(i + 1)
        y1_s[rows, :] = y1
        y2_s[rows, :] = y1
        n_s[rows, :] = (normalize(y1)[0] * norms[4:5] + norms[5:6]).astype(BF)
    loads[6].wait()

    chunks = F4 // LC
    blocks = [(lt, i, qx, p) for lt in range(LC // 128) for i in range(IMGS) for qx in range(2) for p in range(16 // PART)]

    def lanes_of(j):
        return pl.ds(pl.multiple_of(j * LC, LC), LC)

    def second_rows(j):
        return tall4[pl.ds(pl.multiple_of(4 * C3 + j * LC, LC), LC), :]

    def taps_of(j):
        return [depth[:, pl.ds(pl.multiple_of(j * LC + lt * 128, 128), 128)] for lt in range(LC // 128)]

    def image_rows(i):
        return pl.ds(i * TOK4, TOK4)

    def hidden(j, i):
        stage[image_rows(i), :] = nn(n_s[image_rows(i), :], mat4[:, pl.ds(pl.multiple_of(w1_at + j * LC, LC), LC)])

    def spread(j):
        for i in range(IMGS):
            value = stage[image_rows(i), :]
            hid_s[image_rows(i), lanes_of(j)] = value.astype(BF)
            store4(plain, moved, i, value)

    def accumulate(j, i):
        y2_s[image_rows(i), :] += nn(prev[image_rows(i), :], second_rows(j))

    for i in range(IMGS):
        hidden(0, i)
    spread(0)
    prev[...] = jnp.zeros_like(prev)

    def feed(j, carry):
        later, previous = jnp.minimum(j + 1, chunks - 1), jnp.maximum(j - 1, 0)
        kernels = taps_of(j)

        def convolve(lt, i, qx, part):
            lanes = pl.ds(lt * 128, 128)
            total = None
            for t, dy, dx in TAPS:
                term = tap4(plain, moved, i, qx, dy, dx, part, lanes) * kernels[lt][t : t + 1][None]
                total = term if total is None else total + term
            activated, slope = gelu_both(total)
            rows = pl.ds(i * TOK4 + qx * 128 + part * PART * 8, PART * 8)
            cur[rows, lanes] = activated.reshape(PART * 8, 128).astype(BF)
            out_lanes = pl.ds(pl.multiple_of(j * LC + lt * 128, 128), 128)
            slope_s[rows, out_lanes] = slope.reshape(PART * 8, 128).astype(BF)

        products = []
        for i in range(IMGS):
            products += [functools.partial(hidden, later, i), functools.partial(accumulate, previous, i)]
        alternate([functools.partial(convolve, *block) for block in blocks], products)
        prev[...] = cur[...]
        act_s[:, lanes_of(j)] = cur[...]
        spread(later)
        return carry

    lax.fori_loop(0, chunks, feed, 0)

    pools = []
    hat_means = []
    for i in range(IMGS):
        accumulate(chunks - 1, i)
    for i in range(IMGS):
        hat_mean = jnp.mean(normalize(y2_s[image_rows(i), :])[0], axis=0, keepdims=True)
        hat_means.append(hat_mean)
        pools.append(hat_mean * norms[6:7] + norms[7:8])
    pooled = jnp.concatenate(pools + [jnp.zeros((8 - IMGS, C4), F32)], axis=0).astype(BF)
    logits = nn(pooled, mat4[:, wc_at:])

    row = lax.broadcasted_iota(jnp.int32, (8, CLASSES), 0)
    column = lax.broadcasted_iota(jnp.int32, (8, CLASSES), 1)
    target = jnp.full((8, CLASSES), -1, jnp.int32)
    present = jnp.zeros((8, CLASSES), F32)
    for i in range(IMGS):
        target = jnp.where(row == i, labels[i], target)
        present = jnp.where(row == i, valid[i].astype(F32), present)
    goal = (1.0 - SMOOTHING) * (column == target).astype(F32) + SMOOTHING / CLASSES
    shifted = logits - jnp.max(logits, axis=-1, keepdims=True)
    exponent = jnp.exp(shifted)
    mass = jnp.sum(exponent, axis=-1, keepdims=True)
    log_probs = shifted - jnp.log(mass)
    ce = -jnp.sum(goal * log_probs, axis=-1, keepdims=True)
    loss_o[...] = jnp.broadcast_to(jnp.sum(present[:, 0:1] * ce, axis=0, keepdims=True), (8, 128))
    dlogits = (present * inv_count[0] * (exponent / mass - goal)).astype(BF)

    dclass = tn(pooled, dlogits)
    store_columns4(out, dclass[:, :C4], wc_at)
    store_columns4(out, jnp.concatenate([dclass[:, C4:], jnp.zeros((C4, 2 * C4 - CLASSES), F32)], axis=1), wc_at + C4)
    if tall_at + tall_rows < out.shape[1]:
        out[:, tall_at + tall_rows :, :] = jnp.zeros((shards, out.shape[1] - tall_at - tall_rows, C4), BF)
    dpool = nt(dlogits, mat4[:, wc_at:])
    dgain = None
    for i in range(IMGS):
        rows = pl.ds(i * TOK4, TOK4)
        one = dpool[i : i + 1]
        part = one * hat_means[i]
        dgain = part if dgain is None else dgain + part
        xhat, rstd = normalize(y2_s[rows, :])
        dy2 = norm_grad(jnp.broadcast_to(one * (1.0 / TOK4), (TOK4, C4)), xhat, rstd, norms[6:7])
        y2_s[rows, :] = dy2
    gn_o[6:7] = dgain
    gn_o[7:8] = column_sum(dpool)

    for i in range(IMGS):
        nt_s[:, i * TOK4 : i * TOK4 + TOK4] = n_s[image_rows(i), :].T
        n_s[image_rows(i), :] = y2_s[image_rows(i), :].astype(BF)

    def hidden_grad(j, i):
        stage[image_rows(i), :] = nt(n_s[image_rows(i), :], second_rows(j))

    def spread_grad(j):
        for i in range(IMGS):
            store4(plain, moved, i, stage[image_rows(i), :] * slope_s[image_rows(i), lanes_of(j)].astype(F32))

    def first_grad(j):
        store_columns4(out, nn(nt_s[...], hid_s[:, lanes_of(j)]), w1_at + j * LC)

    for i in range(IMGS):
        hidden_grad(0, i)
    spread_grad(0)

    def feed_back(j, carry):
        later, previous = jnp.minimum(j + 1, chunks - 1), jnp.maximum(j - 1, 0)
        kernels = taps_of(j)
        sums = [[None] * 9 for _ in kernels]

        def convolve(lt, i, qx, part):
            lanes = pl.ds(lt * 128, 128)
            out_lanes = pl.ds(pl.multiple_of(j * LC + lt * 128, 128), 128)
            rows = pl.ds(i * TOK4 + qx * 128 + part * PART * 8, PART * 8)
            base = hid_s[rows, out_lanes].astype(F32).reshape(PART, 8, 128)
            acc = None
            for t, dy, dx in TAPS:
                value = tap4(plain, moved, i, qx, -dy, -dx, part, lanes)
                term = value * kernels[lt][t : t + 1][None]
                acc = term if acc is None else acc + term
                tap_sum = jnp.sum(value * base, axis=0)
                sums[lt][t] = tap_sum if sums[lt][t] is None else sums[lt][t] + tap_sum
            cur[rows, lanes] = acc.reshape(PART * 8, 128).astype(BF)

        def second_grad():
            grad = tn(act_s[:, lanes_of(j)], n_s[...]).astype(BF)
            act_s[0:LC, lanes_of(j)] = grad[:, 0:LC]
            act_s[LC : 2 * LC, lanes_of(j)] = grad[:, LC:]

        products = [second_grad, functools.partial(first_grad, previous)]
        products += [functools.partial(hidden_grad, later, i) for i in range(IMGS)]
        alternate([functools.partial(convolve, *block) for block in blocks], products)
        for lt in range(LC // 128):
            for t in range(9):
                gd_s[t, :, pl.ds(pl.multiple_of(j * LC + lt * 128, 128), 128)] = sums[lt][t]
        hid_s[:, lanes_of(j)] = cur[...]
        spread_grad(later)
        return carry

    lax.fori_loop(0, chunks, feed_back, 0)
    first_grad(chunks - 1)
    for j in range(chunks):
        wide = slice(j * LC, j * LC + LC)
        grad = jnp.concatenate([act_s[0:LC, wide], act_s[LC : 2 * LC, wide]], axis=1)
        store_rows(out, grad, 4 * C3 + j * LC, tall_rows, tall_at)
    for t in range(9):
        gd_o[t : t + 1, :] = column_sum(gd_s[t])

    mats_done, tall_done = 4 * (C4 // shards), up(4 * C3, tall_rows) // tall_rows
    early = [(at, mats_done, tall_at) for at in range(shards)]
    early += [(at, tall_at, out.shape[1]) for at in range(tall_done, shards)]
    send_off(out, keep, send, sems, core[0], early, 8)

    def normed_grad(i):
        return nt(hid_s[image_rows(i), :], mat4[:, w1_at : w1_at + F4])

    dgain = dshift = None
    later = normed_grad(0)
    for i in range(IMGS):
        rows = image_rows(i)
        dn = later
        if i + 1 < IMGS:
            later = normed_grad(i + 1)
        xhat, rstd = normalize(y1_s[rows, :])
        part_g, part_s = column_sum(dn * xhat), column_sum(dn)
        dgain = part_g if dgain is None else dgain + part_g
        dshift = part_s if dshift is None else dshift + part_s
        y2_s[rows, :] = y2_s[rows, :] + norm_grad(dn, xhat, rstd, norms[4:5])
    gn_o[4:5] = dgain
    gn_o[5:6] = dshift

    dprod = y2_s[...].astype(BF)
    store_columns4(out, nn(mix_s[...], dprod), 3 * C4)
    for i in range(IMGS):
        rows = pl.ds(i * TOK4, TOK4)
        n_s[rows, :] = nt(dprod[i * TOK4 : i * TOK4 + TOK4], mat4[:, 3 * C4 : 4 * C4]).astype(BF)

    d_s = slope_s

    def attend_back(pair, carry):
        lane = lax.broadcasted_iota(jnp.int32, (TOK4, 128), 1)
        steps = [(pair * 2 + at, head) for at in range(2) for head in range(H4)]
        dqts, dks, dvs, keys = [], [], [], []

        def image(i):
            return pl.ds(pl.multiple_of(i * TOK4, TOK4), TOK4)

        def at(head):
            return head // 2 * 128

        def first_product(i, head):
            start = 2 * C4 + at(head)
            return nt(half_of(qkv_s[image(i), start : start + 128], head % 2), n_s[image(i), at(head) : at(head) + 128])

        def last_products(i, head, ds):
            dks.append(nn(ds, qkv_s[image(i), at(head) : at(head) + 128]))
            if head % 2 == 0:
                keys.append(qkv_s[image(i), C4 + at(head) : C4 + at(head) + 128].T)
            dqts.append(nn(keys[-1][head % 2 * 64 : head % 2 * 64 + 64], ds))
            if head % 2 == 1:
                start, one = at(head), len(dks) - 1
                dqt = (jnp.concatenate(dqts[-2:], axis=0) * SCALE).astype(BF)
                dk = (jnp.where(lane < 64, dks[one - 1], dks[one]) * SCALE).astype(BF)
                dv = jnp.where(lane < 64, dvs[one - 1], dvs[one]).astype(BF)
                d_s[image(i), start : start + 128] = dqt.T
                d_s[image(i), C4 + start : C4 + start + 128] = dk
                d_s[image(i), 2 * C4 + start : 2 * C4 + start + 128] = dv

        later = first_product(*steps[0])
        before = None
        for step, (i, head) in enumerate(steps):
            dp = later
            if step + 1 < len(steps):
                later = first_product(*steps[step + 1])
            soft = p_s[i * H4 + head]
            dvs.append(nn(soft, n_s[image(i), at(head) : at(head) + 128]))
            ds = softmax_grad(soft.astype(F32), dp).astype(BF)
            if step > 0:
                last_products(*steps[step - 1], before)
            before = ds
        last_products(*steps[-1], before)
        return carry

    lax.fori_loop(0, IMGS // 2, attend_back, 0)
    ht = h_s[...].T
    for j in range(3):
        wide = slice(j * C4, j * C4 + C4)
        store_columns4(out, nn(ht, d_s[:, wide]), j * C4)

    def normed_grad0(i):
        return nt(d_s[image_rows(i), 0 : 3 * C4], mat4[:, 0 : 3 * C4])

    sums = [None] * 4
    later = normed_grad0(0)
    for i in range(IMGS):
        rows = image_rows(i)
        dh = later
        if i + 1 < IMGS:
            later = normed_grad0(i + 1)
        hat0, rstd0 = normalize(first[rows, :])
        hat1, rstd1 = normalize(hat0 * norms[0:1] + norms[1:2])
        dy0 = y2_s[rows, :] + norm_grad(dh, hat1, rstd1, norms[2:3])
        n_s[rows, :] = norm_grad(dy0, hat0, rstd0, norms[0:1]).astype(BF)
        parts = [column_sum(dy0 * hat0), column_sum(dy0), column_sum(dh * hat1), column_sum(dh)]
        sums = [part if old is None else old + part for old, part in zip(sums, parts)]
    gn_o[0:4] = jnp.concatenate(sums, axis=0)
    for plane in range(4):
        total = None
        for i in range(IMGS):
            part = tn(x2[i, plane * 256 : plane * 256 + 256, :], n_s[image_rows(i), :])
            total = part if total is None else total + part
        store_rows(out, total, plane * C3, tall_rows, tall_at)
    late = [(at, 0, mats_done) for at in range(shards)] + [(at, tall_at, out.shape[1]) for at in range(tall_done)]
    send_off(out, keep, send, sems, core[0], late, 8 + len(early))
    stores = [load(x2.at[i], dx2_h.at[i], 1 + i) for i in range(IMGS)]
    for i in range(IMGS):
        for plane in range(4):
            grad = nt(n_s[image_rows(i), :], tall4[plane * C3 : plane * C3 + C3, :])
            x2[i, plane * 256 : plane * 256 + 256, :] = grad.astype(BF)
        stores[i].start()
    for one in stores:
        one.wait()
    arrived(out, keep, sems, early, 8)
    arrived(out, keep, sems, late, 8 + len(early))


def feed3_back(dx2, x1, n, hid, slope, act, tall3, mat3, depth, norms, dx1_o, g1_o, g2_o, gd_o, gn_o,
               acc1, acc2, accd, accn, plain, moved, dy_s, dyt_s, nt_s, da_s, stage, cur):
    step = pl.program_id(0)

    @pl.when(step == 0)
    def _():
        for ref in (plain, moved):
            ref[:, 0:1] = jnp.zeros((ref.shape[0], 1, 8, LC), F32)
            ref[:, 17:18] = jnp.zeros((ref.shape[0], 1, 8, LC), F32)
        for ref in (acc1, acc2, accd, accn):
            ref[...] = jnp.zeros_like(ref)

    dy = dx2[0]
    dy_s[...] = dy
    dyt_s[...] = dy.T
    nt_s[...] = n[0].T

    chunks = F3 // LC

    def lanes_of(j):
        return pl.ds(pl.multiple_of(j * LC, LC), LC)

    def hidden_grad(j, plane):
        rows = pl.ds(plane * 256, 256)
        w2 = tall3[pl.ds(pl.multiple_of(PATCH + 4 * C3 + j * LC, LC), LC), :]
        stage[rows, :] = nt(dy_s[rows, :], w2)

    def spread(j):
        for plane in range(4):
            rows = pl.ds(plane * 256, 256)
            store3(plain, moved, plane, stage[rows, :] * slope[0, rows, lanes_of(j)].astype(F32))

    def first_grad(j):
        acc1[:, lanes_of(j)] += nn(nt_s[...], da_s[:, lanes_of(j)])

    for plane in range(4):
        hidden_grad(0, plane)
    spread(0)

    def chunk(j, carry):
        later = jnp.minimum(j + 1, chunks - 1)
        previous = jnp.where(j > 0, j - 1, chunks)
        kernels, sums = [], []
        for lt in range(LC // 128):
            kernels.append(depth[:, pl.ds(pl.multiple_of(j * LC + lt * 128, 128), 128)])
            sums.append([None] * 9)

        def convolve(lt, py, xm, part):
            lanes = pl.ds(lt * 128, 128)
            out_lanes = pl.ds(pl.multiple_of(j * LC + lt * 128, 128), 128)
            rows = pl.ds(class3(py, xm) * 128 + part * PART * 8, PART * 8)
            base = hid[0, rows, out_lanes].astype(F32).reshape(PART, 8, 128)
            out = None
            for t, dy, dx in TAPS:
                value = tap3(plain, moved, py, xm, -dy, -dx, part, lanes)
                term = value * kernels[lt][t : t + 1][None]
                out = term if out is None else out + term
                tap_sum = jnp.sum(value * base, axis=0)
                sums[lt][t] = tap_sum if sums[lt][t] is None else sums[lt][t] + tap_sum
            cur[rows, lanes] = out.reshape(PART * 8, 128).astype(BF)

        def second_grad():
            acc2[:, lanes_of(j)] += nn(dyt_s[...], act[0, :, lanes_of(j)])

        products = [second_grad, functools.partial(first_grad, previous)]
        products += [functools.partial(hidden_grad, later, plane) for plane in range(4)]
        alternate(
            [
                functools.partial(convolve, lt, py, xm, part)
                for lt in range(LC // 128)
                for py in range(2)
                for xm in range(4)
                for part in range(16 // PART)
            ],
            products,
        )
        for lt in range(LC // 128):
            for t in range(9):
                accd[t, :, pl.ds(pl.multiple_of(j * LC + lt * 128, 128), 128)] += sums[lt][t]
        da_s[:, lanes_of(j)] = cur[...]
        spread(later)
        return carry

    lax.fori_loop(0, chunks, chunk, 0)
    first_grad(chunks - 1)

    def normed_grad(b):
        return nt(da_s[b * 256 : b * 256 + 256, 0:F3], mat3[:, 4 * C3P :])

    later = normed_grad(0)
    for b in range(4):
        rows = pl.ds(b * 256, 256)
        dn = later
        if b < 3:
            later = normed_grad(b + 1)
        xhat, rstd = normalize(x1[0, rows, :])
        accn[0:1] += column_sum(dn * xhat)
        accn[1:2] += column_sum(dn)
        dx1_o[0, rows, :] = dx2[0, rows, :].astype(F32) + norm_grad(dn, xhat, rstd, norms[6:7])

    @pl.when(step == IMGS - 1)
    def _():
        g1_o[...] = acc1[:, 0:F3]
        g2_o[...] = acc2[...].T.astype(g2_o.dtype)
        gn_o[...] = accn[...]
        for t in range(9):
            gd_o[t : t + 1, :] = column_sum(accd[t])


def attend3_back(groups, core, dx1, z, h, red, q, k, v, p, mix, patches, tall3, mat3, norms, g1, g2, flat, keep, send, out, sems,
                 tall_s, acce, accr, accq, acck, accv, acco, accn, dk_s, dv_s, kt_s, dqt_s, dr_s):
    step = pl.program_id(0)

    @pl.when(step == 0)
    def _():
        for ref in (acce, accr, accq, acck, accv, acco, accn):
            ref[...] = jnp.zeros_like(ref)

    kt_s[...] = k[0].T
    dk_s[...] = jnp.zeros_like(dk_s)
    dv_s[...] = jnp.zeros_like(dv_s)
    wo = mat3[0:C3, 3 * C3P : 3 * C3P + C3]
    lane = lax.broadcasted_iota(jnp.int32, (256, 128), 1)

    def queries():
        rows = [pl.ds(at * 256, 256) for at in range(4)]
        lanes = [slice(at * 128, at * 128 + 128) for at in range(3)]
        mixed, dks, dvs = [], [], []
        for block in rows:
            dprod = dx1[0, block, :].astype(BF)
            acco[...] += nn(mix[0, :, block], dprod)
            dmix = nt(dprod, wo).astype(BF)
            mixed.append(jnp.concatenate([dmix, jnp.zeros((256, C3P - C3), BF)], axis=1))
        steps = [(at, head) for at in range(4) for head in range(H3)]

        def first(at, head):
            return nt(half_of(v[0, :, lanes[head // 2]], head % 2), mixed[at][:, lanes[head // 2]])

        def last(at, head, ds):
            dks.append(nn(ds, q[0, rows[at], lanes[head // 2]]))
            dqt = nn(kt_s[head * 64 : head * 64 + 64, :], ds) * SCALE
            dqt_s[head * 64 : head * 64 + 64, rows[at]] = dqt.astype(BF)

        later = first(*steps[0])
        before = None
        for step_at, (at, head) in enumerate(steps):
            dp = later
            if step_at + 1 < len(steps):
                later = first(*steps[step_at + 1])
            soft = p[0, head, :, rows[at]]
            dvs.append(nn(soft, mixed[at][:, lanes[head // 2]]))
            ds = softmax_grad(soft.astype(F32), dp).astype(BF)
            if step_at > 0:
                last(*steps[step_at - 1], before)
            before = ds
        last(*steps[-1], before)
        for at in range(4):
            for pair_at in range(2):
                one = at * H3 + 2 * pair_at
                dk_s[:, lanes[pair_at]] += jnp.where(lane < 64, dks[one], dks[one + 1])
                dv_s[:, lanes[pair_at]] += jnp.where(lane < 64, dvs[one], dvs[one + 1])
            dk_s[:, lanes[2]] += dks[at * H3 + 4]
            dv_s[:, lanes[2]] += dvs[at * H3 + 4]

    queries()

    dk = (dk_s[...] * SCALE).astype(BF)
    dv = dv_s[...].astype(BF)
    hat_r, rstd_r = normalize(red[0])
    r = (hat_r * norms[4:5] + norms[5:6]).astype(BF)
    acck[...] += tn(r, dk)
    accv[...] += tn(r, dv)
    dr = nt(dk, mat3[:, C3P : 2 * C3P]) + nt(dv, mat3[:, 2 * C3P : 3 * C3P])
    accn[4:5] += column_sum(dr * hat_r)
    accn[5:6] += column_sum(dr)
    dred = norm_grad(dr, hat_r, rstd_r, norms[4:5]).astype(BF)
    accq[...] += nn(dqt_s[...], h[0])

    def input_grad(b):
        rows = slice(b * 256, b * 256 + 256)
        wr = tall3[PATCH + C3 * b : PATCH + C3 * (b + 1)]
        return contract(dqt_s[:, rows], mat3[:, 0:C3], 0, 1) + nt(dred, wr)

    def weight_grads(b, dz):
        rows = slice(b * 256, b * 256 + 256)
        accr[C3 * b : C3 * (b + 1)] += tn(h[0, rows, :], dred)
        acce[...] += tn(dz, patches[0, rows, :])

    later = input_grad(0)
    before = None
    for b in range(4):
        rows = pl.ds(b * 256, 256)
        dh = later
        if b < 3:
            later = input_grad(b + 1)
        hat0, rstd0 = normalize(z[0, rows, :])
        hat1, rstd1 = normalize(hat0 * norms[0:1] + norms[1:2])
        accn[2:3] += column_sum(dh * hat1)
        accn[3:4] += column_sum(dh)
        dx0 = dx1[0, rows, :] + norm_grad(dh, hat1, rstd1, norms[2:3])
        accn[0:1] += column_sum(dx0 * hat0)
        accn[1:2] += column_sum(dx0)
        dz = norm_grad(dx0, hat0, rstd0, norms[0:1]).astype(BF)
        if b > 0:
            weight_grads(b - 1, before)
        before = dz
    weight_grads(3, before)

    @pl.when(step == IMGS - 1)
    def _():
        shards = out.shape[0]
        mats, slot, flat_at, flat_rows, last, total_rows = places3(shards, groups)
        mat_rows = C3 // shards
        tall = (PATCH + 4 * C3 + F3) // shards // 2
        out[:, mats:, :] = jnp.zeros((shards, total_rows - mats, 2 * C3), BF)
        if tall < mats:
            out[:, tall:mats, :] = jnp.zeros((shards, mats - tall, 2 * C3), BF)
        tall_s[0:PATCH] = acce[...].T
        tall_s[PATCH : PATCH + 4 * C3] = accr[...]
        tall_s[PATCH + 4 * C3 :] = g2[...].astype(F32)
        accq[...] = accq[...].T
        for at in range(shards):
            rows = slice(at * mat_rows, at * mat_rows + mat_rows)
            pieces = [accq[rows, :], acck[rows, 0:C3], accv[rows, 0:C3], acco[rows, :]]
            start = at * 2 * tall
            pairs = [tall_s[start : start + tall], tall_s[start + tall : start + 2 * tall]]
            out[at, 0:tall, :] = jnp.concatenate(pairs, axis=1).astype(BF)
            for b in range(2):
                pair = jnp.concatenate(pieces[2 * b : 2 * b + 2], axis=1)
                out[at, mats + b * slot : mats + b * slot + mat_rows, :] = pair.astype(BF)
                feed = g1[rows, b * 2 * C3 : b * 2 * C3 + 2 * C3]
                out[at, mats + (b + 2) * slot : mats + (b + 2) * slot + mat_rows, :] = feed.astype(BF)
            out[at, flat_at : flat_at + flat_rows, :] = flat[at]
            out[at, last : last + 6, 0:mat_rows] = accn[:, rows].astype(BF)
        pieces = [(at, 0, total_rows) for at in range(shards)]
        send_off(out, keep, send, sems, core[0], pieces, 0)
        arrived(out, keep, sems, pieces, 0)


def whole(shape, dtype=None):
    return pl.BlockSpec(shape, lambda i: (0,) * len(shape), pipeline_mode=pl.Buffered(1))


def per_image(*shape):
    return pl.BlockSpec((1,) + shape, lambda i: (i,) + (0,) * len(shape))


def sds(*shape, dtype=F32):
    return jax.ShapeDtypeStruct(shape, dtype)


def work(microseconds):
    return pl.CostEstimate(flops=microseconds * 10**9, bytes_accessed=microseconds * 3 * 10**6, transcendentals=0)


PARAMS = pltpu.CompilerParams(vmem_limit_bytes=VMEM_BYTES, dimension_semantics=("arbitrary",))


def unpack3(pack, tall3, mat3):
    half = tall3.shape[0] // pack.shape[0] // 2
    size = C3 // pack.shape[0]
    for at in range(pack.shape[0]):
        start = at * 2 * half
        tall3[start : start + half, :] = pack[at, 0:half, 0:C3]
        tall3[start + half : start + 2 * half, :] = pack[at, 0:half, C3:]
        rows = slice(at * size, at * size + size)
        for b in range(2):
            piece = pack[at, half + b * size : half + (b + 1) * size, :]
            blank = jnp.zeros((size, C3P - C3), BF)
            wide = jnp.concatenate([piece[:, :C3], blank, piece[:, C3:], blank], axis=1)
            mat3[rows, b * 2 * C3P : (b + 1) * 2 * C3P] = wide
            feed = pack[at, half + (b + 2) * size : half + (b + 3) * size, :]
            mat3[rows, 4 * C3P + b * 2 * C3 : 4 * C3P + (b + 1) * 2 * C3] = feed


def forward3(packed, *refs):
    if packed:
        pack, patches, depth, norms, tall3, mat3 = refs[:6]

        @pl.when(pl.program_id(0) == 0)
        def _():
            unpack3(pack, tall3, mat3)

    else:
        tall3, mat3, patches, depth, norms = refs[:5]
    refs = refs[6 if packed else 5 :]
    x1 = refs[8]
    embed_attend(patches, tall3, mat3, norms, *refs[:9], *refs[14:16])
    feed3(x1, tall3, mat3, depth, norms, *refs[9:14], *refs[16:])


def run_forward3(weights, patches, depth, norms3):
    packed = len(weights) == 1
    tall_shape, mat_shape = (PATCH + 4 * C3 + F3, C3), (C3, 4 * C3P + F3)
    full = [whole(tall_shape), whole(mat_shape)] if packed else []
    full_shapes = [sds(*tall_shape, dtype=BF), sds(*mat_shape, dtype=BF)] if packed else []
    weight_specs = [whole(weight.shape) for weight in weights]
    image_specs = [per_image(TOK3, PATCH), whole(depth.shape), whole(norms3.shape)]
    outs = pl.pallas_call(
        functools.partial(forward3, packed),
        grid=(IMGS,),
        in_specs=weight_specs + image_specs,
        out_specs=full + [
            per_image(TOK3, C3), per_image(TOK3, C3), per_image(256, C3), per_image(TOK3, C3P), per_image(256, C3P),
            per_image(256, C3P), per_image(H3, 256, TOK3), per_image(C3, TOK3), per_image(TOK3, C3),
            per_image(TOK3, C3), per_image(TOK3, F3), per_image(TOK3, F3), per_image(TOK3, F3), per_image(TOK3, C3),
        ],
        out_shape=full_shapes + [
            sds(IMGS, TOK3, C3), sds(IMGS, TOK3, C3, dtype=BF), sds(IMGS, 256, C3), sds(IMGS, TOK3, C3P, dtype=BF),
            sds(IMGS, 256, C3P, dtype=BF), sds(IMGS, 256, C3P, dtype=BF), sds(IMGS, H3, 256, TOK3, dtype=BF),
            sds(IMGS, C3, TOK3, dtype=BF), sds(IMGS, TOK3, C3),
            sds(IMGS, TOK3, C3, dtype=BF), sds(IMGS, TOK3, F3, dtype=BF), sds(IMGS, TOK3, F3, dtype=BF),
            sds(IMGS, TOK3, F3, dtype=BF), sds(IMGS, TOK3, C3, dtype=BF),
        ],
        scratch_shapes=[
            pltpu.VMEM((TOK3, C3), F32), pltpu.VMEM((C3P, 256), BF),
            pltpu.VMEM((8, 18, 8, LC), F32), pltpu.VMEM((4, 18, 8, LC), F32), pltpu.VMEM((TOK3, LC), F32),
            pltpu.VMEM((TOK3, LC), BF), pltpu.VMEM((TOK3, LC), BF), pltpu.VMEM((TOK3, C3), F32),
        ],
        compiler_params=PARAMS,
        name="forward3",
        cost_estimate=work(85),
    )(*weights, patches, depth, norms3)
    return outs if packed else [*weights, *outs]


def run_section4(labels, valid, inv_count, core, x2, mat4, tall4, depth, norms4, shards, groups):
    vm = pl.BlockSpec(memory_space=pltpu.VMEM)
    sm = pl.BlockSpec(memory_space=pltpu.SMEM)
    hbm = pl.BlockSpec(memory_space=pl.ANY)
    rows = IMGS * TOK4
    half = sds(shards // 2, rows4(shards, groups), C4, dtype=BF)
    return pl.pallas_call(
        section4,
        in_specs=[sm, sm, sm, sm, hbm, hbm, hbm, vm, vm],
        out_specs=[hbm, hbm, hbm, vm, vm, vm],
        out_shape=[
            sds(IMGS, TOK3, C3, dtype=BF), half, half, sds(9, F4), sds(8, C4),
            sds(8, 128),
        ],
        scratch_shapes=[
            pltpu.VMEM(x2.shape, BF), pltpu.VMEM(mat4.shape, BF), pltpu.VMEM(tall4.shape, BF),
            pltpu.SemaphoreType.DMA((8 + 3 * shards,)), pltpu.VMEM((shards,) + half.shape[1:], BF),
            pltpu.VMEM((rows, C4), F32), pltpu.VMEM((rows, C4), F32), pltpu.VMEM((rows, C4), F32),
            pltpu.VMEM((rows, C4), BF), pltpu.VMEM((rows, 3 * C4), BF), pltpu.VMEM((IMGS * H4, 256, 256), BF),
            pltpu.VMEM((C4, rows), BF), pltpu.VMEM((rows, C4), BF), pltpu.VMEM((C4, rows), BF), pltpu.VMEM((rows, F4), BF),
            pltpu.VMEM((rows, F4), BF), pltpu.VMEM((rows, F4), BF), pltpu.VMEM((IMGS, 2, 18, 8, LC), F32),
            pltpu.VMEM((IMGS, 2, 18, 8, LC), F32), pltpu.VMEM((9, 8, F4), F32),
            pltpu.VMEM((rows, LC), F32), pltpu.VMEM((rows, LC), BF), pltpu.VMEM((rows, LC), BF),
        ],
        compiler_params=pltpu.CompilerParams(vmem_limit_bytes=VMEM_BYTES),
        name="section4",
        cost_estimate=work(90),
    )(labels, valid, inv_count, core, x2, mat4, tall4, depth, norms4)


def run_feed3_back(dx2, x1, n, hid, slope, act, tall3, mat3, depth, norms3):
    return pl.pallas_call(
        feed3_back,
        grid=(IMGS,),
        in_specs=[
            per_image(TOK3, C3), per_image(TOK3, C3), per_image(TOK3, C3), per_image(TOK3, F3), per_image(TOK3, F3),
            per_image(TOK3, F3), whole(tall3.shape), whole(mat3.shape), whole(depth.shape), whole(norms3.shape),
        ],
        out_specs=[per_image(TOK3, C3), whole((C3, F3)), whole((F3, C3)), whole((9, F3)), whole((2, C3))],
        out_shape=[sds(IMGS, TOK3, C3), sds(C3, F3), sds(F3, C3, dtype=BF), sds(9, F3), sds(2, C3)],
        scratch_shapes=[
            pltpu.VMEM((C3, F3 + LC), F32), pltpu.VMEM((C3, F3), F32), pltpu.VMEM((9, 8, F3), F32), pltpu.VMEM((2, C3), F32),
            pltpu.VMEM((8, 18, 8, LC), F32), pltpu.VMEM((4, 18, 8, LC), F32), pltpu.VMEM((TOK3, C3), BF),
            pltpu.VMEM((C3, TOK3), BF), pltpu.VMEM((C3, TOK3), BF), pltpu.VMEM((TOK3, F3 + LC), BF),
            pltpu.VMEM((TOK3, LC), F32), pltpu.VMEM((TOK3, LC), BF),
        ],
        compiler_params=PARAMS,
        name="feed3_back",
        cost_estimate=work(68),
    )(dx2, x1, n, hid, slope, act, tall3, mat3, depth, norms3)


def run_attend3_back(core, dx1, z, h, red, q, k, v, p, mix, patches, tall3, mat3, norms3, g1, g2, flat, groups):
    shards = flat.shape[0]
    total_rows = places3(shards, groups)[-1]
    return pl.pallas_call(
        functools.partial(attend3_back, groups),
        grid=(IMGS,),
        in_specs=[
            pl.BlockSpec(memory_space=pltpu.SMEM),
            per_image(TOK3, C3), per_image(TOK3, C3), per_image(TOK3, C3), per_image(256, C3), per_image(TOK3, C3P),
            per_image(256, C3P), per_image(256, C3P), per_image(H3, 256, TOK3), per_image(C3, TOK3),
            per_image(TOK3, PATCH), whole(tall3.shape), whole(mat3.shape), whole(norms3.shape),
            whole(g1.shape), whole(g2.shape), whole(flat.shape),
        ],
        out_specs=[pl.BlockSpec(memory_space=pl.ANY)] * 2,
        out_shape=[sds(shards // 2, total_rows, 2 * C3, dtype=BF)] * 2,
        scratch_shapes=[
            pltpu.VMEM((shards, total_rows, 2 * C3), BF), pltpu.SemaphoreType.DMA((shards,)),
            pltpu.VMEM((PATCH + 4 * C3 + F3, C3), F32),
            pltpu.VMEM((C3, PATCH), F32), pltpu.VMEM((4 * C3, C3), F32), pltpu.VMEM((C3, C3), F32),
            pltpu.VMEM((C3, C3P), F32), pltpu.VMEM((C3, C3P), F32), pltpu.VMEM((C3, C3), F32), pltpu.VMEM((6, C3), F32),
            pltpu.VMEM((256, C3P), F32), pltpu.VMEM((256, C3P), F32), pltpu.VMEM((C3P, 256), BF),
            pltpu.VMEM((C3, TOK3), BF), pltpu.VMEM((256, C3), F32),
        ],
        compiler_params=PARAMS,
        name="attend3_back",
        cost_estimate=work(65),
    )(core, dx1, z, h, red, q, k, v, p, mix, patches, tall3, mat3, norms3, g1, g2, flat)


def pad_mat3(mat):
    pieces = [mat[:, at * C3 : at * C3 + C3] for at in range(4)]
    pieces = [jnp.pad(piece, ((0, 0), (0, C3P - C3))) for piece in pieces]
    return jnp.concatenate(pieces + [mat[:, 4 * C3 :]], axis=1)


def reorder(patches):
    count = patches.shape[0]
    grid = patches.reshape(count, 16, 2, 8, 2, 2, patches.shape[-1])
    return grid.transpose(0, 2, 5, 4, 1, 3, 6).reshape(patches.shape)


def swap(value, axis, mask):
    return lax.ppermute(value, axis, [(at, at ^ mask) for at in range(lax.axis_size(axis))])


def pick(value, index, axis=0):
    return lax.dynamic_index_in_dim(value, index, axis, keepdims=False)


def add_all(own, parts):
    total = own.astype(F32)
    for part in parts:
        total = total + part.astype(F32)
    return total


def chip_sends(keep, got):
    chip = lax.axis_index("fsdp") // 2
    masks = range(1, keep.shape[0])
    return [add_all(pick(keep, chip ^ mask), [pick(got, chip ^ mask)]).astype(BF) for mask in masks]


def chip_own(keep, got):
    chip = lax.axis_index("fsdp") // 2
    return add_all(pick(keep, chip), [pick(got, chip)])


def depth_sends(shard):
    count, me = lax.axis_size("dp"), lax.axis_index("dp")
    cut = shard.reshape(count, shard.shape[0] // count, shard.shape[1])
    return pick(cut, me), [pick(cut, me ^ mask).astype(BF) for mask in range(1, count)]


def exchange(sends, axis, unit):
    return [swap(send, axis, unit * (at + 1)) for at, send in enumerate(sends)]


def depth_gather(piece):
    count, me = lax.axis_size("dp"), lax.axis_index("dp")
    narrow = piece.astype(BF)
    parts = [narrow] + [swap(narrow, "dp", mask) for mask in range(1, count)]
    placed = [lax.select_n(me, *[parts[at ^ other] for other in range(count)]) for at in range(count)]
    return jnp.concatenate(placed, axis=0).astype(F32)


def total_over_all(row):
    count = lax.axis_size("dp") * lax.axis_size("fsdp")
    rows = jnp.broadcast_to(row, (count, row.shape[1]))
    return jnp.sum(lax.all_to_all(rows, ("dp", "fsdp"), 0, 0, tiled=True), axis=0, keepdims=True)


def adamw(master, moment, second, gradient, is_norm):
    step_rate = 0.5 if is_norm else 0.05
    decay_now = 0.0 if is_norm else 0.05
    first = 0.9 * moment + 0.1 * gradient
    second_new = 0.999 * second + 0.001 * gradient * gradient
    first_hat = first * (1.0 / (1.0 - 0.9**STEP))
    second_hat = second_new * (1.0 / (1.0 - 0.999**STEP))
    updated = master - step_rate * (first_hat / (jnp.sqrt(second_hat) + 1e-08) + decay_now * master)
    return (updated, first, second_new)


def body(patches, labels, valid, *state):
    masters, moments, seconds = state[0:7], state[7:14], state[14:21]
    shards, groups = lax.axis_size("fsdp"), lax.axis_size("dp")
    mat3, tall3, mat4, tall4, depth, norms3, norms4 = [master.astype(BF) for master in masters]
    half, m_rows = tall3.shape[0] // 2, mat3.shape[0]
    pack = [jnp.concatenate([tall3[:half], tall3[half:]], axis=1)]
    pack += [mat3[:, at * 2 * C3 : at * 2 * C3 + 2 * C3] for at in range(4)]
    pack = lax.all_gather(jnp.concatenate(pack, axis=0), "fsdp", axis=0)

    small = [jnp.pad(piece.T, ((0, 0), (0, 16 - piece.shape[0]))) for piece in (depth, norms3, norms4)]
    small.append(jnp.full((8, 16), jnp.sum(valid)).astype(BF))
    sizes = [piece.shape[0] for piece in small]
    small = lax.all_gather(jnp.concatenate(small, axis=0), "fsdp", axis=0)
    edges = [0, sizes[0], sizes[0] + sizes[1], sum(sizes[:3])]
    parts = [small[:, edges[at] : edges[at + 1]].reshape(-1, 16).T.astype(F32) for at in range(3)]
    depth_all, norms3_all, norms4_all = parts[0][:9], parts[1][:8], parts[2][:8]
    present = jnp.full((8, 128), jnp.sum(small[:, edges[3], 0].astype(F32)))
    others = exchange([present] * (groups - 1), "dp", 1)

    weights3 = [pack]
    if half % 8 or m_rows % 8:
        tall3_all = jnp.concatenate([pack[:, :half, :C3], pack[:, :half, C3:]], axis=1).reshape(-1, C3)
        mats = pack[:, half:].reshape(shards, 4, m_rows, 2 * C3).transpose(1, 0, 2, 3).reshape(4, C3, 2 * C3)
        mat3_all = [mats[at // 2, :, at % 2 * C3 : at % 2 * C3 + C3] for at in range(4)]
        mat3_all = [jnp.pad(piece, ((0, 0), (0, C3P - C3))) for piece in mat3_all]
        weights3 = [tall3_all, jnp.concatenate(mat3_all + [mats[2], mats[3]], axis=1)]
    tall4_all = lax.all_gather(tall4, "fsdp", axis=0, tiled=True)
    mat4_all = lax.all_gather(mat4, "fsdp", axis=0, tiled=True)

    patches = reorder(patches.reshape(IMGS, TOK3, PATCH))
    depth3, depth4 = depth_all[:, :F3], depth_all[:, F3:]
    tall3_all, mat3_all, z, h, red, q, k, v, p, mix, x1, n, hid, slope, act, x2 = run_forward3(
        weights3, patches, depth3, norms3_all
    )
    x2, others = lax.optimization_barrier((x2, others))
    image_count = add_all(present, others)[0, 0]
    inv_count = (1.0 / image_count).reshape(1)
    core = (lax.axis_index("fsdp") % 2).reshape(1)
    dx2, keep4, send4, gd4, gn4, loss = run_section4(
        labels.reshape(IMGS), valid.reshape(IMGS), inv_count, core, x2, mat4_all, tall4_all, depth4, norms4_all,
        shards, groups,
    )

    core4 = swap(send4, "fsdp", 1)
    sends4 = chip_sends(keep4, core4)
    dx2, keep4, core4, sends4 = lax.optimization_barrier((dx2, keep4, core4, sends4))
    got4 = exchange(sends4, "fsdp", 2)
    dx1, g1, g2, gd3, gn3b = run_feed3_back(dx2, x1, n, hid, slope, act, tall3_all, mat3_all, depth3, norms3_all)
    dx1, keep4, core4, got4 = lax.optimization_barrier((dx1, keep4, core4, got4))
    own4, sends4 = depth_sends(add_all(chip_own(keep4, core4), got4))

    def by_columns(grad):
        return grad.reshape(grad.shape[0], shards, -1).transpose(1, 0, 2).reshape(shards, -1)

    _, slot, flat_at, flat_rows, last, _ = places3(shards, groups)
    flat = jnp.concatenate([by_columns(grad) for grad in (jnp.concatenate([gd3, gd4], axis=1), gn3b, gn4)], axis=1)
    flat = jnp.pad(flat, ((0, 0), (0, flat_rows * 2 * C3 - flat.shape[1])))
    flat = flat.reshape(shards, flat_rows, 2 * C3).astype(BF)
    dx1, own4, sends4, flat = lax.optimization_barrier((dx1, own4, sends4, flat))
    got4 = exchange(sends4, "dp", 1)
    keep3, send3 = run_attend3_back(
        core, dx1, z, h, red, q, k, v, p, mix, patches, tall3_all, mat3_all, norms3_all, g1, g2, flat, groups
    )
    keep3, send3, got4 = lax.optimization_barrier((keep3, send3, got4))
    piece4 = add_all(own4, got4)
    core3 = swap(send3, "fsdp", 1)
    sends3 = chip_sends(keep3, core3)
    keep3, core3, sends3, piece4 = lax.optimization_barrier((keep3, core3, sends3, piece4))
    got3 = exchange(sends3, "fsdp", 2)
    grads4 = depth_gather(piece4)
    keep3, core3, got3, grads4 = lax.optimization_barrier((keep3, core3, got3, grads4))
    own3, sends3 = depth_sends(add_all(chip_own(keep3, core3), got3))
    piece3 = add_all(own3, exchange(sends3, "dp", 1))
    square = jnp.sum(piece4 * piece4) + jnp.sum(piece3 * piece3)
    lane = lax.broadcasted_iota(jnp.int32, (1, 128), 1)
    totals = total_over_all(jnp.where(lane == 0, square, loss[0:1]))
    grads3 = depth_gather(piece3)

    m_rows, t_rows = C4 // shards, masters[3].shape[0]
    blocks4 = [grads4[at * m_rows : at * m_rows + m_rows] for at in range(10)]
    grad_mat4 = jnp.concatenate(blocks4, axis=1)[:, : masters[2].shape[1]]
    grad_tall4 = grads4[10 * m_rows : 10 * m_rows + t_rows]
    t_rows, m_rows = masters[1].shape[0], masters[0].shape[0]
    mats_at, half = up(t_rows // 2, 16), t_rows // 2
    grad_tall3 = jnp.concatenate([grads3[:half, :C3], grads3[:half, C3:]], axis=0)
    grad_mat3 = jnp.concatenate([grads3[mats_at + at * slot : mats_at + at * slot + m_rows] for at in range(4)], axis=1)
    flat = grads3[flat_at : flat_at + flat_rows].reshape(-1)
    sizes = [9 * t_rows, 2 * m_rows, masters[6].size]
    grad_depth = flat[: sizes[0]].reshape(9, t_rows)
    grad_norms3 = jnp.concatenate(
        [grads3[last : last + 6, :m_rows], flat[sizes[0] : sizes[0] + sizes[1]].reshape(2, m_rows)], axis=0
    )
    grad_norms4 = flat[sizes[0] + sizes[1] : sum(sizes)].reshape(masters[6].shape)
    group = [grad_mat3, grad_tall3, grad_mat4, grad_tall4, grad_depth, grad_norms3, grad_norms4]

    grad_norm = jnp.sqrt(totals[0, 0])
    clip_factor = jnp.minimum(1.0, CLIP_LEVEL / (grad_norm + 1e-06))
    results = [adamw(masters[at], moments[at], seconds[at], clip_factor * group[at], at >= 5) for at in range(7)]
    return (
        *[result[0] for result in results],
        *[result[1] for result in results],
        *[result[2] for result in results],
        totals[0, 1],
        image_count,
        grad_norm,
    )


def solution(mesh):
    rows, columns = P("fsdp", None), P(None, "fsdp")
    weights = (rows,) * 4 + (columns,) * 3
    images = P(None, ("dp", "fsdp"))
    in_specs = (P(None, ("dp", "fsdp"), None, None), images, images) + weights * 3
    out_specs = weights * 3 + (P(), P(), P())
    return jax.shard_map(body, mesh=mesh, in_specs=in_specs, out_specs=out_specs, check_vma=False)
```

```python
import functools
import math

import jax
import jax.numpy as jnp
from jax import lax
from jax.experimental import pallas as pl
from jax.experimental.pallas import tpu as pltpu
from jax.sharding import PartitionSpec as P

BF = jnp.bfloat16
F32 = jnp.float32
C3 = 320
C3P = 384
H3 = 5
F3 = 1280
C4 = 512
H4 = 8
F4 = 2048
CLASSES = 1000
PATCH = 768
STEP = 10
IMGS = 4
TOK3 = 1024
TOK4 = 256
LC = 256
PART = 8
EPS = 1e-06
SMOOTHING = 0.1
CLIP_LEVEL = 0.001
SCALE = 0.125
LOG2_E = 1.4426950408889634
VMEM_BYTES = 63 * 2**20


def contract(a, b, ca, cb):
    return lax.dot_general(a, b, (((ca,), (cb,)), ((), ())), preferred_element_type=F32)


def nn(a, b):
    return contract(a, b, 1, 0)


def nt(a, b):
    return contract(a, b, 1, 1)


def tn(a, b):
    return contract(a, b, 0, 0)


def normalize(x):
    centred = x - jnp.mean(x, axis=-1, keepdims=True)
    rstd = lax.rsqrt(jnp.mean(centred * centred, axis=-1, keepdims=True) + EPS)
    return centred * rstd, rstd


def norm_grad(dy, xhat, rstd, gain):
    dx = dy * gain
    return rstd * (dx - jnp.mean(dx, axis=-1, keepdims=True) - xhat * jnp.mean(dx * xhat, axis=-1, keepdims=True))


def fold(x, op):
    x = x.reshape(x.shape[0] // 8, 8, x.shape[1])
    while x.shape[0] > 1:
        half = x.shape[0] // 2
        x = op(x[:half], x[half:])
    return x[0]


def column_sum(x):
    return jnp.sum(fold(x, jnp.add), axis=0, keepdims=True)


def half_of(x, half):
    lane = lax.broadcasted_iota(jnp.int32, x.shape, 1)
    keep = (lane < 64) if half == 0 else (lane >= 64)
    return jnp.where(keep, x, jnp.zeros_like(x))


def softmax_rows0(scores):
    top = jnp.max(fold(scores, jnp.maximum), axis=0, keepdims=True)
    exponent = jnp.exp2((scores - top) * (SCALE * LOG2_E))
    return exponent * (1.0 / column_sum(exponent))


def softmax_grad(soft, grad):
    mean = column_sum(grad * soft) / column_sum(soft)
    return soft * (grad - mean)


def gelu_both(c):
    k0 = 0.7978845608028654
    k1 = 0.044715 * k0
    c2 = c * c
    t = jnp.tanh(c * (k1 * c2 + k0))
    half = 0.5 * t + 0.5
    slope = half + c * (half - half * half) * (6.0 * k1 * c2 + 2.0 * k0)
    return c * half, slope


def shift_down(v):
    lane = lax.broadcasted_iota(jnp.int32, v.shape, 1)
    return jnp.where(lane == 0, 0.0, pltpu.roll(v, 1, 1))


def shift_up(v):
    lane = lax.broadcasted_iota(jnp.int32, v.shape, 1)
    return jnp.where(lane == 7, 0.0, pltpu.roll(v, 7, 1))


def class3(py, xm):
    return py * 4 + (xm & 1) * 2 + (xm >> 1)


def store3(plain, moved, plane, value):
    py, px = plane // 2, plane % 2
    value = value.reshape(2, 16, 8, value.shape[-1])
    for qx in range(2):
        plain[plane * 2 + qx, 1:17] = value[qx]
    if px == 1:
        moved[py * 2, 1:17] = shift_down(value[1])
    else:
        moved[py * 2 + 1, 1:17] = shift_up(value[0])


def tap3(plain, moved, py, xm, dy, dx, part, lanes):
    row = (py + dy) % 2
    start = 1 + (py + dy) // 2 + part * PART
    at = xm + dx
    if at == -1:
        return moved[row * 2, start : start + PART, :, lanes]
    if at == 4:
        return moved[row * 2 + 1, start : start + PART, :, lanes]
    return plain[class3(row, at), start : start + PART, :, lanes]


def store4(plain, moved, image, value):
    value = value.reshape(2, 16, 8, value.shape[-1])
    for qx in range(2):
        plain[image, qx, 1:17] = value[qx]
    moved[image, 0, 1:17] = shift_down(value[1])
    moved[image, 1, 1:17] = shift_up(value[0])


def tap4(plain, moved, image, qx, dy, dx, part, lanes):
    start = 1 + dy + part * PART
    at = qx + dx
    if at == -1:
        return moved[image, 0, start : start + PART, :, lanes]
    if at == 2:
        return moved[image, 1, start : start + PART, :, lanes]
    return plain[image, at, start : start + PART, :, lanes]


def up(value, unit):
    return -(-value // unit) * unit


def rows4(shards, groups):
    return up(10 * (C4 // shards) + (4 * C3 + F4) // shards, math.lcm(16, groups))


def places3(shards, groups):
    tall = (PATCH + 4 * C3 + F3) // shards // 2
    mats = up(tall, 16)
    slot = up(C3 // shards, 8)
    flat = up(mats + 4 * slot, 16)
    flat_rows = -(-(9 * (F3 + F4) + 2 * C3 + 8 * C4) // (shards * 2 * C3))
    last = flat + up(flat_rows, 8)
    return mats, slot, flat, flat_rows, last, up(last + 8, 8 * groups)


def piece_copy(out, target, sems, piece, at):
    shard, start, end = piece
    rows = pl.ds(start, end - start)
    return pltpu.make_async_copy(out.at[shard, rows], target.at[shard // 2, rows], sems.at[at])


def send_off(out, keep, send, sems, core, pieces, base):
    for at, piece in enumerate(pieces):

        @pl.when(core == piece[0] % 2)
        def _():
            piece_copy(out, keep, sems, piece, base + at).start()

        @pl.when(core != piece[0] % 2)
        def _():
            piece_copy(out, send, sems, piece, base + at).start()


def arrived(out, keep, sems, pieces, base):
    for at, piece in enumerate(pieces):
        piece_copy(out, keep, sems, piece, base + at).wait()


def store_columns4(out, value, column):
    size = C4 // out.shape[0]
    block, lane = column // C4, column % C4
    start = block * size
    lanes = slice(lane, lane + value.shape[1])
    if not isinstance(column, int):
        start = pl.multiple_of(start, size)
        lanes = pl.ds(pl.multiple_of(lane, LC), value.shape[1])
    for at in range(out.shape[0]):
        out[at, pl.ds(start, size), lanes] = value[at * size : at * size + size].astype(BF)


def store_rows(out, value, row, size, offset):
    at = row
    while at < row + value.shape[0]:
        shard = at // size
        end = min((shard + 1) * size, row + value.shape[0])
        start = offset + at - shard * size
        out[shard, start : start + end - at, :] = value[at - row : end - row].astype(BF)
        at = end


def alternate(many, few):
    done = 0
    for at, one in enumerate(many):
        one()
        while done < len(few) and (done + 1) * len(many) <= (at + 1) * len(few):
            few[done]()
            done += 1


TAPS = [(t, t // 3 - 1, t % 3 - 1) for t in range(9)]


def embed_attend(patches, tall3, mat3, norms, z_o, h_o, red_o, q_o, k_o, v_o, p_o, mix_o, x1_o, x0_s, vt_s):
    def embed(b):
        return nn(patches[0, b * 256 : b * 256 + 256, :], tall3[0:PATCH])

    def project(b, h):
        q_o[0, b * 256 : b * 256 + 256, :] = nn(h, mat3[:, 0:C3P]).astype(BF)
        return nn(h, tall3[PATCH + C3 * b : PATCH + C3 * (b + 1)])

    reduced = None
    later = embed(0)
    for b in range(4):
        rows = pl.ds(b * 256, 256)
        z = later
        if b < 3:
            later = embed(b + 1)
        z_o[0, rows, :] = z
        x0 = normalize(z)[0] * norms[0:1] + norms[1:2]
        x0_s[rows, :] = x0
        h = (normalize(x0)[0] * norms[2:3] + norms[3:4]).astype(BF)
        h_o[0, rows, :] = h
        if b > 0:
            part = project(b - 1, before)
            reduced = part if reduced is None else reduced + part
        before = h
    reduced = reduced + project(3, before)
    red_o[0] = reduced
    r = (normalize(reduced)[0] * norms[4:5] + norms[5:6]).astype(BF)
    k = nn(r, mat3[:, C3P : 2 * C3P]).astype(BF)
    v = nn(r, mat3[:, 2 * C3P : 3 * C3P]).astype(BF)
    k_o[0] = k
    v_o[0] = v
    vt_s[...] = v.T

    def queries():
        rows = [pl.ds(at * 256, 256) for at in range(4)]
        steps = [(rows[at], head) for at in range(4) for head in range(H3)]

        def raw(block, head):
            lanes = slice(head // 2 * 128, head // 2 * 128 + 128)
            return nt(half_of(k_o[0, :, lanes], head % 2), q_o[0, block, lanes])

        def mix(block, head, soft):
            mix_o[0, head * 64 : head * 64 + 64, block] = nn(vt_s[head * 64 : head * 64 + 64, :], soft).astype(BF)
            if head == H3 - 1:
                product = tn(mix_o[0, :, block], mat3[0:C3, 3 * C3P : 3 * C3P + C3])
                x1_o[0, block, :] = x0_s[block, :] + product

        later = raw(*steps[0])
        before = None
        for at, (block, head) in enumerate(steps):
            scores = later
            if at + 1 < len(steps):
                later = raw(*steps[at + 1])
            soft = softmax_rows0(scores).astype(BF)
            p_o[0, head, :, block] = soft
            if at > 0:
                mix(*steps[at - 1], before)
            before = soft
        mix(*steps[-1], before)

    queries()


def feed3(x1, tall3, mat3, depth, norms, n_o, hid_o, slope_o, act_o, x2_o, plain, moved, stage, cur, prev, total):
    @pl.when(pl.program_id(0) == 0)
    def _():
        for ref in (plain, moved):
            ref[:, 0:1] = jnp.zeros((ref.shape[0], 1, 8, LC), F32)
            ref[:, 17:18] = jnp.zeros((ref.shape[0], 1, 8, LC), F32)

    for b in range(4):
        rows = pl.ds(b * 256, 256)
        n_o[0, rows, :] = (normalize(x1[0, rows, :])[0] * norms[6:7] + norms[7:8]).astype(BF)

    chunks = F3 // LC

    def lanes_of(j):
        return pl.ds(pl.multiple_of(j * LC, LC), LC)

    def hidden(j, plane):
        rows = pl.ds(plane * 256, 256)
        stage[rows, :] = nn(n_o[0, rows, :], mat3[:, pl.ds(pl.multiple_of(4 * C3P + j * LC, LC), LC)])

    def spread(j):
        for plane in range(4):
            rows = pl.ds(plane * 256, 256)
            value = stage[rows, :]
            hid_o[0, rows, lanes_of(j)] = value.astype(BF)
            store3(plain, moved, plane, value)

    def second(j, b):
        rows = pl.ds(b * 256, 256)
        return total[rows, :] + nn(prev[rows, :], tall3[pl.ds(pl.multiple_of(PATCH + 4 * C3 + j * LC, LC), LC), :])

    for plane in range(4):
        hidden(0, plane)
    spread(0)
    total[...] = x1[0]
    prev[...] = jnp.zeros_like(prev)

    def chunk(j, carry):
        later = jnp.minimum(j + 1, chunks - 1)
        previous = jnp.maximum(j - 1, 0)
        kernels = [depth[:, pl.ds(pl.multiple_of(j * LC + lt * 128, 128), 128)] for lt in range(LC // 128)]

        def convolve(lt, py, xm, part):
            lanes = pl.ds(lt * 128, 128)
            out_lanes = pl.ds(pl.multiple_of(j * LC + lt * 128, 128), 128)
            out = None
            for t, dy, dx in TAPS:
                term = tap3(plain, moved, py, xm, dy, dx, part, lanes) * kernels[lt][t : t + 1][None]
                out = term if out is None else out + term
            activated, slope = gelu_both(out)
            rows = pl.ds(class3(py, xm) * 128 + part * PART * 8, PART * 8)
            cur[rows, lanes] = activated.reshape(PART * 8, 128).astype(BF)
            slope_o[0, rows, out_lanes] = slope.reshape(PART * 8, 128).astype(BF)

        def accumulate(b):
            total[b * 256 : b * 256 + 256, :] = second(previous, b)

        products = []
        for b in range(4):
            products += [functools.partial(hidden, later, b), functools.partial(accumulate, b)]
        alternate(
            [
                functools.partial(convolve, lt, py, xm, part)
                for lt in range(LC // 128)
                for py in range(2)
                for xm in range(4)
                for part in range(16 // PART)
            ],
            products,
        )
        prev[...] = cur[...]
        act_o[0, :, lanes_of(j)] = cur[...]
        spread(later)
        return carry

    lax.fori_loop(0, chunks, chunk, 0)
    for b in range(4):
        x2_o[0, b * 256 : b * 256 + 256, :] = second(chunks - 1, b).astype(BF)


def section4(
    labels, valid, inv_count, core, x2_h, mat4_h, tall4_h, depth, norms,
    dx2_h, keep, send, gd_o, gn_o, loss_o,
    x2, mat4, tall4, sems, out, first, y1_s, y2_s, h_s, qkv_s, p_s, mix_s, n_s, nt_s, hid_s, slope_s, act_s, plain,
    moved, gd_s, stage, cur, prev,
):
    def load(source, target, at):
        return pltpu.make_async_copy(source, target, sems.at[at])

    loads = [load(tall4_h.at[0 : 4 * C3], tall4.at[0 : 4 * C3], 0)]
    loads += [load(x2_h.at[i], x2.at[i], 1 + i) for i in range(IMGS)]
    loads += [load(mat4_h, mat4, 5), load(tall4_h.at[4 * C3 :], tall4.at[4 * C3 :], 6)]
    for one in loads:
        one.start()
    for ref in (plain, moved):
        for at in (0, 17):
            ref[:, :, at : at + 1] = jnp.zeros((IMGS, 2, 1, 8, LC), F32)

    w1_at = 4 * C4
    wc_at = 4 * C4 + F4
    shards = out.shape[0]
    tall_rows = (4 * C3 + F4) // shards
    tall_at = 10 * (C4 // shards)

    loads[0].wait()
    def downsample(i):
        loads[1 + i].wait()
        prod = None
        for plane in range(4):
            part = nn(x2[i, plane * 256 : plane * 256 + 256, :], tall4[plane * C3 : plane * C3 + C3, :])
            prod = part if prod is None else prod + part
        return prod

    def project(i):
        rows = pl.ds(i * TOK4, TOK4)
        for j in range(3):
            wide = slice(j * C4, j * C4 + C4)
            qkv_s[rows, wide] = nn(h_s[rows, :], mat4[:, wide]).astype(BF)

    later = downsample(0)
    for i in range(IMGS):
        rows = pl.ds(i * TOK4, TOK4)
        prod = later
        if i + 1 < IMGS:
            later = downsample(i + 1)
        first[rows, :] = prod
        y0 = normalize(prod)[0] * norms[0:1] + norms[1:2]
        y1_s[rows, :] = y0
        if i == 1:
            loads[5].wait()
        if i > 0:
            project(i - 1)
        h_s[rows, :] = (normalize(y0)[0] * norms[2:3] + norms[3:4]).astype(BF)
    project(IMGS - 1)

    def attend(pair, carry):
        steps = [(pair * IMGS + at, head) for at in range(IMGS) for head in range(H4)]

        def image(i):
            return pl.ds(pl.multiple_of(i * TOK4, TOK4), TOK4)

        def raw(i, head):
            at = head // 2 * 128
            key = half_of(qkv_s[image(i), C4 + at : C4 + at + 128], head % 2)
            return nt(key, qkv_s[image(i), at : at + 128])

        def mix(i, head, soft):
            at = 2 * C4 + head // 2 * 128
            if head % 2 == 0:
                values.append(qkv_s[image(i), at : at + 128].T)
            half = values[-1][head % 2 * 64 : head % 2 * 64 + 64]
            mix_s[head * 64 : head * 64 + 64, image(i)] = nn(half, soft).astype(BF)

        values = []
        later = raw(*steps[0])
        before = None
        for at, (i, head) in enumerate(steps):
            scores = later
            if at + 1 < len(steps):
                later = raw(*steps[at + 1])
            soft = softmax_rows0(scores).astype(BF)
            p_s[i * H4 + head] = soft
            if at > 0:
                mix(*steps[at - 1], before)
            before = soft
        mix(*steps[-1], before)
        return carry

    lax.fori_loop(0, 1, attend, 0)

    def output(i):
        return tn(mix_s[:, i * TOK4 : i * TOK4 + TOK4], mat4[:, 3 * C4 : 4 * C4])

    later = output(0)
    for i in range(IMGS):
        rows = pl.ds(i * TOK4, TOK4)
        y1 = y1_s[rows, :] + later
        if i + 1 < IMGS:
            later = output(i + 1)
        y1_s[rows, :] = y1
        y2_s[rows, :] = y1
        n_s[rows, :] = (normalize(y1)[0] * norms[4:5] + norms[5:6]).astype(BF)
    loads[6].wait()

    chunks = F4 // LC
    blocks = [(lt, i, qx, p) for lt in range(LC // 128) for i in range(IMGS) for qx in range(2) for p in range(16 // PART)]

    def lanes_of(j):
        return pl.ds(pl.multiple_of(j * LC, LC), LC)

    def second_rows(j):
        return tall4[pl.ds(pl.multiple_of(4 * C3 + j * LC, LC), LC), :]

    def taps_of(j):
        return [depth[:, pl.ds(pl.multiple_of(j * LC + lt * 128, 128), 128)] for lt in range(LC // 128)]

    def image_rows(i):
        return pl.ds(i * TOK4, TOK4)

    def hidden(j, i):
        stage[image_rows(i), :] = nn(n_s[image_rows(i), :], mat4[:, pl.ds(pl.multiple_of(w1_at + j * LC, LC), LC)])

    def spread(j):
        for i in range(IMGS):
            value = stage[image_rows(i), :]
            hid_s[image_rows(i), lanes_of(j)] = value.astype(BF)
            store4(plain, moved, i, value)

    def accumulate(j, i):
        y2_s[image_rows(i), :] += nn(prev[image_rows(i), :], second_rows(j))

    for i in range(IMGS):
        hidden(0, i)
    spread(0)
    prev[...] = jnp.zeros_like(prev)

    def feed(j, carry):
        later, previous = jnp.minimum(j + 1, chunks - 1), jnp.maximum(j - 1, 0)
        kernels = taps_of(j)

        def convolve(lt, i, qx, part):
            lanes = pl.ds(lt * 128, 128)
            total = None
            for t, dy, dx in TAPS:
                term = tap4(plain, moved, i, qx, dy, dx, part, lanes) * kernels[lt][t : t + 1][None]
                total = term if total is None else total + term
            activated, slope = gelu_both(total)
            rows = pl.ds(i * TOK4 + qx * 128 + part * PART * 8, PART * 8)
            cur[rows, lanes] = activated.reshape(PART * 8, 128).astype(BF)
            out_lanes = pl.ds(pl.multiple_of(j * LC + lt * 128, 128), 128)
            slope_s[rows, out_lanes] = slope.reshape(PART * 8, 128).astype(BF)

        products = []
        for i in range(IMGS):
            products += [functools.partial(hidden, later, i), functools.partial(accumulate, previous, i)]
        alternate([functools.partial(convolve, *block) for block in blocks], products)
        prev[...] = cur[...]
        act_s[:, lanes_of(j)] = cur[...]
        spread(later)
        return carry

    lax.fori_loop(0, chunks, feed, 0)

    pools = []
    hat_means = []
    for i in range(IMGS):
        accumulate(chunks - 1, i)
    for i in range(IMGS):
        hat_mean = jnp.mean(normalize(y2_s[image_rows(i), :])[0], axis=0, keepdims=True)
        hat_means.append(hat_mean)
        pools.append(hat_mean * norms[6:7] + norms[7:8])
    pooled = jnp.concatenate(pools + [jnp.zeros((8 - IMGS, C4), F32)], axis=0).astype(BF)
    logits = nn(pooled, mat4[:, wc_at:])

    row = lax.broadcasted_iota(jnp.int32, (8, CLASSES), 0)
    column = lax.broadcasted_iota(jnp.int32, (8, CLASSES), 1)
    target = jnp.full((8, CLASSES), -1, jnp.int32)
    present = jnp.zeros((8, CLASSES), F32)
    for i in range(IMGS):
        target = jnp.where(row == i, labels[i], target)
        present = jnp.where(row == i, valid[i].astype(F32), present)
    goal = (1.0 - SMOOTHING) * (column == target).astype(F32) + SMOOTHING / CLASSES
    shifted = logits - jnp.max(logits, axis=-1, keepdims=True)
    exponent = jnp.exp(shifted)
    mass = jnp.sum(exponent, axis=-1, keepdims=True)
    log_probs = shifted - jnp.log(mass)
    ce = -jnp.sum(goal * log_probs, axis=-1, keepdims=True)
    loss_o[...] = jnp.broadcast_to(jnp.sum(present[:, 0:1] * ce, axis=0, keepdims=True), (8, 128))
    dlogits = (present * inv_count[0] * (exponent / mass - goal)).astype(BF)

    dclass = tn(pooled, dlogits)
    store_columns4(out, dclass[:, :C4], wc_at)
    store_columns4(out, jnp.concatenate([dclass[:, C4:], jnp.zeros((C4, 2 * C4 - CLASSES), F32)], axis=1), wc_at + C4)
    if tall_at + tall_rows < out.shape[1]:
        out[:, tall_at + tall_rows :, :] = jnp.zeros((shards, out.shape[1] - tall_at - tall_rows, C4), BF)
    dpool = nt(dlogits, mat4[:, wc_at:])
    dgain = None
    for i in range(IMGS):
        rows = pl.ds(i * TOK4, TOK4)
        one = dpool[i : i + 1]
        part = one * hat_means[i]
        dgain = part if dgain is None else dgain + part
        xhat, rstd = normalize(y2_s[rows, :])
        dy2 = norm_grad(jnp.broadcast_to(one * (1.0 / TOK4), (TOK4, C4)), xhat, rstd, norms[6:7])
        y2_s[rows, :] = dy2
    gn_o[6:7] = dgain
    gn_o[7:8] = column_sum(dpool)

    for i in range(IMGS):
        nt_s[:, i * TOK4 : i * TOK4 + TOK4] = n_s[image_rows(i), :].T
        n_s[image_rows(i), :] = y2_s[image_rows(i), :].astype(BF)

    def hidden_grad(j, i):
        stage[image_rows(i), :] = nt(n_s[image_rows(i), :], second_rows(j))

    def spread_grad(j):
        for i in range(IMGS):
            store4(plain, moved, i, stage[image_rows(i), :] * slope_s[image_rows(i), lanes_of(j)].astype(F32))

    def first_grad(j):
        store_columns4(out, nn(nt_s[...], hid_s[:, lanes_of(j)]), w1_at + j * LC)

    for i in range(IMGS):
        hidden_grad(0, i)
    spread_grad(0)

    def feed_back(j, carry):
        later, previous = jnp.minimum(j + 1, chunks - 1), jnp.maximum(j - 1, 0)
        kernels = taps_of(j)
        sums = [[None] * 9 for _ in kernels]

        def convolve(lt, i, qx, part):
            lanes = pl.ds(lt * 128, 128)
            out_lanes = pl.ds(pl.multiple_of(j * LC + lt * 128, 128), 128)
            rows = pl.ds(i * TOK4 + qx * 128 + part * PART * 8, PART * 8)
            base = hid_s[rows, out_lanes].astype(F32).reshape(PART, 8, 128)
            acc = None
            for t, dy, dx in TAPS:
                value = tap4(plain, moved, i, qx, -dy, -dx, part, lanes)
                term = value * kernels[lt][t : t + 1][None]
                acc = term if acc is None else acc + term
                tap_sum = jnp.sum(value * base, axis=0)
                sums[lt][t] = tap_sum if sums[lt][t] is None else sums[lt][t] + tap_sum
            cur[rows, lanes] = acc.reshape(PART * 8, 128).astype(BF)

        def second_grad():
            grad = tn(act_s[:, lanes_of(j)], n_s[...]).astype(BF)
            act_s[0:LC, lanes_of(j)] = grad[:, 0:LC]
            act_s[LC : 2 * LC, lanes_of(j)] = grad[:, LC:]

        products = [second_grad, functools.partial(first_grad, previous)]
        products += [functools.partial(hidden_grad, later, i) for i in range(IMGS)]
        alternate([functools.partial(convolve, *block) for block in blocks], products)
        for lt in range(LC // 128):
            for t in range(9):
                gd_s[t, :, pl.ds(pl.multiple_of(j * LC + lt * 128, 128), 128)] = sums[lt][t]
        hid_s[:, lanes_of(j)] = cur[...]
        spread_grad(later)
        return carry

    lax.fori_loop(0, chunks, feed_back, 0)
    first_grad(chunks - 1)
    for j in range(chunks):
        wide = slice(j * LC, j * LC + LC)
        grad = jnp.concatenate([act_s[0:LC, wide], act_s[LC : 2 * LC, wide]], axis=1)
        store_rows(out, grad, 4 * C3 + j * LC, tall_rows, tall_at)
    for t in range(9):
        gd_o[t : t + 1, :] = column_sum(gd_s[t])

    mats_done, tall_done = 4 * (C4 // shards), up(4 * C3, tall_rows) // tall_rows
    early = [(at, mats_done, tall_at) for at in range(shards)]
    early += [(at, tall_at, out.shape[1]) for at in range(tall_done, shards)]
    send_off(out, keep, send, sems, core[0], early, 8)

    def normed_grad(i):
        return nt(hid_s[image_rows(i), :], mat4[:, w1_at : w1_at + F4])

    dgain = dshift = None
    later = normed_grad(0)
    for i in range(IMGS):
        rows = image_rows(i)
        dn = later
        if i + 1 < IMGS:
            later = normed_grad(i + 1)
        xhat, rstd = normalize(y1_s[rows, :])
        part_g, part_s = column_sum(dn * xhat), column_sum(dn)
        dgain = part_g if dgain is None else dgain + part_g
        dshift = part_s if dshift is None else dshift + part_s
        y2_s[rows, :] = y2_s[rows, :] + norm_grad(dn, xhat, rstd, norms[4:5])
    gn_o[4:5] = dgain
    gn_o[5:6] = dshift

    dprod = y2_s[...].astype(BF)
    store_columns4(out, nn(mix_s[...], dprod), 3 * C4)
    for i in range(IMGS):
        rows = pl.ds(i * TOK4, TOK4)
        n_s[rows, :] = nt(dprod[i * TOK4 : i * TOK4 + TOK4], mat4[:, 3 * C4 : 4 * C4]).astype(BF)

    d_s = slope_s

    def attend_back(pair, carry):
        lane = lax.broadcasted_iota(jnp.int32, (TOK4, 128), 1)
        steps = [(pair * IMGS + at, head) for at in range(IMGS) for head in range(H4)]
        dqts, dks, dvs, keys = [], [], [], []

        def image(i):
            return pl.ds(pl.multiple_of(i * TOK4, TOK4), TOK4)

        def at(head):
            return head // 2 * 128

        def first_product(i, head):
            start = 2 * C4 + at(head)
            return nt(half_of(qkv_s[image(i), start : start + 128], head % 2), n_s[image(i), at(head) : at(head) + 128])

        def last_products(i, head, ds):
            dks.append(nn(ds, qkv_s[image(i), at(head) : at(head) + 128]))
            if head % 2 == 0:
                keys.append(qkv_s[image(i), C4 + at(head) : C4 + at(head) + 128].T)
            dqts.append(nn(keys[-1][head % 2 * 64 : head % 2 * 64 + 64], ds))
            if head % 2 == 1:
                start, one = at(head), len(dks) - 1
                dqt = (jnp.concatenate(dqts[-2:], axis=0) * SCALE).astype(BF)
                dk = (jnp.where(lane < 64, dks[one - 1], dks[one]) * SCALE).astype(BF)
                dv = jnp.where(lane < 64, dvs[one - 1], dvs[one]).astype(BF)
                d_s[image(i), start : start + 128] = dqt.T
                d_s[image(i), C4 + start : C4 + start + 128] = dk
                d_s[image(i), 2 * C4 + start : 2 * C4 + start + 128] = dv

        later = first_product(*steps[0])
        before = None
        for step, (i, head) in enumerate(steps):
            dp = later
            if step + 1 < len(steps):
                later = first_product(*steps[step + 1])
            soft = p_s[i * H4 + head]
            dvs.append(nn(soft, n_s[image(i), at(head) : at(head) + 128]))
            ds = softmax_grad(soft.astype(F32), dp).astype(BF)
            if step > 0:
                last_products(*steps[step - 1], before)
            before = ds
        last_products(*steps[-1], before)
        return carry

    lax.fori_loop(0, 1, attend_back, 0)
    ht = h_s[...].T
    for j in range(3):
        wide = slice(j * C4, j * C4 + C4)
        store_columns4(out, nn(ht, d_s[:, wide]), j * C4)

    def normed_grad0(i):
        return nt(d_s[image_rows(i), 0 : 3 * C4], mat4[:, 0 : 3 * C4])

    sums = [None] * 4
    later = normed_grad0(0)
    for i in range(IMGS):
        rows = image_rows(i)
        dh = later
        if i + 1 < IMGS:
            later = normed_grad0(i + 1)
        hat0, rstd0 = normalize(first[rows, :])
        hat1, rstd1 = normalize(hat0 * norms[0:1] + norms[1:2])
        dy0 = y2_s[rows, :] + norm_grad(dh, hat1, rstd1, norms[2:3])
        n_s[rows, :] = norm_grad(dy0, hat0, rstd0, norms[0:1]).astype(BF)
        parts = [column_sum(dy0 * hat0), column_sum(dy0), column_sum(dh * hat1), column_sum(dh)]
        sums = [part if old is None else old + part for old, part in zip(sums, parts)]
    gn_o[0:4] = jnp.concatenate(sums, axis=0)
    for plane in range(4):
        total = None
        for i in range(IMGS):
            part = tn(x2[i, plane * 256 : plane * 256 + 256, :], n_s[image_rows(i), :])
            total = part if total is None else total + part
        store_rows(out, total, plane * C3, tall_rows, tall_at)
    late = [(at, 0, mats_done) for at in range(shards)] + [(at, tall_at, out.shape[1]) for at in range(tall_done)]
    send_off(out, keep, send, sems, core[0], late, 8 + len(early))
    stores = [load(x2.at[i], dx2_h.at[i], 1 + i) for i in range(IMGS)]
    for i in range(IMGS):
        for plane in range(4):
            grad = nt(n_s[image_rows(i), :], tall4[plane * C3 : plane * C3 + C3, :])
            x2[i, plane * 256 : plane * 256 + 256, :] = grad.astype(BF)
        stores[i].start()
    for one in stores:
        one.wait()
    arrived(out, keep, sems, early, 8)
    arrived(out, keep, sems, late, 8 + len(early))


def feed3_back(dx2, x1, n, hid, slope, act, tall3, mat3, depth, norms, dx1_o, g1_o, g2_o, gd_o, gn_o,
               acc1, acc2, accd, accn, plain, moved, dy_s, dyt_s, nt_s, da_s, stage, cur):
    step = pl.program_id(0)

    @pl.when(step == 0)
    def _():
        for ref in (plain, moved):
            ref[:, 0:1] = jnp.zeros((ref.shape[0], 1, 8, LC), F32)
            ref[:, 17:18] = jnp.zeros((ref.shape[0], 1, 8, LC), F32)
        for ref in (acc1, acc2, accd, accn):
            ref[...] = jnp.zeros_like(ref)

    dy = dx2[0]
    dy_s[...] = dy
    dyt_s[...] = dy.T
    nt_s[...] = n[0].T

    chunks = F3 // LC

    def lanes_of(j):
        return pl.ds(pl.multiple_of(j * LC, LC), LC)

    def hidden_grad(j, plane):
        rows = pl.ds(plane * 256, 256)
        w2 = tall3[pl.ds(pl.multiple_of(PATCH + 4 * C3 + j * LC, LC), LC), :]
        stage[rows, :] = nt(dy_s[rows, :], w2)

    def spread(j):
        for plane in range(4):
            rows = pl.ds(plane * 256, 256)
            store3(plain, moved, plane, stage[rows, :] * slope[0, rows, lanes_of(j)].astype(F32))

    def first_grad(j):
        acc1[:, lanes_of(j)] += nn(nt_s[...], da_s[:, lanes_of(j)])

    for plane in range(4):
        hidden_grad(0, plane)
    spread(0)

    def chunk(j, carry):
        later = jnp.minimum(j + 1, chunks - 1)
        previous = jnp.where(j > 0, j - 1, chunks)
        kernels, sums = [], []
        for lt in range(LC // 128):
            kernels.append(depth[:, pl.ds(pl.multiple_of(j * LC + lt * 128, 128), 128)])
            sums.append([None] * 9)

        def convolve(lt, py, xm, part):
            lanes = pl.ds(lt * 128, 128)
            out_lanes = pl.ds(pl.multiple_of(j * LC + lt * 128, 128), 128)
            rows = pl.ds(class3(py, xm) * 128 + part * PART * 8, PART * 8)
            base = hid[0, rows, out_lanes].astype(F32).reshape(PART, 8, 128)
            out = None
            for t, dy, dx in TAPS:
                value = tap3(plain, moved, py, xm, -dy, -dx, part, lanes)
                term = value * kernels[lt][t : t + 1][None]
                out = term if out is None else out + term
                tap_sum = jnp.sum(value * base, axis=0)
                sums[lt][t] = tap_sum if sums[lt][t] is None else sums[lt][t] + tap_sum
            cur[rows, lanes] = out.reshape(PART * 8, 128).astype(BF)

        def second_grad():
            acc2[:, lanes_of(j)] += nn(dyt_s[...], act[0, :, lanes_of(j)])

        products = [second_grad, functools.partial(first_grad, previous)]
        products += [functools.partial(hidden_grad, later, plane) for plane in range(4)]
        alternate(
            [
                functools.partial(convolve, lt, py, xm, part)
                for lt in range(LC // 128)
                for py in range(2)
                for xm in range(4)
                for part in range(16 // PART)
            ],
            products,
        )
        for lt in range(LC // 128):
            for t in range(9):
                accd[t, :, pl.ds(pl.multiple_of(j * LC + lt * 128, 128), 128)] += sums[lt][t]
        da_s[:, lanes_of(j)] = cur[...]
        spread(later)
        return carry

    lax.fori_loop(0, chunks, chunk, 0)
    first_grad(chunks - 1)

    def normed_grad(b):
        return nt(da_s[b * 256 : b * 256 + 256, 0:F3], mat3[:, 4 * C3P :])

    later = normed_grad(0)
    for b in range(4):
        rows = pl.ds(b * 256, 256)
        dn = later
        if b < 3:
            later = normed_grad(b + 1)
        xhat, rstd = normalize(x1[0, rows, :])
        accn[0:1] += column_sum(dn * xhat)
        accn[1:2] += column_sum(dn)
        dx1_o[0, rows, :] = dx2[0, rows, :].astype(F32) + norm_grad(dn, xhat, rstd, norms[6:7])

    @pl.when(step == IMGS - 1)
    def _():
        g1_o[...] = acc1[:, 0:F3]
        g2_o[...] = acc2[...].T.astype(g2_o.dtype)
        gn_o[...] = accn[...]
        for t in range(9):
            gd_o[t : t + 1, :] = column_sum(accd[t])


def attend3_back(groups, core, dx1, z, h, red, q, k, v, p, mix, patches, tall3, mat3, norms, g1, g2, flat, keep, send, out, sems,
                 tall_s, acce, accr, accq, acck, accv, acco, accn, dk_s, dv_s, kt_s, dqt_s, dr_s):
    step = pl.program_id(0)

    @pl.when(step == 0)
    def _():
        for ref in (acce, accr, accq, acck, accv, acco, accn):
            ref[...] = jnp.zeros_like(ref)

    kt_s[...] = k[0].T
    dk_s[...] = jnp.zeros_like(dk_s)
    dv_s[...] = jnp.zeros_like(dv_s)
    wo = mat3[0:C3, 3 * C3P : 3 * C3P + C3]
    lane = lax.broadcasted_iota(jnp.int32, (256, 128), 1)

    def queries():
        rows = [pl.ds(at * 256, 256) for at in range(4)]
        lanes = [slice(at * 128, at * 128 + 128) for at in range(3)]
        mixed, dks, dvs = [], [], []
        for block in rows:
            dprod = dx1[0, block, :].astype(BF)
            acco[...] += nn(mix[0, :, block], dprod)
            dmix = nt(dprod, wo).astype(BF)
            mixed.append(jnp.concatenate([dmix, jnp.zeros((256, C3P - C3), BF)], axis=1))
        steps = [(at, head) for at in range(4) for head in range(H3)]

        def first(at, head):
            return nt(half_of(v[0, :, lanes[head // 2]], head % 2), mixed[at][:, lanes[head // 2]])

        def last(at, head, ds):
            dks.append(nn(ds, q[0, rows[at], lanes[head // 2]]))
            dqt = nn(kt_s[head * 64 : head * 64 + 64, :], ds) * SCALE
            dqt_s[head * 64 : head * 64 + 64, rows[at]] = dqt.astype(BF)

        later = first(*steps[0])
        before = None
        for step_at, (at, head) in enumerate(steps):
            dp = later
            if step_at + 1 < len(steps):
                later = first(*steps[step_at + 1])
            soft = p[0, head, :, rows[at]]
            dvs.append(nn(soft, mixed[at][:, lanes[head // 2]]))
            ds = softmax_grad(soft.astype(F32), dp).astype(BF)
            if step_at > 0:
                last(*steps[step_at - 1], before)
            before = ds
        last(*steps[-1], before)
        for at in range(4):
            for pair_at in range(2):
                one = at * H3 + 2 * pair_at
                dk_s[:, lanes[pair_at]] += jnp.where(lane < 64, dks[one], dks[one + 1])
                dv_s[:, lanes[pair_at]] += jnp.where(lane < 64, dvs[one], dvs[one + 1])
            dk_s[:, lanes[2]] += dks[at * H3 + 4]
            dv_s[:, lanes[2]] += dvs[at * H3 + 4]

    queries()

    dk = (dk_s[...] * SCALE).astype(BF)
    dv = dv_s[...].astype(BF)
    hat_r, rstd_r = normalize(red[0])
    r = (hat_r * norms[4:5] + norms[5:6]).astype(BF)
    acck[...] += tn(r, dk)
    accv[...] += tn(r, dv)
    dr = nt(dk, mat3[:, C3P : 2 * C3P]) + nt(dv, mat3[:, 2 * C3P : 3 * C3P])
    accn[4:5] += column_sum(dr * hat_r)
    accn[5:6] += column_sum(dr)
    dred = norm_grad(dr, hat_r, rstd_r, norms[4:5]).astype(BF)
    accq[...] += nn(dqt_s[...], h[0])

    def input_grad(b):
        rows = slice(b * 256, b * 256 + 256)
        wr = tall3[PATCH + C3 * b : PATCH + C3 * (b + 1)]
        return contract(dqt_s[:, rows], mat3[:, 0:C3], 0, 1) + nt(dred, wr)

    def weight_grads(b, dz):
        rows = slice(b * 256, b * 256 + 256)
        accr[C3 * b : C3 * (b + 1)] += tn(h[0, rows, :], dred)
        acce[...] += tn(dz, patches[0, rows, :])

    later = input_grad(0)
    before = None
    for b in range(4):
        rows = pl.ds(b * 256, 256)
        dh = later
        if b < 3:
            later = input_grad(b + 1)
        hat0, rstd0 = normalize(z[0, rows, :])
        hat1, rstd1 = normalize(hat0 * norms[0:1] + norms[1:2])
        accn[2:3] += column_sum(dh * hat1)
        accn[3:4] += column_sum(dh)
        dx0 = dx1[0, rows, :] + norm_grad(dh, hat1, rstd1, norms[2:3])
        accn[0:1] += column_sum(dx0 * hat0)
        accn[1:2] += column_sum(dx0)
        dz = norm_grad(dx0, hat0, rstd0, norms[0:1]).astype(BF)
        if b > 0:
            weight_grads(b - 1, before)
        before = dz
    weight_grads(3, before)

    @pl.when(step == IMGS - 1)
    def _():
        shards = out.shape[0]
        mats, slot, flat_at, flat_rows, last, total_rows = places3(shards, groups)
        mat_rows = C3 // shards
        tall = (PATCH + 4 * C3 + F3) // shards // 2
        out[:, mats:, :] = jnp.zeros((shards, total_rows - mats, 2 * C3), BF)
        if tall < mats:
            out[:, tall:mats, :] = jnp.zeros((shards, mats - tall, 2 * C3), BF)
        tall_s[0:PATCH] = acce[...].T
        tall_s[PATCH : PATCH + 4 * C3] = accr[...]
        tall_s[PATCH + 4 * C3 :] = g2[...].astype(F32)
        accq[...] = accq[...].T
        for at in range(shards):
            rows = slice(at * mat_rows, at * mat_rows + mat_rows)
            pieces = [accq[rows, :], acck[rows, 0:C3], accv[rows, 0:C3], acco[rows, :]]
            start = at * 2 * tall
            pairs = [tall_s[start : start + tall], tall_s[start + tall : start + 2 * tall]]
            out[at, 0:tall, :] = jnp.concatenate(pairs, axis=1).astype(BF)
            for b in range(2):
                pair = jnp.concatenate(pieces[2 * b : 2 * b + 2], axis=1)
                out[at, mats + b * slot : mats + b * slot + mat_rows, :] = pair.astype(BF)
                feed = g1[rows, b * 2 * C3 : b * 2 * C3 + 2 * C3]
                out[at, mats + (b + 2) * slot : mats + (b + 2) * slot + mat_rows, :] = feed.astype(BF)
            out[at, flat_at : flat_at + flat_rows, :] = flat[at]
            out[at, last : last + 6, 0:mat_rows] = accn[:, rows].astype(BF)
        pieces = [(at, 0, total_rows) for at in range(shards)]
        send_off(out, keep, send, sems, core[0], pieces, 0)
        arrived(out, keep, sems, pieces, 0)


def whole(shape, dtype=None):
    return pl.BlockSpec(shape, lambda i: (0,) * len(shape), pipeline_mode=pl.Buffered(1))


def per_image(*shape):
    return pl.BlockSpec((1,) + shape, lambda i: (i,) + (0,) * len(shape))


def sds(*shape, dtype=F32):
    return jax.ShapeDtypeStruct(shape, dtype)


def work(microseconds):
    return pl.CostEstimate(flops=microseconds * 10**9, bytes_accessed=microseconds * 3 * 10**6, transcendentals=0)


PARAMS = pltpu.CompilerParams(vmem_limit_bytes=VMEM_BYTES, dimension_semantics=("arbitrary",))


def unpack3(pack, tall3, mat3):
    half = tall3.shape[0] // pack.shape[0] // 2
    size = C3 // pack.shape[0]
    for at in range(pack.shape[0]):
        start = at * 2 * half
        tall3[start : start + half, :] = pack[at, 0:half, 0:C3]
        tall3[start + half : start + 2 * half, :] = pack[at, 0:half, C3:]
        rows = slice(at * size, at * size + size)
        for b in range(2):
            piece = pack[at, half + b * size : half + (b + 1) * size, :]
            blank = jnp.zeros((size, C3P - C3), BF)
            wide = jnp.concatenate([piece[:, :C3], blank, piece[:, C3:], blank], axis=1)
            mat3[rows, b * 2 * C3P : (b + 1) * 2 * C3P] = wide
            feed = pack[at, half + (b + 2) * size : half + (b + 3) * size, :]
            mat3[rows, 4 * C3P + b * 2 * C3 : 4 * C3P + (b + 1) * 2 * C3] = feed


def forward3(packed, *refs):
    if packed:
        pack, patches, depth, norms, tall3, mat3 = refs[:6]

        @pl.when(pl.program_id(0) == 0)
        def _():
            unpack3(pack, tall3, mat3)

    else:
        tall3, mat3, patches, depth, norms = refs[:5]
    refs = refs[6 if packed else 5 :]
    x1 = refs[8]
    embed_attend(patches, tall3, mat3, norms, *refs[:9], *refs[14:16])
    feed3(x1, tall3, mat3, depth, norms, *refs[9:14], *refs[16:])


def run_forward3(weights, patches, depth, norms3):
    packed = len(weights) == 1
    tall_shape, mat_shape = (PATCH + 4 * C3 + F3, C3), (C3, 4 * C3P + F3)
    full = [whole(tall_shape), whole(mat_shape)] if packed else []
    full_shapes = [sds(*tall_shape, dtype=BF), sds(*mat_shape, dtype=BF)] if packed else []
    weight_specs = [whole(weight.shape) for weight in weights]
    image_specs = [per_image(TOK3, PATCH), whole(depth.shape), whole(norms3.shape)]
    outs = pl.pallas_call(
        functools.partial(forward3, packed),
        grid=(IMGS,),
        in_specs=weight_specs + image_specs,
        out_specs=full + [
            per_image(TOK3, C3), per_image(TOK3, C3), per_image(256, C3), per_image(TOK3, C3P), per_image(256, C3P),
            per_image(256, C3P), per_image(H3, 256, TOK3), per_image(C3, TOK3), per_image(TOK3, C3),
            per_image(TOK3, C3), per_image(TOK3, F3), per_image(TOK3, F3), per_image(TOK3, F3), per_image(TOK3, C3),
        ],
        out_shape=full_shapes + [
            sds(IMGS, TOK3, C3), sds(IMGS, TOK3, C3, dtype=BF), sds(IMGS, 256, C3), sds(IMGS, TOK3, C3P, dtype=BF),
            sds(IMGS, 256, C3P, dtype=BF), sds(IMGS, 256, C3P, dtype=BF), sds(IMGS, H3, 256, TOK3, dtype=BF),
            sds(IMGS, C3, TOK3, dtype=BF), sds(IMGS, TOK3, C3),
            sds(IMGS, TOK3, C3, dtype=BF), sds(IMGS, TOK3, F3, dtype=BF), sds(IMGS, TOK3, F3, dtype=BF),
            sds(IMGS, TOK3, F3, dtype=BF), sds(IMGS, TOK3, C3, dtype=BF),
        ],
        scratch_shapes=[
            pltpu.VMEM((TOK3, C3), F32), pltpu.VMEM((C3P, 256), BF),
            pltpu.VMEM((8, 18, 8, LC), F32), pltpu.VMEM((4, 18, 8, LC), F32), pltpu.VMEM((TOK3, LC), F32),
            pltpu.VMEM((TOK3, LC), BF), pltpu.VMEM((TOK3, LC), BF), pltpu.VMEM((TOK3, C3), F32),
        ],
        compiler_params=PARAMS,
        name="forward3",
        cost_estimate=work(85),
    )(*weights, patches, depth, norms3)
    return outs if packed else [*weights, *outs]


def run_section4(labels, valid, inv_count, core, x2, mat4, tall4, depth, norms4, shards, groups):
    vm = pl.BlockSpec(memory_space=pltpu.VMEM)
    sm = pl.BlockSpec(memory_space=pltpu.SMEM)
    hbm = pl.BlockSpec(memory_space=pl.ANY)
    rows = IMGS * TOK4
    half = sds(shards // 2, rows4(shards, groups), C4, dtype=BF)
    return pl.pallas_call(
        section4,
        in_specs=[sm, sm, sm, sm, hbm, hbm, hbm, vm, vm],
        out_specs=[hbm, hbm, hbm, vm, vm, vm],
        out_shape=[
            sds(IMGS, TOK3, C3, dtype=BF), half, half, sds(9, F4), sds(8, C4),
            sds(8, 128),
        ],
        scratch_shapes=[
            pltpu.VMEM(x2.shape, BF), pltpu.VMEM(mat4.shape, BF), pltpu.VMEM(tall4.shape, BF),
            pltpu.SemaphoreType.DMA((8 + 3 * shards,)), pltpu.VMEM((shards,) + half.shape[1:], BF),
            pltpu.VMEM((rows, C4), F32), pltpu.VMEM((rows, C4), F32), pltpu.VMEM((rows, C4), F32),
            pltpu.VMEM((rows, C4), BF), pltpu.VMEM((rows, 3 * C4), BF), pltpu.VMEM((IMGS * H4, 256, 256), BF),
            pltpu.VMEM((C4, rows), BF), pltpu.VMEM((rows, C4), BF), pltpu.VMEM((C4, rows), BF), pltpu.VMEM((rows, F4), BF),
            pltpu.VMEM((rows, F4), BF), pltpu.VMEM((rows, F4), BF), pltpu.VMEM((IMGS, 2, 18, 8, LC), F32),
            pltpu.VMEM((IMGS, 2, 18, 8, LC), F32), pltpu.VMEM((9, 8, F4), F32),
            pltpu.VMEM((rows, LC), F32), pltpu.VMEM((rows, LC), BF), pltpu.VMEM((rows, LC), BF),
        ],
        compiler_params=pltpu.CompilerParams(vmem_limit_bytes=VMEM_BYTES),
        name="section4",
        cost_estimate=work(90),
    )(labels, valid, inv_count, core, x2, mat4, tall4, depth, norms4)


def run_feed3_back(dx2, x1, n, hid, slope, act, tall3, mat3, depth, norms3):
    return pl.pallas_call(
        feed3_back,
        grid=(IMGS,),
        in_specs=[
            per_image(TOK3, C3), per_image(TOK3, C3), per_image(TOK3, C3), per_image(TOK3, F3), per_image(TOK3, F3),
            per_image(TOK3, F3), whole(tall3.shape), whole(mat3.shape), whole(depth.shape), whole(norms3.shape),
        ],
        out_specs=[per_image(TOK3, C3), whole((C3, F3)), whole((F3, C3)), whole((9, F3)), whole((2, C3))],
        out_shape=[sds(IMGS, TOK3, C3), sds(C3, F3), sds(F3, C3, dtype=BF), sds(9, F3), sds(2, C3)],
        scratch_shapes=[
            pltpu.VMEM((C3, F3 + LC), F32), pltpu.VMEM((C3, F3), F32), pltpu.VMEM((9, 8, F3), F32), pltpu.VMEM((2, C3), F32),
            pltpu.VMEM((8, 18, 8, LC), F32), pltpu.VMEM((4, 18, 8, LC), F32), pltpu.VMEM((TOK3, C3), BF),
            pltpu.VMEM((C3, TOK3), BF), pltpu.VMEM((C3, TOK3), BF), pltpu.VMEM((TOK3, F3 + LC), BF),
            pltpu.VMEM((TOK3, LC), F32), pltpu.VMEM((TOK3, LC), BF),
        ],
        compiler_params=PARAMS,
        name="feed3_back",
        cost_estimate=work(68),
    )(dx2, x1, n, hid, slope, act, tall3, mat3, depth, norms3)


def run_attend3_back(core, dx1, z, h, red, q, k, v, p, mix, patches, tall3, mat3, norms3, g1, g2, flat, groups):
    shards = flat.shape[0]
    total_rows = places3(shards, groups)[-1]
    return pl.pallas_call(
        functools.partial(attend3_back, groups),
        grid=(IMGS,),
        in_specs=[
            pl.BlockSpec(memory_space=pltpu.SMEM),
            per_image(TOK3, C3), per_image(TOK3, C3), per_image(TOK3, C3), per_image(256, C3), per_image(TOK3, C3P),
            per_image(256, C3P), per_image(256, C3P), per_image(H3, 256, TOK3), per_image(C3, TOK3),
            per_image(TOK3, PATCH), whole(tall3.shape), whole(mat3.shape), whole(norms3.shape),
            whole(g1.shape), whole(g2.shape), whole(flat.shape),
        ],
        out_specs=[pl.BlockSpec(memory_space=pl.ANY)] * 2,
        out_shape=[sds(shards // 2, total_rows, 2 * C3, dtype=BF)] * 2,
        scratch_shapes=[
            pltpu.VMEM((shards, total_rows, 2 * C3), BF), pltpu.SemaphoreType.DMA((shards,)),
            pltpu.VMEM((PATCH + 4 * C3 + F3, C3), F32),
            pltpu.VMEM((C3, PATCH), F32), pltpu.VMEM((4 * C3, C3), F32), pltpu.VMEM((C3, C3), F32),
            pltpu.VMEM((C3, C3P), F32), pltpu.VMEM((C3, C3P), F32), pltpu.VMEM((C3, C3), F32), pltpu.VMEM((6, C3), F32),
            pltpu.VMEM((256, C3P), F32), pltpu.VMEM((256, C3P), F32), pltpu.VMEM((C3P, 256), BF),
            pltpu.VMEM((C3, TOK3), BF), pltpu.VMEM((256, C3), F32),
        ],
        compiler_params=PARAMS,
        name="attend3_back",
        cost_estimate=work(65),
    )(core, dx1, z, h, red, q, k, v, p, mix, patches, tall3, mat3, norms3, g1, g2, flat)


def pad_mat3(mat):
    pieces = [mat[:, at * C3 : at * C3 + C3] for at in range(4)]
    pieces = [jnp.pad(piece, ((0, 0), (0, C3P - C3))) for piece in pieces]
    return jnp.concatenate(pieces + [mat[:, 4 * C3 :]], axis=1)


def reorder(patches):
    count = patches.shape[0]
    grid = patches.reshape(count, 16, 2, 8, 2, 2, patches.shape[-1])
    return grid.transpose(0, 2, 5, 4, 1, 3, 6).reshape(patches.shape)


def swap(value, axis, mask):
    return lax.ppermute(value, axis, [(at, at ^ mask) for at in range(lax.axis_size(axis))])


def pick(value, index, axis=0):
    return lax.dynamic_index_in_dim(value, index, axis, keepdims=False)


def add_all(own, parts):
    total = own.astype(F32)
    for part in parts:
        total = total + part.astype(F32)
    return total


def chip_sends(keep, got):
    chip = lax.axis_index("fsdp") // 2
    masks = range(1, keep.shape[0])
    return [add_all(pick(keep, chip ^ mask), [pick(got, chip ^ mask)]).astype(BF) for mask in masks]


def chip_own(keep, got):
    chip = lax.axis_index("fsdp") // 2
    return add_all(pick(keep, chip), [pick(got, chip)])


def depth_sends(shard):
    count, me = lax.axis_size("dp"), lax.axis_index("dp")
    cut = shard.reshape(count, shard.shape[0] // count, shard.shape[1])
    return pick(cut, me), [pick(cut, me ^ mask).astype(BF) for mask in range(1, count)]


def exchange(sends, axis, unit):
    return [swap(send, axis, unit * (at + 1)) for at, send in enumerate(sends)]


def depth_gather(piece):
    count, me = lax.axis_size("dp"), lax.axis_index("dp")
    narrow = piece.astype(BF)
    parts = [narrow] + [swap(narrow, "dp", mask) for mask in range(1, count)]
    placed = [lax.select_n(me, *[parts[at ^ other] for other in range(count)]) for at in range(count)]
    return jnp.concatenate(placed, axis=0).astype(F32)


def total_over_all(row):
    count = lax.axis_size("dp") * lax.axis_size("fsdp")
    rows = jnp.broadcast_to(row, (count, row.shape[1]))
    return jnp.sum(lax.all_to_all(rows, ("dp", "fsdp"), 0, 0, tiled=True), axis=0, keepdims=True)


def adamw(master, moment, second, gradient, is_norm):
    step_rate = 0.5 if is_norm else 0.05
    decay_now = 0.0 if is_norm else 0.05
    first = 0.9 * moment + 0.1 * gradient
    second_new = 0.999 * second + 0.001 * gradient * gradient
    first_hat = first * (1.0 / (1.0 - 0.9**STEP))
    second_hat = second_new * (1.0 / (1.0 - 0.999**STEP))
    updated = master - step_rate * (first_hat / (jnp.sqrt(second_hat) + 1e-08) + decay_now * master)
    return (updated, first, second_new)


def body(patches, labels, valid, *state):
    masters, moments, seconds = state[0:7], state[7:14], state[14:21]
    shards, groups = lax.axis_size("fsdp"), lax.axis_size("dp")
    mat3, tall3, mat4, tall4, depth, norms3, norms4 = [master.astype(BF) for master in masters]
    half, m_rows = tall3.shape[0] // 2, mat3.shape[0]
    pack = [jnp.concatenate([tall3[:half], tall3[half:]], axis=1)]
    pack += [mat3[:, at * 2 * C3 : at * 2 * C3 + 2 * C3] for at in range(4)]
    pack = lax.all_gather(jnp.concatenate(pack, axis=0), "fsdp", axis=0)

    small = [jnp.pad(piece.T, ((0, 0), (0, 16 - piece.shape[0]))) for piece in (depth, norms3, norms4)]
    small.append(jnp.full((8, 16), jnp.sum(valid)).astype(BF))
    sizes = [piece.shape[0] for piece in small]
    small = lax.all_gather(jnp.concatenate(small, axis=0), "fsdp", axis=0)
    edges = [0, sizes[0], sizes[0] + sizes[1], sum(sizes[:3])]
    parts = [small[:, edges[at] : edges[at + 1]].reshape(-1, 16).T.astype(F32) for at in range(3)]
    depth_all, norms3_all, norms4_all = parts[0][:9], parts[1][:8], parts[2][:8]
    present = jnp.full((8, 128), jnp.sum(small[:, edges[3], 0].astype(F32)))
    others = exchange([present] * (groups - 1), "dp", 1)

    weights3 = [pack]
    if half % 8 or m_rows % 8:
        tall3_all = jnp.concatenate([pack[:, :half, :C3], pack[:, :half, C3:]], axis=1).reshape(-1, C3)
        mats = pack[:, half:].reshape(shards, 4, m_rows, 2 * C3).transpose(1, 0, 2, 3).reshape(4, C3, 2 * C3)
        mat3_all = [mats[at // 2, :, at % 2 * C3 : at % 2 * C3 + C3] for at in range(4)]
        mat3_all = [jnp.pad(piece, ((0, 0), (0, C3P - C3))) for piece in mat3_all]
        weights3 = [tall3_all, jnp.concatenate(mat3_all + [mats[2], mats[3]], axis=1)]
    tall4_all = lax.all_gather(tall4, "fsdp", axis=0, tiled=True)
    mat4_all = lax.all_gather(mat4, "fsdp", axis=0, tiled=True)

    patches = reorder(patches.reshape(IMGS, TOK3, PATCH))
    depth3, depth4 = depth_all[:, :F3], depth_all[:, F3:]
    tall3_all, mat3_all, z, h, red, q, k, v, p, mix, x1, n, hid, slope, act, x2 = run_forward3(
        weights3, patches, depth3, norms3_all
    )
    x2, others = lax.optimization_barrier((x2, others))
    image_count = add_all(present, others)[0, 0]
    inv_count = (1.0 / image_count).reshape(1)
    core = (lax.axis_index("fsdp") % 2).reshape(1)
    dx2, keep4, send4, gd4, gn4, loss = run_section4(
        labels.reshape(IMGS), valid.reshape(IMGS), inv_count, core, x2, mat4_all, tall4_all, depth4, norms4_all,
        shards, groups,
    )

    core4 = swap(send4, "fsdp", 1)
    sends4 = chip_sends(keep4, core4)
    dx2, keep4, core4, sends4 = lax.optimization_barrier((dx2, keep4, core4, sends4))
    got4 = exchange(sends4, "fsdp", 2)
    dx1, g1, g2, gd3, gn3b = run_feed3_back(dx2, x1, n, hid, slope, act, tall3_all, mat3_all, depth3, norms3_all)
    dx1, keep4, core4, got4 = lax.optimization_barrier((dx1, keep4, core4, got4))
    own4, sends4 = depth_sends(add_all(chip_own(keep4, core4), got4))

    def by_columns(grad):
        return grad.reshape(grad.shape[0], shards, -1).transpose(1, 0, 2).reshape(shards, -1)

    _, slot, flat_at, flat_rows, last, _ = places3(shards, groups)
    flat = jnp.concatenate([by_columns(grad) for grad in (jnp.concatenate([gd3, gd4], axis=1), gn3b, gn4)], axis=1)
    flat = jnp.pad(flat, ((0, 0), (0, flat_rows * 2 * C3 - flat.shape[1])))
    flat = flat.reshape(shards, flat_rows, 2 * C3).astype(BF)
    dx1, own4, sends4, flat = lax.optimization_barrier((dx1, own4, sends4, flat))
    got4 = exchange(sends4, "dp", 1)
    keep3, send3 = run_attend3_back(
        core, dx1, z, h, red, q, k, v, p, mix, patches, tall3_all, mat3_all, norms3_all, g1, g2, flat, groups
    )
    keep3, send3, got4 = lax.optimization_barrier((keep3, send3, got4))
    piece4 = add_all(own4, got4)
    core3 = swap(send3, "fsdp", 1)
    sends3 = chip_sends(keep3, core3)
    keep3, core3, sends3, piece4 = lax.optimization_barrier((keep3, core3, sends3, piece4))
    got3 = exchange(sends3, "fsdp", 2)
    grads4 = depth_gather(piece4)
    keep3, core3, got3, grads4 = lax.optimization_barrier((keep3, core3, got3, grads4))
    own3, sends3 = depth_sends(add_all(chip_own(keep3, core3), got3))
    piece3 = add_all(own3, exchange(sends3, "dp", 1))
    square = jnp.sum(piece4 * piece4) + jnp.sum(piece3 * piece3)
    lane = lax.broadcasted_iota(jnp.int32, (1, 128), 1)
    totals = total_over_all(jnp.where(lane == 0, square, loss[0:1]))
    grads3 = depth_gather(piece3)

    m_rows, t_rows = C4 // shards, masters[3].shape[0]
    blocks4 = [grads4[at * m_rows : at * m_rows + m_rows] for at in range(10)]
    grad_mat4 = jnp.concatenate(blocks4, axis=1)[:, : masters[2].shape[1]]
    grad_tall4 = grads4[10 * m_rows : 10 * m_rows + t_rows]
    t_rows, m_rows = masters[1].shape[0], masters[0].shape[0]
    mats_at, half = up(t_rows // 2, 16), t_rows // 2
    grad_tall3 = jnp.concatenate([grads3[:half, :C3], grads3[:half, C3:]], axis=0)
    grad_mat3 = jnp.concatenate([grads3[mats_at + at * slot : mats_at + at * slot + m_rows] for at in range(4)], axis=1)
    flat = grads3[flat_at : flat_at + flat_rows].reshape(-1)
    sizes = [9 * t_rows, 2 * m_rows, masters[6].size]
    grad_depth = flat[: sizes[0]].reshape(9, t_rows)
    grad_norms3 = jnp.concatenate(
        [grads3[last : last + 6, :m_rows], flat[sizes[0] : sizes[0] + sizes[1]].reshape(2, m_rows)], axis=0
    )
    grad_norms4 = flat[sizes[0] + sizes[1] : sum(sizes)].reshape(masters[6].shape)
    group = [grad_mat3, grad_tall3, grad_mat4, grad_tall4, grad_depth, grad_norms3, grad_norms4]

    grad_norm = jnp.sqrt(totals[0, 0])
    clip_factor = jnp.minimum(1.0, CLIP_LEVEL / (grad_norm + 1e-06))
    results = [adamw(masters[at], moments[at], seconds[at], clip_factor * group[at], at >= 5) for at in range(7)]
    return (
        *[result[0] for result in results],
        *[result[1] for result in results],
        *[result[2] for result in results],
        totals[0, 1],
        image_count,
        grad_norm,
    )


def solution(mesh):
    rows, columns = P("fsdp", None), P(None, "fsdp")
    weights = (rows,) * 4 + (columns,) * 3
    images = P(None, ("dp", "fsdp"))
    in_specs = (P(None, ("dp", "fsdp"), None, None), images, images) + weights * 3
    out_specs = weights * 3 + (P(), P(), P())
    return jax.shard_map(body, mesh=mesh, in_specs=in_specs, out_specs=out_specs, check_vma=False)
```
